32 devices in a mesh: rep: 4 (over z), grp: 8 (over y, x, core).
Axes of the slice: x: 2, y: 2, z: 4, core: 2. Of those that a mesh axis runs over, the one named last changes fastest.
Arguments:
- tokens: bfloat16 [4, 192, 32, 1024], P(None, None, ('rep', 'grp')), may hold values from -6 to 6
- cotangent: bfloat16 [4, 192, 32, 1024], P(None, None, ('rep', 'grp')), may hold values from -6 to 6
- seq_lengths: int32 [4, 64], replicated, may hold values from 1 to 128, as said below
- w_qkv: bfloat16 [1024, 3072], P('grp'), may hold values from -0.1875 to 0.1875
- w_out: bfloat16 [1024, 1024], P('grp'), may hold values from -1.5 to 1.5
- w_in: bfloat16 [1024, 5248], P('grp'), may hold values from -0.1875 to 0.1875
- w_down: bfloat16 [2624, 1024], P('grp'), may hold values from -0.125 to 0.125
- attn_gain: bfloat16 [1024], P('grp'), may hold values from 0.099609375 to 1.8984375
- mlp_gain: bfloat16 [1024], P('grp'), may hold values from 0.099609375 to 1.8984375
Outputs:
- layer_out: bfloat16 [4, 192, 32, 1024], P(None, None, ('rep', 'grp'))
- grad_tokens: bfloat16 [4, 192, 32, 1024], P(None, None, ('rep', 'grp'))
- grad_attn_gain: float32 [1024], P('grp')
- grad_mlp_gain: float32 [1024], P('grp')
- grad_w_qkv: float32 [1024, 3072], P('grp')
- grad_w_out: float32 [1024, 1024], P('grp')
- grad_w_in: float32 [1024, 5248], P('grp')
- grad_w_down: float32 [2624, 1024], P('grp')
The draws below stay inside these ranges and needn't reach their ends.
Inputs may be any that keep to these rules, and one draw needn't show every extreme that they name: `seq_lengths`: the lengths of one micro-batch sum to 192 times the number of devices; the 2 sequences s of one device (s div 2 the same), each padded to whole blocks of 128 tokens, fill exactly 2 blocks; in every micro-batch the longest sequence fills exactly 1 whole block. Hence the tokens of one micro-batch that go from one device to another number at most 256 / (number of devices), and in every micro-batch some device receives exactly that many from every device.
All inputs are finite; a program needn't handle non-finite values.
Results may differ from the reference program's by a relative error of at most 0.02.
Values may be sent and summed in bfloat16 or wider, within the bound.
A program may use at most 576 MiB of HBM per device.

```python
import jax
import jax.numpy as jnp
from jax import lax

D = 1024
HEADS = 16
HD = 64
FF = 2624
BLK = 128
NBLK = 2
MICRO = 4
SEQ_DEV = 2
CAP = 256
TOK_DEV = 192
SEQS = 64
N_REP = 4
N_GRP = 8


def deal_micro(micro_key):
    devices = N_REP * N_GRP
    split_keys = jax.random.split(micro_key, 3)
    full_device = jax.random.randint(split_keys[0], (), 0, devices)
    scores = jax.random.randint(split_keys[1], (devices, NBLK - 1), 0, 1 << 20) * NBLK
    scores = scores + jnp.arange(NBLK - 1, dtype=jnp.int32)[None, :]
    cut_points = jnp.sort(jnp.argsort(scores, axis=1)[:, :SEQ_DEV - 1].astype(jnp.int32) + 1, axis=1)
    low_edge = jnp.zeros((devices, 1), jnp.int32)
    high_edge = jnp.full((devices, 1), NBLK, jnp.int32)
    bounds = jnp.concatenate([low_edge, cut_points, high_edge], axis=1)
    fixed_bounds = jnp.concatenate([jnp.zeros((1,), jnp.int32), NBLK - SEQ_DEV + 1 + jnp.arange(SEQ_DEV, dtype=jnp.int32)])
    is_full = (jnp.arange(devices, dtype=jnp.int32) == full_device)[:, None]
    bounds = jnp.where(is_full, fixed_bounds[None, :], bounds)
    block_counts = (bounds[:, 1:] - bounds[:, :-1]).reshape(-1)
    slot_ids = jnp.arange(SEQS, dtype=jnp.int32)
    owner_device = slot_ids // SEQ_DEV
    slot_count = SEQS - SEQ_DEV
    removed = (CAP - TOK_DEV) * devices
    base_cut = removed // slot_count
    spread_top = min(base_cut, 126 - base_cut) + 1
    order_ids = slot_ids - SEQ_DEV * (owner_device > full_device).astype(jnp.int32)
    order_ids = jnp.where(owner_device == full_device, 0, order_ids)
    jitter = jax.random.randint(split_keys[2], (SEQS,), 0, spread_top)
    trimmed = base_cut + (order_ids < removed % slot_count).astype(jnp.int32)
    trimmed = trimmed + jitter[order_ids] - jitter[(order_ids + 1) % slot_count]
    trimmed = jnp.where(owner_device == full_device, 0, trimmed)
    return (block_counts * BLK - trimmed).astype(jnp.int32)


def draw_seq_lengths(key, part):
    return jax.vmap(deal_micro)(jax.random.split(jax.random.fold_in(key, 11), MICRO))


def levels(stream_key, dims, cuts, low, top_value):
    gain = 1.0
    for dim, parts in cuts:
        heights = jax.random.uniform(jax.random.fold_in(jax.random.fold_in(stream_key, 6), dim), (parts,), jnp.float32, low / len(cuts), top_value / len(cuts))
        gain = gain * jnp.repeat(jnp.exp(heights), dims[dim] // parts).reshape((-1,) + (1,) * (len(dims) - 1 - dim))
    return gain


def bell_draw(rng, shape, spread, limit, shards=(), held_as=jnp.bfloat16):
    values = spread * jax.random.normal(rng, shape, jnp.float32)
    if shards:
        values = values * levels(rng, shape, shards, -0.22, 0.18)
    return jnp.clip(values, -limit, limit).astype(held_as)


def setup_inputs(seed: int = 0) -> dict:
    streams_of = jax.random.split(jax.random.key(seed), 10)
    tokens = bell_draw(streams_of[0], (MICRO, TOK_DEV, N_REP * N_GRP, D), 1.0, 6.0, ((2, 32),))
    cotangent = bell_draw(streams_of[1], (MICRO, TOK_DEV, N_REP * N_GRP, D), 1.0, 6.0, ((2, 32),))
    seq_lengths = draw_seq_lengths(jax.random.fold_in(streams_of[9], 71), 0)
    w_qkv = bell_draw(streams_of[3], (D, 3 * D), D ** -0.5, 0.1875, ((0, 8),))
    w_out = bell_draw(streams_of[4], (D, D), (D // 64) ** -0.5, 1.5, ((0, 8),))
    w_in = bell_draw(streams_of[5], (D, 2 * FF), D ** -0.5, 0.1875, ((0, 8),))
    w_down = bell_draw(streams_of[6], (FF, D), FF ** -0.5, 0.125, ((0, 8),))
    attn_gain = jnp.clip(1.0 + 0.18 * jax.random.normal(streams_of[7], (D,), jnp.float32), 0.099609375, 1.8984375).astype(jnp.bfloat16)
    mlp_gain = jnp.clip(1.0 + 0.18 * jax.random.normal(streams_of[8], (D,), jnp.float32), 0.099609375, 1.8984375).astype(jnp.bfloat16)
    return {"tokens": tokens, "cotangent": cotangent, "seq_lengths": seq_lengths, "w_qkv": w_qkv, "w_out": w_out, "w_in": w_in, "w_down": w_down, "attn_gain": attn_gain, "mlp_gain": mlp_gain}


EPS = 1e-05
THETA = 160000.0
NEG = -1e+30

@jax.custom_vjp
def low(v):
    return lax.optimization_barrier(v.astype(jnp.bfloat16)).astype(jnp.float32)

@jax.custom_vjp
def low_back(v):
    return v

def low_keep(v):
    return (low(v), None)

def low_pass(kept, grad):
    return (grad,)

def back_keep(v):
    return (v, None)

def back_low(kept, grad):
    return (low(grad),)
low.defvjp(low_keep, low_pass)
low_back.defvjp(back_keep, back_low)

def hidden_norm(values):
    center = values - lax.optimization_barrier(jnp.mean(values, axis=-1, keepdims=True))
    return center * lax.rsqrt(lax.optimization_barrier(jnp.mean(center * center, axis=-1, keepdims=True)) + EPS)

def rotary_tables(position):
    half_width = HD // 2
    frequency = THETA ** (-2.0 * jnp.arange(half_width, dtype=jnp.float32) / HD)
    angles = position.astype(jnp.float32)[:, None] * frequency[None, :]
    cosine = jnp.concatenate([jnp.cos(angles), jnp.cos(angles)], axis=1)
    sine = jnp.concatenate([jnp.sin(angles), jnp.sin(angles)], axis=1)
    return (cosine[:, None, :], sine[:, None, :])

def rotate(values, cosine, sine):
    half_width = HD // 2
    turned = jnp.concatenate([-values[..., half_width:], values[..., :half_width]], axis=-1)
    return values * cosine + turned * sine

def mat_high(left, right):
    return jnp.dot(left, right, preferred_element_type=jnp.float32, precision=lax.Precision.HIGHEST)

def layer_rows(hidden, segment, position, qkv_w, out_w, in_w, down_w, gain_one, gain_two):
    high = lax.Precision.HIGHEST
    row_total = hidden.shape[0]
    normed = low(hidden_norm(hidden) * gain_one)
    packed = low_back(mat_high(normed, qkv_w))
    cosine, sine = rotary_tables(position)
    queries = low(rotate(packed[:, :D].reshape(row_total, HEADS, HD), cosine, sine))
    keys_rot = low(rotate(packed[:, D:2 * D].reshape(row_total, HEADS, HD), cosine, sine))
    values_low = low(packed[:, 2 * D:].reshape(row_total, HEADS, HD))
    scores = jnp.einsum('qhd,khd->hqk', queries, keys_rot, precision=high) * HD ** (-0.5)
    scores = low_back(scores)
    same_seq = segment[:, None] == segment[None, :]
    scores = jnp.where(same_seq[None], scores, NEG)
    top_score = lax.optimization_barrier(jnp.max(scores, axis=-1, keepdims=True))
    expo = jnp.exp(scores - top_score)
    weights_low = low(expo / lax.optimization_barrier(jnp.sum(expo, axis=-1, keepdims=True)))
    context = jnp.einsum('hqk,khd->qhd', weights_low, values_low, precision=high).reshape(row_total, D)
    context = low(low_back(context))
    middle = hidden + low_back(mat_high(context, out_w))
    normed_two = low(hidden_norm(middle) * gain_two)
    gate_up = low_back(mat_high(normed_two, in_w))
    activated = low(jax.nn.gelu(gate_up[:, :FF], approximate=False) * gate_up[:, FF:])
    return middle + low_back(mat_high(activated, down_w))

def dest_plan(lengths_row, device):
    seq_starts = (jnp.cumsum(lengths_row) - lengths_row).astype(jnp.int32)
    row_ids = jnp.arange(CAP, dtype=jnp.int32)
    own_slots = (device * SEQ_DEV + jnp.arange(SEQ_DEV, dtype=jnp.int32)).astype(jnp.int32)
    own_blocks = ((lengths_row[own_slots] + (BLK - 1)) // BLK).astype(jnp.int32)
    own_first = ((jnp.cumsum(own_blocks) - own_blocks) * BLK).astype(jnp.int32)
    slot_rank = lax.optimization_barrier(jnp.sum((own_first[None, :] <= row_ids[:, None]).astype(jnp.int32), axis=1)).astype(jnp.int32) - 1
    in_sequence = row_ids - own_first[slot_rank]
    sequence = own_slots[slot_rank]
    is_valid = in_sequence < lengths_row[sequence]
    given_pos = (seq_starts[sequence] + in_sequence).astype(jnp.int32)
    return (is_valid, given_pos, jnp.where(is_valid, slot_rank, -1), jnp.where(is_valid, in_sequence, 0))

def take_rows(table, index):
    return table[index]

def reference(tokens, cotangent, seq_lengths, w_qkv, w_out, w_in, w_down, attn_gain, mlp_gain):
    devices = N_REP * N_GRP
    given_total = TOK_DEV * devices
    device_ids = jnp.arange(devices, dtype=jnp.int32)
    per_device = jax.vmap(dest_plan, in_axes=(None, 0))
    per_micro = jax.vmap(per_device, in_axes=(0, None))
    is_valid, given_pos, segment, position = per_micro(seq_lengths, device_ids)
    safe_pos = jnp.where(is_valid, given_pos, 0).reshape(MICRO, devices * CAP)
    keep_mask = is_valid.reshape(MICRO, devices * CAP, 1)
    flat_tokens = tokens.astype(jnp.float32).reshape(MICRO, given_total, D)
    flat_cot = cotangent.astype(jnp.float32).reshape(MICRO, given_total, D)
    inputs = jnp.where(keep_mask, jax.vmap(take_rows)(flat_tokens, safe_pos), 0.0).reshape(-1, CAP, D)
    cot_rows = jnp.where(keep_mask, jax.vmap(take_rows)(flat_cot, safe_pos), 0.0).reshape(-1, CAP, D)
    segments = segment.reshape(-1, CAP)
    positions = position.reshape(-1, CAP)
    weights = (w_qkv.astype(jnp.float32), w_out.astype(jnp.float32), w_in.astype(jnp.float32), w_down.astype(jnp.float32), attn_gain.astype(jnp.float32), mlp_gain.astype(jnp.float32))

    def forward(hidden_all, qkv_w, out_w, in_w, down_w, gain_one, gain_two):

        def one_group(items):
            hidden, seg_row, pos_row = items
            return layer_rows(hidden, seg_row, pos_row, qkv_w, out_w, in_w, down_w, gain_one, gain_two)
        return lax.map(jax.checkpoint(one_group), (hidden_all, segments, positions))
    outputs, pullback = jax.vjp(forward, inputs, *weights)
    grads_all = pullback(cot_rows)
    drop_pos = jnp.where(is_valid, given_pos, given_total).reshape(MICRO, devices * CAP)

    def put_rows(index, rows_in):
        return jnp.zeros((given_total, D), rows_in.dtype).at[index].set(rows_in, mode='drop')
    out_given = jax.vmap(put_rows)(drop_pos, outputs.reshape(MICRO, devices * CAP, D))
    grad_given = jax.vmap(put_rows)(drop_pos, grads_all[0].reshape(MICRO, devices * CAP, D))
    layer_out = out_given.reshape(MICRO, TOK_DEV, devices, D).astype(jnp.bfloat16)
    grad_tokens = grad_given.reshape(MICRO, TOK_DEV, devices, D).astype(jnp.bfloat16)
    return (layer_out, grad_tokens, grads_all[5], grads_all[6], grads_all[1], grads_all[2], grads_all[3], grads_all[4])
```

```python
import functools
import math

import jax
import jax.numpy as jnp
import numpy as np
from jax import lax
from jax.experimental import pallas as pl
from jax.experimental.pallas import tpu as pltpu
from jax.sharding import PartitionSpec as P

D = 1024
HEADS = 16
HD = 64
FF = 2624
BLK = 128
MICRO = 4
SEQ_DEV = 2
CAP = 256
TOK_DEV = 192
ROWS = MICRO * CAP
BLOCKS = ROWS // BLK
PAIRS = HEADS // 2
LANES = 2 * HD

EPS = 1e-05
THETA = 160000.0
NEG = -1e30
ROOT_HALF = math.sqrt(0.5)
INV_ROOT_TWO_PI = 1.0 / math.sqrt(2.0 * math.pi)
SCALE = HD**-0.5

FF_TILE = 384
FF_STEPS = -(-FF // FF_TILE)
FF_PAD = FF_STEPS * FF_TILE
ROW_CHUNK = 256
CHUNK_ROWS = 16

F32 = jnp.float32
BF16 = jnp.bfloat16
MIB = 1 << 20


def dot(left, right, left_dim=1, right_dim=0):
    return lax.dot_general(
        left, right, (((left_dim,), (right_dim,)), ((), ())), preferred_element_type=F32
    )


def params(mib, steps=1):
    return pltpu.CompilerParams(
        vmem_limit_bytes=mib * MIB, dimension_semantics=("arbitrary",) * steps
    )


def cost(flops, moved, transcendentals=0):
    return pl.CostEstimate(
        flops=flops, bytes_accessed=moved, transcendentals=transcendentals
    )


def normed(values):
    center = values - jnp.mean(values, axis=-1, keepdims=True)
    inverse = lax.rsqrt(jnp.mean(center * center, axis=-1, keepdims=True) + EPS)
    return center * inverse, inverse


def norm_back(grad, normal, inverse):
    centred = grad - jnp.mean(grad, axis=-1, keepdims=True)
    return inverse * (centred - normal * jnp.mean(grad * normal, axis=-1, keepdims=True))


def rotary_tables(width):
    half = HD // 2
    frequency = THETA ** (-2.0 * jnp.arange(half, dtype=F32) / HD)
    angles = jnp.arange(BLK, dtype=F32)[:, None] * frequency[None, :]
    cosine, sine = jnp.cos(angles), jnp.sin(angles)
    cosine = jnp.concatenate([cosine, cosine], axis=1)
    sine = jnp.concatenate([-sine, sine], axis=1)
    return (jnp.tile(cosine, (1, width // HD)), jnp.tile(sine, (1, width // HD)))


def turned(values):
    axis = values.ndim - 1
    half = HD // 2
    width = values.shape[axis]
    lane = lax.broadcasted_iota(jnp.int32, values.shape, axis) % HD
    return jnp.where(
        lane < half,
        pltpu.roll(values, width - half, axis),
        pltpu.roll(values, half, axis),
    )


def pack_kernel(micros, rows_ref, want_ref, out_ref):
    total = None
    for step in range(micros):
        want = want_ref[step]
        mine = lax.broadcasted_iota(jnp.int32, (TOK_DEV, want.shape[1]), 0)
        pick = (mine == want).astype(F32).astype(BF16)
        term = dot(pick, rows_ref[step], 0, 0)
        total = term if total is None else total + term
    out_ref[...] = total.astype(BF16).reshape(out_ref.shape)


def pack_rows(rows, want, devices, micros):
    groups = MICRO // micros
    slots = want.shape[-1]
    return pl.pallas_call(
        functools.partial(pack_kernel, micros),
        grid=(groups,),
        in_specs=[
            pl.BlockSpec((micros, TOK_DEV, D), lambda g: (g, 0, 0)),
            pl.BlockSpec((micros, 1, slots), lambda g: (g, 0, 0)),
        ],
        out_specs=pl.BlockSpec((devices, 1, CHUNK_ROWS, D), lambda g: (0, g, 0, 0)),
        out_shape=jax.ShapeDtypeStruct((devices, groups, CHUNK_ROWS, D), BF16),
        compiler_params=params(40),
        cost_estimate=cost(2 * MICRO * TOK_DEV * slots * D, 4 * groups * slots * D),
    )(rows, want)


def spread_kernel(micros, back_ref, want_ref, out_ref):
    arrived = back_ref[...].reshape(-1, D)
    for step in range(micros):
        want = want_ref[step]
        mine = lax.broadcasted_iota(jnp.int32, (TOK_DEV, want.shape[1]), 0)
        pick = (mine == want).astype(F32).astype(BF16)
        out_ref[step] = dot(pick, arrived).astype(BF16)


def spread_rows(back, want, devices, micros):
    groups = MICRO // micros
    slots = want.shape[-1]
    return pl.pallas_call(
        functools.partial(spread_kernel, micros),
        grid=(groups,),
        in_specs=[
            pl.BlockSpec((devices, 1, CHUNK_ROWS, D), lambda g: (0, g, 0, 0)),
            pl.BlockSpec((micros, 1, slots), lambda g: (g, 0, 0)),
        ],
        out_specs=pl.BlockSpec((micros, TOK_DEV, D), lambda g: (g, 0, 0)),
        out_shape=jax.ShapeDtypeStruct((MICRO, TOK_DEV, D), BF16),
        compiler_params=params(40),
        cost_estimate=cost(2 * MICRO * TOK_DEV * slots * D, 4 * groups * slots * D),
    )(back, want)


def row_pick(start_ref, length_ref, slot_ref, group, micros):
    parts = []
    for step in range(micros):
        slots = slot_ref[step]
        for block in range(CAP // BLK):
            micro = group * micros + step
            place = lax.broadcasted_iota(jnp.int32, (BLK, slots.shape[1]), 0)
            given = jnp.where(
                place < length_ref[micro, block], place + start_ref[micro, block], -1
            )
            parts.append((given == slots).astype(F32).astype(BF16))
    return jnp.concatenate(parts, axis=0)


def unpack_kernel(
    micros, with_norm, start_ref, length_ref, slot_ref, arrived_ref, gain_ref, *outs
):
    pick = row_pick(start_ref, length_ref, slot_ref, pl.program_id(0), micros)
    rows = dot(pick, arrived_ref[...].reshape(-1, D))
    outs[0][...] = rows.astype(BF16)
    if with_norm:
        outs[1][...] = (normed(rows)[0] * gain_ref[...]).astype(BF16)


def unpack_rows(arrived, starts, lengths, slots, gain, devices, micros, with_norm):
    groups = MICRO // micros
    width = slots.shape[-1]
    out_spec = pl.BlockSpec((micros * CAP, D), lambda g: (g, 0))
    out_type = jax.ShapeDtypeStruct((ROWS, D), BF16)
    count = 2 if with_norm else 1
    return pl.pallas_call(
        functools.partial(unpack_kernel, micros, with_norm),
        grid=(groups,),
        in_specs=[
            pl.BlockSpec(memory_space=pltpu.SMEM),
            pl.BlockSpec(memory_space=pltpu.SMEM),
            pl.BlockSpec((micros, 1, width), lambda g: (g, 0, 0)),
            pl.BlockSpec((devices, 1, CHUNK_ROWS, D), lambda g: (0, g, 0, 0)),
            pl.BlockSpec((1, D), lambda g: (0, 0)),
        ],
        out_specs=[out_spec] * count,
        out_shape=[out_type] * count,
        compiler_params=params(40),
        cost_estimate=cost(2 * ROWS * width * D, 4 * groups * width * D),
    )(starts, lengths, slots, arrived, gain)


def repack_kernel(micros, start_ref, length_ref, slot_ref, rows_ref, out_ref):
    pick = row_pick(start_ref, length_ref, slot_ref, pl.program_id(0), micros)
    out_ref[...] = dot(pick, rows_ref[...], 0, 0).astype(BF16).reshape(out_ref.shape)


def repack_rows(rows, starts, lengths, slots, devices, micros):
    groups = MICRO // micros
    width = slots.shape[-1]
    return pl.pallas_call(
        functools.partial(repack_kernel, micros),
        grid=(groups,),
        in_specs=[
            pl.BlockSpec(memory_space=pltpu.SMEM),
            pl.BlockSpec(memory_space=pltpu.SMEM),
            pl.BlockSpec((micros, 1, width), lambda g: (g, 0, 0)),
            pl.BlockSpec((micros * CAP, D), lambda g: (g, 0)),
        ],
        out_specs=pl.BlockSpec((devices, 1, CHUNK_ROWS, D), lambda g: (0, g, 0, 0)),
        out_shape=jax.ShapeDtypeStruct((devices, groups, CHUNK_ROWS, D), BF16),
        compiler_params=params(40),
        cost_estimate=cost(2 * ROWS * width * D, 4 * groups * width * D),
    )(starts, lengths, slots, rows)


QKV_TILE = 512


def qkv_kernel(act_ref, weight_ref, cos_ref, sin_ref, out_ref):
    packed = dot(act_ref[...], weight_ref[...])
    is_value = pl.program_id(0) >= 2 * D // QKV_TILE

    @pl.when(is_value)
    def _():
        out_ref[...] = packed.astype(BF16)

    @pl.when(jnp.logical_not(is_value))
    def _():
        split = packed.reshape(BLOCKS, BLK, QKV_TILE)
        spun = split * cos_ref[...][None] + turned(split) * sin_ref[...][None]
        out_ref[...] = spun.reshape(ROWS, QKV_TILE).astype(BF16)


def qkv_rows(act, weight, cosine, sine):
    return pl.pallas_call(
        qkv_kernel,
        grid=(3 * D // QKV_TILE,),
        in_specs=[
            pl.BlockSpec((ROWS, D), lambda j: (0, 0)),
            pl.BlockSpec((D, QKV_TILE), lambda j: (0, j)),
            pl.BlockSpec((BLK, QKV_TILE), lambda j: (0, 0)),
            pl.BlockSpec((BLK, QKV_TILE), lambda j: (0, 0)),
        ],
        out_specs=pl.BlockSpec((ROWS, QKV_TILE), lambda j: (0, j)),
        out_shape=jax.ShapeDtypeStruct((ROWS, 3 * D), BF16),
        compiler_params=params(40),
        cost_estimate=cost(2 * ROWS * D * 3 * D, 2 * (3 * D * D + ROWS * 4 * D)),
    )(act, weight, cosine, sine)


def head_masks(dtype):
    lane = lax.broadcasted_iota(jnp.int32, (BLK, LANES), 1)
    low = (lane < HD).astype(F32).astype(dtype)
    high = (lane >= HD).astype(F32).astype(dtype)
    return low, high


def attend_kernel(length_ref, q_ref, k_ref, v_ref, out_ref, prob_ref):
    block = pl.program_id(0)
    length = length_ref[block // 2, block % 2]
    low, high = head_masks(BF16)
    valid = lax.broadcasted_iota(jnp.int32, (BLK, BLK), 1) < length
    for pair in range(PAIRS):
        lanes = slice(pair * LANES, (pair + 1) * LANES)
        query, key, value = q_ref[:, lanes], k_ref[:, lanes], v_ref[:, lanes]
        scores = dot(query, jnp.concatenate([key * low, key * high], axis=0), 1, 1)
        parts = []
        for head in range(2):
            score = scores[:, head * BLK : (head + 1) * BLK] * SCALE
            score = jnp.where(valid, score, NEG)
            expo = jnp.exp(score - jnp.max(score, axis=-1, keepdims=True))
            parts.append(expo / jnp.sum(expo, axis=-1, keepdims=True))
        prob = jnp.concatenate(parts, axis=1).astype(BF16)
        prob_ref[0, pair] = prob
        both = jnp.concatenate([value * low, value * high], axis=0)
        out_ref[:, lanes] = dot(prob, both).astype(BF16)


def attend(qkv, lengths):
    return pl.pallas_call(
        attend_kernel,
        grid=(BLOCKS,),
        in_specs=[
            pl.BlockSpec(memory_space=pltpu.SMEM),
            pl.BlockSpec((BLK, D), lambda b: (b, 0)),
            pl.BlockSpec((BLK, D), lambda b: (b, 1)),
            pl.BlockSpec((BLK, D), lambda b: (b, 2)),
        ],
        out_specs=[
            pl.BlockSpec((BLK, D), lambda b: (b, 0)),
            pl.BlockSpec((1, PAIRS, BLK, 2 * BLK), lambda b: (b, 0, 0, 0)),
        ],
        out_shape=[
            jax.ShapeDtypeStruct((ROWS, D), BF16),
            jax.ShapeDtypeStruct((BLOCKS, PAIRS, BLK, 2 * BLK), BF16),
        ],
        compiler_params=params(32),
        cost_estimate=cost(8 * ROWS * BLK * D, 2 * ROWS * 6 * D, ROWS * HEADS * BLK),
    )(lengths, qkv, qkv, qkv)


def attend_back_kernel(
    q_ref, k_ref, v_ref, grad_ref, prob_ref, cos_ref, sin_ref, out_ref
):
    low, high = head_masks(BF16)
    lane = lax.broadcasted_iota(jnp.int32, (BLK, LANES), 1)
    is_low = lane < HD
    cosine, sine = cos_ref[...], sin_ref[...]
    for pair in range(PAIRS):
        lanes = slice(pair * LANES, (pair + 1) * LANES)
        query, key, value = q_ref[:, lanes], k_ref[:, lanes], v_ref[:, lanes]
        grad, prob = grad_ref[:, lanes], prob_ref[0, pair]
        grad_v = dot(prob, grad, 0, 0)
        grad_v = jnp.where(is_low, grad_v[:BLK], grad_v[BLK:])
        grad_p = dot(grad, jnp.concatenate([value * low, value * high], axis=0), 1, 1)
        parts = []
        for head in range(2):
            keys = slice(head * BLK, (head + 1) * BLK)
            weight, slope = prob[:, keys].astype(F32), grad_p[:, keys]
            inner = jnp.sum(weight * slope, axis=-1, keepdims=True)
            parts.append(weight * (slope - inner))
        grad_s = jnp.concatenate(parts, axis=1).astype(BF16)
        both = jnp.concatenate([key * low, key * high], axis=0)
        grad_q = dot(grad_s, both) * SCALE
        grad_k = dot(grad_s, query, 0, 0)
        grad_k = jnp.where(is_low, grad_k[:BLK], grad_k[BLK:]) * SCALE
        start = pair * LANES
        out_ref[:, start : start + LANES] = (
            grad_q * cosine - turned(grad_q) * sine
        ).astype(BF16)
        out_ref[:, D + start : D + start + LANES] = (
            grad_k * cosine - turned(grad_k) * sine
        ).astype(BF16)
        out_ref[:, 2 * D + start : 2 * D + start + LANES] = grad_v.astype(BF16)


def attend_back(qkv, grad_o, prob, cosine, sine):
    return pl.pallas_call(
        attend_back_kernel,
        grid=(BLOCKS,),
        in_specs=[
            pl.BlockSpec((BLK, D), lambda b: (b, 0)),
            pl.BlockSpec((BLK, D), lambda b: (b, 1)),
            pl.BlockSpec((BLK, D), lambda b: (b, 2)),
            pl.BlockSpec((BLK, D), lambda b: (b, 0)),
            pl.BlockSpec((1, PAIRS, BLK, 2 * BLK), lambda b: (b, 0, 0, 0)),
            pl.BlockSpec((BLK, LANES), lambda b: (0, 0)),
            pl.BlockSpec((BLK, LANES), lambda b: (0, 0)),
        ],
        out_specs=pl.BlockSpec((BLK, 3 * D), lambda b: (b, 0)),
        out_shape=jax.ShapeDtypeStruct((ROWS, 3 * D), BF16),
        compiler_params=params(32),
        cost_estimate=cost(20 * ROWS * BLK * D, 2 * ROWS * 9 * D),
    )(qkv, qkv, qkv, grad_o, prob, cosine, sine)


def middle_kernel(attn_ref, hidden_ref, weight_ref, gain_ref, mid_ref, act_ref):
    middle = hidden_ref[...].astype(F32) + dot(attn_ref[...], weight_ref[...])
    mid_ref[...] = middle
    act_ref[...] = (normed(middle)[0] * gain_ref[...]).astype(BF16)


def middle_rows(attn_o, hidden, weight, gain):
    tile = pl.BlockSpec((ROW_CHUNK, D), lambda i: (i, 0))
    return pl.pallas_call(
        middle_kernel,
        grid=(ROWS // ROW_CHUNK,),
        in_specs=[
            tile,
            tile,
            pl.BlockSpec((D, D), lambda i: (0, 0)),
            pl.BlockSpec((1, D), lambda i: (0, 0)),
        ],
        out_specs=[tile, tile],
        out_shape=[
            jax.ShapeDtypeStruct((ROWS, D), F32),
            jax.ShapeDtypeStruct((ROWS, D), BF16),
        ],
        compiler_params=params(32),
        cost_estimate=cost(2 * ROWS * D * D, 2 * D * D + 10 * ROWS * D),
    )(attn_o, hidden, weight, gain)


def ffn_kernel(
    act_ref,
    top_ref,
    mid_ref,
    gelu_w_ref,
    line_w_ref,
    down_ref,
    layer_ref,
    grad_b_ref,
    grad_gelu_ref,
    grad_line_ref,
    grad_down_ref,
    total,
    act_t,
    down_clean,
    kept_c,
    kept_gelu,
    kept_line,
):
    step = pl.program_id(0)

    @pl.when(step == 0)
    def _():
        total[...] = mid_ref[...]
        grad_b_ref[...] = jnp.zeros_like(grad_b_ref)
        act_t[...] = act_ref[...].T

    row = lax.broadcasted_iota(jnp.int32, (FF_TILE, D), 0) + step * FF_TILE
    down_clean[...] = jnp.where(row < FF, down_ref[...].astype(F32), 0.0).astype(BF16)

    def rows_step(index, carry):
        rows = pl.ds(pl.multiple_of(index * ROW_CHUNK, ROW_CHUNK), ROW_CHUNK)
        act, top = act_ref[rows, :], top_ref[rows, :]
        gelu_in = dot(act, gelu_w_ref[...])
        linear = dot(act, line_w_ref[...])
        grad_c = dot(top, down_clean[...], 1, 1)
        phi = 0.5 * (1.0 + lax.erf(gelu_in * ROOT_HALF))
        gelu_out = gelu_in * phi
        slope = phi + gelu_in * (jnp.exp(-0.5 * gelu_in * gelu_in) * INV_ROOT_TWO_PI)
        act_c = (gelu_out * linear).astype(BF16)
        grad_gelu = (grad_c * linear * slope).astype(BF16)
        grad_line = (grad_c * gelu_out).astype(BF16)
        kept_c[rows, :] = act_c
        kept_gelu[rows, :] = grad_gelu
        kept_line[rows, :] = grad_line
        total[rows, :] += dot(act_c, down_clean[...])
        grad_b_ref[rows, :] += dot(grad_gelu, gelu_w_ref[...], 1, 1) + dot(
            grad_line, line_w_ref[...], 1, 1
        )
        return carry

    lax.fori_loop(0, ROWS // ROW_CHUNK, rows_step, 0)
    grad_gelu_ref[...] = dot(act_t[...], kept_gelu[...]).astype(BF16)
    grad_line_ref[...] = dot(act_t[...], kept_line[...]).astype(BF16)
    grad_down_ref[...] = dot(kept_c[...], top_ref[...], 0, 0).astype(BF16)

    @pl.when(step == FF_STEPS - 1)
    def _():
        layer_ref[...] = total[...].astype(BF16)


def ffn(act, top, middle, full_in, full_down):
    whole = pl.BlockSpec((ROWS, D), lambda j: (0, 0))
    tall = pl.BlockSpec((D, FF_TILE), lambda j: (0, j))
    wide = pl.BlockSpec((FF_TILE, D), lambda j: (j, 0))
    return pl.pallas_call(
        ffn_kernel,
        grid=(FF_STEPS,),
        in_specs=[
            whole,
            whole,
            whole,
            tall,
            pl.BlockSpec((D, FF_TILE), lambda j: (0, j + FF_STEPS)),
            wide,
        ],
        out_specs=[whole, whole, tall, tall, wide],
        out_shape=[
            jax.ShapeDtypeStruct((ROWS, D), BF16),
            jax.ShapeDtypeStruct((ROWS, D), F32),
            jax.ShapeDtypeStruct((D, FF_PAD), BF16),
            jax.ShapeDtypeStruct((D, FF_PAD), BF16),
            jax.ShapeDtypeStruct((FF, D), BF16),
        ],
        scratch_shapes=[
            pltpu.VMEM((ROWS, D), F32),
            pltpu.VMEM((D, ROWS), BF16),
            pltpu.VMEM((FF_TILE, D), BF16),
            pltpu.VMEM((ROWS, FF_TILE), BF16),
            pltpu.VMEM((ROWS, FF_TILE), BF16),
            pltpu.VMEM((ROWS, FF_TILE), BF16),
        ],
        compiler_params=params(60),
        cost_estimate=cost(18 * ROWS * D * FF, 12 * D * FF, 2 * ROWS * FF),
    )(act, top, middle, full_in, full_in, full_down)


def branch_kernel(
    grad_b_ref,
    mid_ref,
    top_ref,
    attn_ref,
    weight_ref,
    gain_ref,
    grad_mid_ref,
    grad_o_ref,
    grad_w_ref,
    grad_gain_ref,
    total,
):
    step = pl.program_id(0)

    @pl.when(step == 0)
    def _():
        total[...] = jnp.zeros_like(total)
        grad_gain_ref[...] = jnp.zeros_like(grad_gain_ref)

    grad_b = grad_b_ref[...]
    normal, inverse = normed(mid_ref[...])
    grad_gain_ref[...] += jnp.sum(grad_b * normal, axis=0, keepdims=True)
    grad_mid = top_ref[...].astype(F32) + norm_back(
        grad_b * gain_ref[...], normal, inverse
    )
    grad_mid_ref[...] = grad_mid
    grad_r = grad_mid.astype(BF16)
    grad_o_ref[...] = dot(grad_r, weight_ref[...], 1, 1).astype(BF16)
    total[...] += dot(attn_ref[...], grad_r, 0, 0)

    @pl.when(step == ROWS // ROW_CHUNK - 1)
    def _():
        grad_w_ref[...] = total[...].astype(BF16)


def branch_back(grad_b, middle, top, attn_o, weight, gain):
    tile = pl.BlockSpec((ROW_CHUNK, D), lambda i: (i, 0))
    square = pl.BlockSpec((D, D), lambda i: (0, 0))
    line = pl.BlockSpec((1, D), lambda i: (0, 0))
    return pl.pallas_call(
        branch_kernel,
        grid=(ROWS // ROW_CHUNK,),
        in_specs=[tile, tile, tile, tile, square, line],
        out_specs=[tile, tile, square, line],
        out_shape=[
            jax.ShapeDtypeStruct((ROWS, D), F32),
            jax.ShapeDtypeStruct((ROWS, D), BF16),
            jax.ShapeDtypeStruct((D, D), BF16),
            jax.ShapeDtypeStruct((1, D), F32),
        ],
        scratch_shapes=[pltpu.VMEM((D, D), F32)],
        compiler_params=params(40),
        cost_estimate=cost(4 * ROWS * D * D, 4 * D * D + 18 * ROWS * D),
    )(grad_b, middle, top, attn_o, weight, gain)


def input_kernel(
    grad_qkv_ref, weight_ref, hidden_ref, grad_mid_ref, gain_ref, out_ref, grad_gain_ref
):
    @pl.when(pl.program_id(0) == 0)
    def _():
        grad_gain_ref[...] = jnp.zeros_like(grad_gain_ref)

    grad_a = dot(grad_qkv_ref[...], weight_ref[...], 1, 1)
    normal, inverse = normed(hidden_ref[...].astype(F32))
    grad_gain_ref[...] += jnp.sum(grad_a * normal, axis=0, keepdims=True)
    out_ref[...] = (
        grad_mid_ref[...] + norm_back(grad_a * gain_ref[...], normal, inverse)
    ).astype(BF16)


def input_back(grad_qkv, weight, hidden, grad_mid, gain):
    tile = pl.BlockSpec((ROW_CHUNK, D), lambda i: (i, 0))
    line = pl.BlockSpec((1, D), lambda i: (0, 0))
    return pl.pallas_call(
        input_kernel,
        grid=(ROWS // ROW_CHUNK,),
        in_specs=[
            pl.BlockSpec((ROW_CHUNK, 3 * D), lambda i: (i, 0)),
            pl.BlockSpec((D, 3 * D), lambda i: (0, 0)),
            tile,
            tile,
            line,
        ],
        out_specs=[tile, line],
        out_shape=[
            jax.ShapeDtypeStruct((ROWS, D), BF16),
            jax.ShapeDtypeStruct((1, D), F32),
        ],
        compiler_params=params(40),
        cost_estimate=cost(6 * ROWS * D * D, 6 * D * D + 14 * ROWS * D),
    )(grad_qkv, weight, hidden, grad_mid, gain)


def qkv_grad_kernel(act_ref, grad_ref, out_ref, act_t):
    @pl.when(pl.program_id(0) == 0)
    def _():
        act_t[...] = act_ref[...].T

    out_ref[...] = dot(act_t[...], grad_ref[...]).astype(BF16)


def qkv_grad(act, grad_qkv):
    return pl.pallas_call(
        qkv_grad_kernel,
        grid=(3 * D // QKV_TILE,),
        in_specs=[
            pl.BlockSpec((ROWS, D), lambda j: (0, 0)),
            pl.BlockSpec((ROWS, QKV_TILE), lambda j: (0, j)),
        ],
        out_specs=pl.BlockSpec((D, QKV_TILE), lambda j: (0, j)),
        out_shape=jax.ShapeDtypeStruct((D, 3 * D), BF16),
        scratch_shapes=[pltpu.VMEM((D, ROWS), BF16)],
        compiler_params=params(32),
        cost_estimate=cost(6 * ROWS * D * D, 2 * (7 * D * D)),
    )(act, grad_qkv)


def plan(seq_lengths, device, devices, micros):
    pair_cap = CAP // devices
    slots = devices * CHUNK_ROWS
    slot = jnp.arange(slots, dtype=jnp.int32)
    peer, inner = slot // CHUNK_ROWS, slot % CHUNK_ROWS
    rank, part = inner % pair_cap, inner // pair_cap
    micro = jnp.arange(MICRO, dtype=jnp.int32)
    mine = (micro % micros)[:, None] == part[None, :]
    seq = jnp.arange(seq_lengths.shape[1], dtype=jnp.int32)
    ahead = seq[None, :] < SEQ_DEV * peer[:, None]
    peer_start = jnp.sum(
        jnp.where(ahead[None], seq_lengths[:, None, :], 0), axis=2, dtype=jnp.int32
    )
    want = jnp.where(
        mine, (peer_start - device + devices - 1) // devices + rank[None, :], -1
    )
    own_seq = device * SEQ_DEV + jnp.arange(SEQ_DEV, dtype=jnp.int32)
    starts = jnp.sum(
        jnp.where(seq[None, None, :] < own_seq[None, :, None], seq_lengths[:, None, :], 0),
        axis=2,
        dtype=jnp.int32,
    )
    lengths = jnp.sum(
        jnp.where(seq[None, None, :] == own_seq[None, :, None], seq_lengths[:, None, :], 0),
        axis=2,
        dtype=jnp.int32,
    )
    first = (starts[:, :1] - peer[None, :] + devices - 1) // devices
    given = jnp.where(mine, (first + rank[None, :]) * devices + peer[None, :], -2)
    return want[:, None, :], starts, lengths, given[:, None, :]


def body(tokens, cotangent, seq_lengths, w_qkv, w_out, w_in, w_down, attn_gain, mlp_gain):
    group_size = lax.axis_size("grp")
    devices = lax.axis_size("rep") * group_size
    device = lax.axis_index("rep") * group_size + lax.axis_index("grp")
    micros = min(MICRO, max(1, CHUNK_ROWS * devices // CAP))
    both = ("rep", "grp")

    def swap(rows):
        return lax.all_to_all(rows, both, split_axis=0, concat_axis=0, tiled=True)

    def gather(rows):
        return lax.all_gather(rows, "grp", axis=0, tiled=True)

    want, starts, lengths, given = plan(seq_lengths, device, devices, micros)
    token_rows = swap(pack_rows(tokens[:, :, 0], want, devices, micros))
    top_rows = swap(pack_rows(cotangent[:, :, 0], want, devices, micros))
    gains = lax.all_gather(jnp.stack([attn_gain, mlp_gain]), "grp", axis=1, tiled=True)
    gain_one = gains[:1].astype(F32)
    gain_two = gains[1:].astype(F32)
    full_qkv = gather(w_qkv)
    full_out = gather(w_out)
    gap = jnp.zeros((w_in.shape[0], FF_PAD - FF), BF16)
    full_in = gather(jnp.concatenate([w_in[:, :FF], gap, w_in[:, FF:], gap], axis=1))
    full_down = gather(w_down)

    cosine, sine = rotary_tables(QKV_TILE)
    hidden, act_a = unpack_rows(
        token_rows, starts, lengths, given, gain_one, devices, micros, True
    )
    (top,) = unpack_rows(
        top_rows, starts, lengths, given, gain_one, devices, micros, False
    )
    qkv = qkv_rows(act_a, full_qkv, cosine, sine)
    attn_o, prob = attend(qkv, lengths)
    middle, act_b = middle_rows(attn_o, hidden, full_out, gain_two)
    layer_rows, grad_b, grad_gelu_w, grad_line_w, grad_down_w = ffn(
        act_b, top, middle, full_in, full_down
    )
    layer_back = swap(repack_rows(layer_rows, starts, lengths, given, devices, micros))

    def owned(part):
        return lax.psum_scatter(part, "grp", scatter_dimension=0, tiled=True)

    def summed(part):
        return lax.psum(part, "rep")

    grad_down = summed(owned(grad_down_w))
    grad_gelu = summed(owned(grad_gelu_w))
    grad_line = summed(owned(grad_line_w))
    grad_mid, grad_o, grad_out_w, grad_gain_two = branch_back(
        grad_b, middle, top, attn_o, full_out, gain_two
    )
    grad_out = summed(owned(grad_out_w))
    grad_qkv_rows = attend_back(qkv, grad_o, prob, cosine[:, :LANES], sine[:, :LANES])
    grad_qkv_w = qkv_grad(act_a, grad_qkv_rows)
    grad_qkv = summed(owned(grad_qkv_w))
    grad_rows, grad_gain_one = input_back(
        grad_qkv_rows, full_qkv, hidden, grad_mid, gain_one
    )
    grad_back = swap(repack_rows(grad_rows, starts, lengths, given, devices, micros))
    gain_parts = jnp.concatenate([grad_gain_one, grad_gain_two], axis=0)
    gain_parts = gain_parts.reshape(2, 1, group_size, -1)
    gain_parts = jnp.broadcast_to(
        gain_parts, (2, devices // group_size, *gain_parts.shape[2:])
    ).reshape(2, devices, -1)
    gain_sums = jnp.sum(
        lax.all_to_all(gain_parts, both, split_axis=1, concat_axis=1, tiled=True), axis=1
    )
    layer_out = spread_rows(layer_back, want, devices, micros)[:, :, None, :]
    grad_tokens = spread_rows(grad_back, want, devices, micros)[:, :, None, :]
    return (
        layer_out,
        grad_tokens,
        gain_sums[0],
        gain_sums[1],
        grad_qkv.astype(F32),
        grad_out.astype(F32),
        jnp.concatenate([grad_gelu[:, :FF], grad_line[:, :FF]], axis=1).astype(F32),
        grad_down.astype(F32),
    )


def solution(mesh):
    return jax.shard_map(
        body,
        mesh=mesh,
        in_specs=(
            P(None, None, ("rep", "grp"), None),
            P(None, None, ("rep", "grp"), None),
            P(),
            P("grp", None),
            P("grp", None),
            P("grp", None),
            P("grp", None),
            P("grp"),
            P("grp"),
        ),
        out_specs=(
            P(None, None, ("rep", "grp"), None),
            P(None, None, ("rep", "grp"), None),
            P("grp"),
            P("grp"),
            P("grp", None),
            P("grp", None),
            P("grp", None),
            P("grp", None),
        ),
        check_vma=False,
    )
```

```python
import functools
import math

import jax
import jax.numpy as jnp
import numpy as np
from jax import lax
from jax.experimental import pallas as pl
from jax.experimental.pallas import tpu as pltpu
from jax.sharding import PartitionSpec as P

D = 1024
HEADS = 16
HD = 64
FF = 2624
BLK = 128
MICRO = 4
SEQ_DEV = 2
CAP = 256
TOK_DEV = 192
ROWS = MICRO * CAP
BLOCKS = ROWS // BLK
PAIRS = HEADS // 2
LANES = 2 * HD

EPS = 1e-05
THETA = 160000.0
NEG = -1e30
ROOT_HALF = math.sqrt(0.5)
INV_ROOT_TWO_PI = 1.0 / math.sqrt(2.0 * math.pi)
SCALE = HD**-0.5

FF_TILE = 384
FF_STEPS = -(-FF // FF_TILE)
FF_PAD = FF_STEPS * FF_TILE
ROW_CHUNK = 256
CHUNK_ROWS = 16
SHARDS = 8
REPLICAS = 4

F32 = jnp.float32
BF16 = jnp.bfloat16
MIB = 1 << 20


def dot(left, right, left_dim=1, right_dim=0):
    return lax.dot_general(
        left, right, (((left_dim,), (right_dim,)), ((), ())), preferred_element_type=F32
    )


def params(mib, steps=1):
    return pltpu.CompilerParams(
        vmem_limit_bytes=mib * MIB, dimension_semantics=("arbitrary",) * steps
    )


def cost(flops, moved, transcendentals=0):
    return pl.CostEstimate(
        flops=flops, bytes_accessed=moved, transcendentals=transcendentals
    )


def normed(values):
    center = values - jnp.mean(values, axis=-1, keepdims=True)
    inverse = lax.rsqrt(jnp.mean(center * center, axis=-1, keepdims=True) + EPS)
    return center * inverse, inverse


def norm_back(grad, normal, inverse):
    centred = grad - jnp.mean(grad, axis=-1, keepdims=True)
    return inverse * (centred - normal * jnp.mean(grad * normal, axis=-1, keepdims=True))


def rotary_tables(width):
    half = HD // 2
    frequency = THETA ** (-2.0 * jnp.arange(half, dtype=F32) / HD)
    angles = jnp.arange(BLK, dtype=F32)[:, None] * frequency[None, :]
    cosine, sine = jnp.cos(angles), jnp.sin(angles)
    cosine = jnp.concatenate([cosine, cosine], axis=1)
    sine = jnp.concatenate([-sine, sine], axis=1)
    return (jnp.tile(cosine, (1, width // HD)), jnp.tile(sine, (1, width // HD)))


def turned(values):
    axis = values.ndim - 1
    half = HD // 2
    width = values.shape[axis]
    lane = lax.broadcasted_iota(jnp.int32, values.shape, axis) % HD
    return jnp.where(
        lane < half,
        pltpu.roll(values, width - half, axis),
        pltpu.roll(values, half, axis),
    )


def pack_kernel(micros, rows_ref, want_ref, out_ref):
    total = None
    for step in range(micros):
        want = want_ref[step]
        mine = lax.broadcasted_iota(jnp.int32, (TOK_DEV, want.shape[1]), 0)
        pick = (mine == want).astype(F32).astype(BF16)
        term = dot(pick, rows_ref[step], 0, 0)
        total = term if total is None else total + term
    out_ref[...] = total.astype(BF16).reshape(out_ref.shape)


def pack_rows(rows, want, devices, micros):
    groups = MICRO // micros
    slots = want.shape[-1]
    return pl.pallas_call(
        functools.partial(pack_kernel, micros),
        grid=(groups,),
        in_specs=[
            pl.BlockSpec((micros, TOK_DEV, D), lambda g: (g, 0, 0)),
            pl.BlockSpec((micros, 1, slots), lambda g: (g, 0, 0)),
        ],
        out_specs=pl.BlockSpec((devices, 1, CHUNK_ROWS, D), lambda g: (0, g, 0, 0)),
        out_shape=jax.ShapeDtypeStruct((devices, groups, CHUNK_ROWS, D), BF16),
        compiler_params=params(40),
        cost_estimate=cost(2 * MICRO * TOK_DEV * slots * D, 4 * groups * slots * D),
    )(rows, want)


def spread_kernel(micros, back_ref, want_ref, out_ref):
    arrived = back_ref[...].reshape(-1, D)
    for step in range(micros):
        want = want_ref[step]
        mine = lax.broadcasted_iota(jnp.int32, (TOK_DEV, want.shape[1]), 0)
        pick = (mine == want).astype(F32).astype(BF16)
        out_ref[step] = dot(pick, arrived).astype(BF16)


def spread_rows(back, want, devices, micros):
    groups = MICRO // micros
    slots = want.shape[-1]
    return pl.pallas_call(
        functools.partial(spread_kernel, micros),
        grid=(groups,),
        in_specs=[
            pl.BlockSpec((devices, 1, CHUNK_ROWS, D), lambda g: (0, g, 0, 0)),
            pl.BlockSpec((micros, 1, slots), lambda g: (g, 0, 0)),
        ],
        out_specs=pl.BlockSpec((micros, TOK_DEV, D), lambda g: (g, 0, 0)),
        out_shape=jax.ShapeDtypeStruct((MICRO, TOK_DEV, D), BF16),
        compiler_params=params(40),
        cost_estimate=cost(2 * MICRO * TOK_DEV * slots * D, 4 * groups * slots * D),
    )(back, want)


def row_pick(start_ref, length_ref, slot_ref, group, micros):
    parts = []
    for step in range(micros):
        slots = slot_ref[step]
        for block in range(CAP // BLK):
            micro = group * micros + step
            place = lax.broadcasted_iota(jnp.int32, (BLK, slots.shape[1]), 0)
            given = jnp.where(
                place < length_ref[micro, block], place + start_ref[micro, block], -1
            )
            parts.append((given == slots).astype(F32).astype(BF16))
    return jnp.concatenate(parts, axis=0)


def unpack_kernel(
    micros, with_norm, start_ref, length_ref, slot_ref, arrived_ref, gain_ref, *outs
):
    pick = row_pick(start_ref, length_ref, slot_ref, pl.program_id(0), micros)
    rows = dot(pick, arrived_ref[...].reshape(-1, D))
    outs[0][...] = rows.astype(BF16)
    if with_norm:
        outs[1][...] = (normed(rows)[0] * gain_ref[...]).astype(BF16)


def unpack_rows(arrived, starts, lengths, slots, gain, devices, micros, with_norm):
    groups = MICRO // micros
    width = slots.shape[-1]
    out_spec = pl.BlockSpec((micros * CAP, D), lambda g: (g, 0))
    out_type = jax.ShapeDtypeStruct((ROWS, D), BF16)
    count = 2 if with_norm else 1
    return pl.pallas_call(
        functools.partial(unpack_kernel, micros, with_norm),
        grid=(groups,),
        in_specs=[
            pl.BlockSpec(memory_space=pltpu.SMEM),
            pl.BlockSpec(memory_space=pltpu.SMEM),
            pl.BlockSpec((micros, 1, width), lambda g: (g, 0, 0)),
            pl.BlockSpec((devices, 1, CHUNK_ROWS, D), lambda g: (0, g, 0, 0)),
            pl.BlockSpec((1, D), lambda g: (0, 0)),
        ],
        out_specs=[out_spec] * count,
        out_shape=[out_type] * count,
        compiler_params=params(40),
        cost_estimate=cost(2 * ROWS * width * D, 4 * groups * width * D),
    )(starts, lengths, slots, arrived, gain)


def repack_kernel(micros, start_ref, length_ref, slot_ref, rows_ref, out_ref):
    pick = row_pick(start_ref, length_ref, slot_ref, pl.program_id(0), micros)
    out_ref[...] = dot(pick, rows_ref[...], 0, 0).astype(BF16).reshape(out_ref.shape)


def repack_rows(rows, starts, lengths, slots, devices, micros):
    groups = MICRO // micros
    width = slots.shape[-1]
    return pl.pallas_call(
        functools.partial(repack_kernel, micros),
        grid=(groups,),
        in_specs=[
            pl.BlockSpec(memory_space=pltpu.SMEM),
            pl.BlockSpec(memory_space=pltpu.SMEM),
            pl.BlockSpec((micros, 1, width), lambda g: (g, 0, 0)),
            pl.BlockSpec((micros * CAP, D), lambda g: (g, 0)),
        ],
        out_specs=pl.BlockSpec((devices, 1, CHUNK_ROWS, D), lambda g: (0, g, 0, 0)),
        out_shape=jax.ShapeDtypeStruct((devices, groups, CHUNK_ROWS, D), BF16),
        compiler_params=params(40),
        cost_estimate=cost(2 * ROWS * width * D, 4 * groups * width * D),
    )(starts, lengths, slots, rows)


QKV_TILE = 512


def qkv_kernel(act_ref, weight_ref, cos_ref, sin_ref, out_ref):
    packed = dot(act_ref[...], weight_ref[...])
    is_value = pl.program_id(0) >= 2 * D // QKV_TILE

    @pl.when(is_value)
    def _():
        out_ref[...] = packed.astype(BF16)

    @pl.when(jnp.logical_not(is_value))
    def _():
        split = packed.reshape(BLOCKS, BLK, QKV_TILE)
        spun = split * cos_ref[...][None] + turned(split) * sin_ref[...][None]
        out_ref[...] = spun.reshape(ROWS, QKV_TILE).astype(BF16)


def qkv_rows(act, weight, cosine, sine):
    return pl.pallas_call(
        qkv_kernel,
        grid=(3 * D // QKV_TILE,),
        in_specs=[
            pl.BlockSpec((ROWS, D), lambda j: (0, 0)),
            pl.BlockSpec((D, QKV_TILE), lambda j: (0, j)),
            pl.BlockSpec((BLK, QKV_TILE), lambda j: (0, 0)),
            pl.BlockSpec((BLK, QKV_TILE), lambda j: (0, 0)),
        ],
        out_specs=pl.BlockSpec((ROWS, QKV_TILE), lambda j: (0, j)),
        out_shape=jax.ShapeDtypeStruct((ROWS, 3 * D), BF16),
        compiler_params=params(40),
        cost_estimate=cost(2 * ROWS * D * 3 * D, 2 * (3 * D * D + ROWS * 4 * D)),
    )(act, weight, cosine, sine)


def head_masks(dtype):
    lane = lax.broadcasted_iota(jnp.int32, (BLK, LANES), 1)
    low = (lane < HD).astype(F32).astype(dtype)
    high = (lane >= HD).astype(F32).astype(dtype)
    return low, high


def attend_kernel(length_ref, q_ref, k_ref, v_ref, out_ref, prob_ref):
    block = pl.program_id(0)
    length = length_ref[block // 2, block % 2]
    low, high = head_masks(BF16)
    valid = lax.broadcasted_iota(jnp.int32, (BLK, BLK), 1) < length
    for pair in range(PAIRS):
        lanes = slice(pair * LANES, (pair + 1) * LANES)
        query, key, value = q_ref[:, lanes], k_ref[:, lanes], v_ref[:, lanes]
        scores = dot(query, jnp.concatenate([key * low, key * high], axis=0), 1, 1)
        parts = []
        for head in range(2):
            score = scores[:, head * BLK : (head + 1) * BLK] * SCALE
            score = jnp.where(valid, score, NEG)
            expo = jnp.exp(score - jnp.max(score, axis=-1, keepdims=True))
            parts.append(expo / jnp.sum(expo, axis=-1, keepdims=True))
        prob = jnp.concatenate(parts, axis=1).astype(BF16)
        prob_ref[0, pair] = prob
        both = jnp.concatenate([value * low, value * high], axis=0)
        out_ref[:, lanes] = dot(prob, both).astype(BF16)


def attend(qkv, lengths):
    return pl.pallas_call(
        attend_kernel,
        grid=(BLOCKS,),
        in_specs=[
            pl.BlockSpec(memory_space=pltpu.SMEM),
            pl.BlockSpec((BLK, D), lambda b: (b, 0)),
            pl.BlockSpec((BLK, D), lambda b: (b, 1)),
            pl.BlockSpec((BLK, D), lambda b: (b, 2)),
        ],
        out_specs=[
            pl.BlockSpec((BLK, D), lambda b: (b, 0)),
            pl.BlockSpec((1, PAIRS, BLK, 2 * BLK), lambda b: (b, 0, 0, 0)),
        ],
        out_shape=[
            jax.ShapeDtypeStruct((ROWS, D), BF16),
            jax.ShapeDtypeStruct((BLOCKS, PAIRS, BLK, 2 * BLK), BF16),
        ],
        compiler_params=params(32),
        cost_estimate=cost(8 * ROWS * BLK * D, 2 * ROWS * 6 * D, ROWS * HEADS * BLK),
    )(lengths, qkv, qkv, qkv)


def attend_back_kernel(
    q_ref, k_ref, v_ref, grad_ref, prob_ref, cos_ref, sin_ref, out_ref
):
    low, high = head_masks(BF16)
    lane = lax.broadcasted_iota(jnp.int32, (BLK, LANES), 1)
    is_low = lane < HD
    cosine, sine = cos_ref[...], sin_ref[...]
    for pair in range(PAIRS):
        lanes = slice(pair * LANES, (pair + 1) * LANES)
        query, key, value = q_ref[:, lanes], k_ref[:, lanes], v_ref[:, lanes]
        grad, prob = grad_ref[:, lanes], prob_ref[0, pair]
        grad_v = dot(prob, grad, 0, 0)
        grad_v = jnp.where(is_low, grad_v[:BLK], grad_v[BLK:])
        grad_p = dot(grad, jnp.concatenate([value * low, value * high], axis=0), 1, 1)
        parts = []
        for head in range(2):
            keys = slice(head * BLK, (head + 1) * BLK)
            weight, slope = prob[:, keys].astype(F32), grad_p[:, keys]
            inner = jnp.sum(weight * slope, axis=-1, keepdims=True)
            parts.append(weight * (slope - inner))
        grad_s = jnp.concatenate(parts, axis=1).astype(BF16)
        both = jnp.concatenate([key * low, key * high], axis=0)
        grad_q = dot(grad_s, both) * SCALE
        grad_k = dot(grad_s, query, 0, 0)
        grad_k = jnp.where(is_low, grad_k[:BLK], grad_k[BLK:]) * SCALE
        start = pair * LANES
        out_ref[:, start : start + LANES] = (
            grad_q * cosine - turned(grad_q) * sine
        ).astype(BF16)
        out_ref[:, D + start : D + start + LANES] = (
            grad_k * cosine - turned(grad_k) * sine
        ).astype(BF16)
        out_ref[:, 2 * D + start : 2 * D + start + LANES] = grad_v.astype(BF16)


def attend_back(qkv, grad_o, prob, cosine, sine):
    return pl.pallas_call(
        attend_back_kernel,
        grid=(BLOCKS,),
        in_specs=[
            pl.BlockSpec((BLK, D), lambda b: (b, 0)),
            pl.BlockSpec((BLK, D), lambda b: (b, 1)),
            pl.BlockSpec((BLK, D), lambda b: (b, 2)),
            pl.BlockSpec((BLK, D), lambda b: (b, 0)),
            pl.BlockSpec((1, PAIRS, BLK, 2 * BLK), lambda b: (b, 0, 0, 0)),
            pl.BlockSpec((BLK, LANES), lambda b: (0, 0)),
            pl.BlockSpec((BLK, LANES), lambda b: (0, 0)),
        ],
        out_specs=pl.BlockSpec((BLK, 3 * D), lambda b: (b, 0)),
        out_shape=jax.ShapeDtypeStruct((ROWS, 3 * D), BF16),
        compiler_params=params(32),
        cost_estimate=cost(20 * ROWS * BLK * D, 2 * ROWS * 9 * D),
    )(qkv, qkv, qkv, grad_o, prob, cosine, sine)


def middle_kernel(attn_ref, hidden_ref, weight_ref, gain_ref, mid_ref, act_ref):
    middle = hidden_ref[...].astype(F32) + dot(attn_ref[...], weight_ref[...])
    mid_ref[...] = middle
    act_ref[...] = (normed(middle)[0] * gain_ref[...]).astype(BF16)


def middle_rows(attn_o, hidden, weight, gain):
    tile = pl.BlockSpec((ROW_CHUNK, D), lambda i: (i, 0))
    return pl.pallas_call(
        middle_kernel,
        grid=(ROWS // ROW_CHUNK,),
        in_specs=[
            tile,
            tile,
            pl.BlockSpec((D, D), lambda i: (0, 0)),
            pl.BlockSpec((1, D), lambda i: (0, 0)),
        ],
        out_specs=[tile, tile],
        out_shape=[
            jax.ShapeDtypeStruct((ROWS, D), F32),
            jax.ShapeDtypeStruct((ROWS, D), BF16),
        ],
        compiler_params=params(32),
        cost_estimate=cost(2 * ROWS * D * D, 2 * D * D + 10 * ROWS * D),
    )(attn_o, hidden, weight, gain)


def ffn_kernel(
    act_ref,
    top_ref,
    mid_ref,
    in_ref,
    down_ref,
    layer_ref,
    grad_b_ref,
    grad_in_ref,
    grad_down_ref,
    total,
    act_t,
    down_clean,
    kept_c,
    kept_gu,
):
    step = pl.program_id(0)

    @pl.when(step == 0)
    def _():
        total[...] = mid_ref[...]
        grad_b_ref[...] = jnp.zeros_like(grad_b_ref)
        act_t[...] = act_ref[...].T

    row = lax.broadcasted_iota(jnp.int32, (FF_TILE, D), 0) + step * FF_TILE
    down_clean[...] = jnp.where(row < FF, down_ref[...].astype(F32), 0.0).astype(BF16)

    def rows_step(index, carry):
        rows = pl.ds(pl.multiple_of(index * ROW_CHUNK, ROW_CHUNK), ROW_CHUNK)
        act, top = act_ref[rows, :], top_ref[rows, :]
        gate_up = dot(act, in_ref[...])
        gelu_in, linear = gate_up[:, :FF_TILE], gate_up[:, FF_TILE:]
        grad_c = dot(top, down_clean[...], 1, 1)
        phi = 0.5 * (1.0 + lax.erf(gelu_in * ROOT_HALF))
        gelu_out = gelu_in * phi
        slope = phi + gelu_in * (jnp.exp(-0.5 * gelu_in * gelu_in) * INV_ROOT_TWO_PI)
        act_c = (gelu_out * linear).astype(BF16)
        kept_c[rows, :] = act_c
        kept_gu[rows, :FF_TILE] = (grad_c * linear * slope).astype(BF16)
        kept_gu[rows, FF_TILE:] = (grad_c * gelu_out).astype(BF16)
        total[rows, :] += dot(act_c, down_clean[...])
        grad_b_ref[rows, :] += dot(kept_gu[rows, :], in_ref[...], 1, 1)
        return carry

    lax.fori_loop(0, ROWS // ROW_CHUNK, rows_step, 0)
    grad_in_ref[...] = dot(act_t[...], kept_gu[...]).astype(BF16)
    grad_down_ref[...] = dot(kept_c[...], top_ref[...], 0, 0).astype(BF16)

    @pl.when(step == FF_STEPS - 1)
    def _():
        layer_ref[...] = total[...].astype(BF16)


def ffn(act, top, middle, full_in, full_down):
    whole = pl.BlockSpec((ROWS, D), lambda j: (0, 0))
    tall = pl.BlockSpec((D, 2 * FF_TILE), lambda j: (0, j))
    wide = pl.BlockSpec((FF_TILE, D), lambda j: (j, 0))
    return pl.pallas_call(
        ffn_kernel,
        grid=(FF_STEPS,),
        in_specs=[
            whole,
            whole,
            whole,
            tall,
            wide,
        ],
        out_specs=[whole, whole, tall, wide],
        out_shape=[
            jax.ShapeDtypeStruct((ROWS, D), BF16),
            jax.ShapeDtypeStruct((ROWS, D), F32),
            jax.ShapeDtypeStruct((D, 2 * FF_PAD), BF16),
            jax.ShapeDtypeStruct((FF, D), BF16),
        ],
        scratch_shapes=[
            pltpu.VMEM((ROWS, D), F32),
            pltpu.VMEM((D, ROWS), BF16),
            pltpu.VMEM((FF_TILE, D), BF16),
            pltpu.VMEM((ROWS, FF_TILE), BF16),
            pltpu.VMEM((ROWS, 2 * FF_TILE), BF16),
        ],
        compiler_params=params(60),
        cost_estimate=cost(18 * ROWS * D * FF, 12 * D * FF, 2 * ROWS * FF),
    )(act, top, middle, full_in, full_down)


def branch_kernel(
    grad_b_ref,
    mid_ref,
    top_ref,
    attn_ref,
    weight_ref,
    gain_ref,
    grad_mid_ref,
    grad_o_ref,
    grad_w_ref,
    grad_gain_ref,
    total,
):
    step = pl.program_id(0)

    @pl.when(step == 0)
    def _():
        total[...] = jnp.zeros_like(total)
        grad_gain_ref[...] = jnp.zeros_like(grad_gain_ref)

    grad_b = grad_b_ref[...]
    normal, inverse = normed(mid_ref[...])
    grad_gain_ref[...] += jnp.sum(grad_b * normal, axis=0, keepdims=True)
    grad_mid = top_ref[...].astype(F32) + norm_back(
        grad_b * gain_ref[...], normal, inverse
    )
    grad_mid_ref[...] = grad_mid
    grad_r = grad_mid.astype(BF16)
    grad_o_ref[...] = dot(grad_r, weight_ref[...], 1, 1).astype(BF16)
    total[...] += dot(attn_ref[...], grad_r, 0, 0)

    @pl.when(step == ROWS // ROW_CHUNK - 1)
    def _():
        grad_w_ref[...] = total[...].astype(BF16)


def branch_back(grad_b, middle, top, attn_o, weight, gain):
    tile = pl.BlockSpec((ROW_CHUNK, D), lambda i: (i, 0))
    square = pl.BlockSpec((D, D), lambda i: (0, 0))
    line = pl.BlockSpec((1, D), lambda i: (0, 0))
    return pl.pallas_call(
        branch_kernel,
        grid=(ROWS // ROW_CHUNK,),
        in_specs=[
            *[tile] * 4,
            square,
            line,
        ],
        out_specs=[tile, tile, square, line],
        out_shape=[
            jax.ShapeDtypeStruct((ROWS, D), F32),
            jax.ShapeDtypeStruct((ROWS, D), BF16),
            jax.ShapeDtypeStruct((D, D), BF16),
            jax.ShapeDtypeStruct((1, D), F32),
        ],
        scratch_shapes=[pltpu.VMEM((D, D), F32)],
        compiler_params=params(40),
        cost_estimate=cost(4 * ROWS * D * D, 4 * D * D + 18 * ROWS * D),
    )(grad_b, middle, top, attn_o, weight, gain)


def input_kernel(
    grad_qkv_ref, weight_ref, hidden_ref, grad_mid_ref, gain_ref, out_ref, grad_gain_ref
):
    @pl.when(pl.program_id(0) == 0)
    def _():
        grad_gain_ref[...] = jnp.zeros_like(grad_gain_ref)

    grad_a = dot(grad_qkv_ref[...], weight_ref[...], 1, 1)
    normal, inverse = normed(hidden_ref[...].astype(F32))
    grad_gain_ref[...] += jnp.sum(grad_a * normal, axis=0, keepdims=True)
    out_ref[...] = (
        grad_mid_ref[...] + norm_back(grad_a * gain_ref[...], normal, inverse)
    ).astype(BF16)


def input_back(grad_qkv, weight, hidden, grad_mid, gain):
    tile = pl.BlockSpec((ROW_CHUNK, D), lambda i: (i, 0))
    line = pl.BlockSpec((1, D), lambda i: (0, 0))
    return pl.pallas_call(
        input_kernel,
        grid=(ROWS // ROW_CHUNK,),
        in_specs=[
            pl.BlockSpec((ROW_CHUNK, 3 * D), lambda i: (i, 0)),
            pl.BlockSpec((D, 3 * D), lambda i: (0, 0)),
            tile,
            tile,
            line,
        ],
        out_specs=[tile, line],
        out_shape=[
            jax.ShapeDtypeStruct((ROWS, D), BF16),
            jax.ShapeDtypeStruct((1, D), F32),
        ],
        compiler_params=params(40),
        cost_estimate=cost(6 * ROWS * D * D, 6 * D * D + 14 * ROWS * D),
    )(grad_qkv, weight, hidden, grad_mid, gain)


def qkv_grad_kernel(act_ref, grad_ref, out_ref, act_t):
    @pl.when(pl.program_id(0) == 0)
    def _():
        act_t[...] = act_ref[...].T

    out_ref[...] = dot(act_t[...], grad_ref[...]).astype(BF16)


def qkv_grad(act, grad_qkv):
    return pl.pallas_call(
        qkv_grad_kernel,
        grid=(3 * D // QKV_TILE,),
        in_specs=[
            pl.BlockSpec((ROWS, D), lambda j: (0, 0)),
            pl.BlockSpec((ROWS, QKV_TILE), lambda j: (0, j)),
        ],
        out_specs=pl.BlockSpec((D, QKV_TILE), lambda j: (0, j)),
        out_shape=jax.ShapeDtypeStruct((D, 3 * D), BF16),
        scratch_shapes=[pltpu.VMEM((D, ROWS), BF16)],
        compiler_params=params(32),
        cost_estimate=cost(6 * ROWS * D * D, 2 * (7 * D * D)),
    )(act, grad_qkv)


MESH = pl.DeviceIdType.MESH
REDUCE_CHUNKS = (
    (0, 0, 512),
    (0, 512, 512),
    (1, 0, 1792),
    (1, 1792, 1792),
    (1, 3584, 1792),
    (2, 0, 1024),
    (3, 0, 1536),
    (3, 1536, 1536),
)
HOP_CORE, HOP_X, HOP_Y, HOP_XY, HOP_YX, HOP_IN, HOP_MID, HOP_OUT = range(8)


def place():
    rep, grp = lax.axis_index("rep"), lax.axis_index("grp")
    core, x, y = grp % 2, grp // 2 % 2, grp // 4
    return rep, grp, core, x, y, grp + 1 - 2 * core, grp + 2 - 4 * x, grp + 4 - 8 * y


def reduce_kernel(*refs):
    tensors, refs = refs[:4], refs[4:]
    outs, refs = refs[:4], refs[4:]
    chunks = len(REDUCE_CHUNKS)
    sums, from_core, from_near, from_cross, from_far = (
        refs[i * chunks : (i + 1) * chunks] for i in range(5)
    )
    load_sem, send_sem, recv_sem, store_sem = refs[5 * chunks :]
    rep, grp, core, x, y, by_core, by_x, by_y = place()
    is_middle = (rep == 1) | (rep == 2)
    inward, outward, across = 1 + rep // 2, 3 * (rep // 2), 3 - rep

    barrier = pltpu.get_barrier_semaphore()
    for near in (by_core, by_x, by_y):
        pl.semaphore_signal(barrier, device_id=(rep, near), device_id_type=MESH)

    @pl.when(is_middle)
    def _():
        pl.semaphore_signal(barrier, device_id=(across, grp), device_id_type=MESH)
        pl.semaphore_signal(barrier, device_id=(outward, grp), device_id_type=MESH)
        pl.semaphore_wait(barrier, 5)

    @pl.when(jnp.logical_not(is_middle))
    def _():
        pl.semaphore_signal(barrier, device_id=(inward, grp), device_id_type=MESH)
        pl.semaphore_wait(barrier, 4)

    def hop(chunk, which):
        tensor, start, width = REDUCE_CHUNKS[chunk]
        half = width // 2
        left, right, columns = pl.ds(0, half), pl.ds(half, half), pl.ds(start, width)
        total, far = sums[chunk], from_far[chunk]
        near, cross = from_near[chunk], from_cross[chunk]
        if which == HOP_CORE:
            source, target = tensors[tensor].at[:, :, 1 - core, :, columns], from_core[chunk]
        elif which == HOP_X:
            source, target = total.at[:, 1 - x, :, left], near.at[0]
        elif which == HOP_Y:
            source, target = total.at[1 - y, :, :, right], near.at[1]
        elif which == HOP_XY:
            source, target = total.at[1 - y, x, :, left], cross.at[0]
        elif which == HOP_YX:
            source, target = total.at[y, 1 - x, :, right], cross.at[1]
        elif which == HOP_IN:
            source, target = total.at[y, x], far.at[0]
        elif which == HOP_MID:
            source, target = total.at[y, x], far.at[1]
        else:
            source, target = far.at[0], outs[tensor].at[:, columns]
        to_rep = (rep, rep, rep, rep, rep, inward, across, outward)[which]
        to_grp = (by_core, by_x, by_y, by_y, by_x, grp, grp, grp)[which]
        return pltpu.make_async_remote_copy(
            src_ref=source,
            dst_ref=target,
            send_sem=send_sem.at[chunk, which],
            recv_sem=recv_sem.at[chunk, which],
            device_id=(to_rep, to_grp),
            device_id_type=MESH,
        )

    def load(chunk):
        tensor, start, width = REDUCE_CHUNKS[chunk]
        return pltpu.make_async_copy(
            tensors[tensor].at[:, :, core, :, pl.ds(start, width)],
            sums[chunk],
            load_sem.at[chunk],
        )

    def store(chunk):
        tensor, start, width = REDUCE_CHUNKS[chunk]
        return pltpu.make_async_copy(
            from_far[chunk].at[0],
            outs[tensor].at[:, pl.ds(start, width)],
            store_sem.at[chunk],
        )

    def add(one, other):
        return (one.astype(F32) + other.astype(F32)).astype(BF16)

    def after_core(chunk):
        load(chunk).wait()
        hop(chunk, HOP_CORE).wait_recv()
        total = sums[chunk]

        def plane(index, carry):
            row, column = index // 2, index % 2
            total[row, column] = add(total[row, column], from_core[chunk][row, column])
            return carry

        lax.fori_loop(0, 4, plane, 0)
        hop(chunk, HOP_X).start()
        hop(chunk, HOP_Y).start()

    def after_near(chunk):
        half = REDUCE_CHUNKS[chunk][2] // 2
        hop(chunk, HOP_X).wait_recv()
        hop(chunk, HOP_Y).wait_recv()
        total, near = sums[chunk], from_near[chunk]

        def plane(index, carry):
            total[index, x, :, :half] = add(total[index, x, :, :half], near[0, index])
            total[y, index, :, half:] = add(total[y, index, :, half:], near[1, index])
            return carry

        lax.fori_loop(0, 2, plane, 0)
        hop(chunk, HOP_XY).start()
        hop(chunk, HOP_YX).start()

    def after_cross(chunk):
        half = REDUCE_CHUNKS[chunk][2] // 2
        hop(chunk, HOP_XY).wait_recv()
        hop(chunk, HOP_YX).wait_recv()
        total, cross = sums[chunk], from_cross[chunk]
        total[y, x, :, :half] = add(total[y, x, :, :half], cross[0])
        total[y, x, :, half:] = add(total[y, x, :, half:], cross[1])

        @pl.when(jnp.logical_not(is_middle))
        def _():
            hop(chunk, HOP_IN).start()

    def after_in(chunk):
        @pl.when(is_middle)
        def _():
            hop(chunk, HOP_IN).wait_recv()
            total = sums[chunk]
            total[y, x] = add(total[y, x], from_far[chunk][0])
            hop(chunk, HOP_MID).start()

    def after_middle(chunk):
        @pl.when(is_middle)
        def _():
            hop(chunk, HOP_MID).wait_recv()
            far = from_far[chunk]
            far[0] = add(sums[chunk][y, x], far[1])
            hop(chunk, HOP_OUT).start()
            store(chunk).start()

    for chunk in range(chunks):
        load(chunk).start()
        hop(chunk, HOP_CORE).start()
    stages = (after_core, after_near, after_cross, after_in, after_middle)
    for step in range(chunks + len(stages) - 1):
        for late, stage in enumerate(stages):
            if 0 <= step - late < chunks:
                stage(step - late)
    for chunk in range(chunks):
        for which in (HOP_CORE, HOP_X, HOP_Y, HOP_XY, HOP_YX):
            hop(chunk, which).wait_send()

    @pl.when(is_middle)
    def _():
        for chunk in range(chunks):
            hop(chunk, HOP_MID).wait_send()
            hop(chunk, HOP_OUT).wait_send()
            store(chunk).wait()

    @pl.when(jnp.logical_not(is_middle))
    def _():
        for chunk in range(chunks):
            hop(chunk, HOP_IN).wait_send()
            hop(chunk, HOP_OUT).wait_recv()


def reduce_all(parts):
    split = [part.reshape(2, 2, 2, -1, part.shape[1]) for part in parts]
    shapes = [(v.shape[3], width) for v, width in ((split[t], w) for t, _, w in REDUCE_CHUNKS)]
    anywhere = pl.BlockSpec(memory_space=pl.ANY)
    chunks = len(REDUCE_CHUNKS)
    moved = sum(v.size for v in split)
    return pl.pallas_call(
        reduce_kernel,
        in_specs=[anywhere] * 4,
        out_specs=[anywhere] * 4,
        out_shape=[jax.ShapeDtypeStruct(v.shape[3:], BF16) for v in split],
        scratch_shapes=[
            *[pltpu.VMEM((2, 2, r, w), BF16) for r, w in shapes],
            *[pltpu.VMEM((2, 2, r, w), BF16) for r, w in shapes],
            *[pltpu.VMEM((2, 2, r, w // 2), BF16) for r, w in shapes],
            *[pltpu.VMEM((2, r, w // 2), BF16) for r, w in shapes],
            *[pltpu.VMEM((2, r, w), BF16) for r, w in shapes],
            pltpu.SemaphoreType.DMA((chunks,)),
            pltpu.SemaphoreType.DMA((chunks, 8)),
            pltpu.SemaphoreType.DMA((chunks, 8)),
            pltpu.SemaphoreType.DMA((chunks,)),
        ],
        compiler_params=pltpu.CompilerParams(
            vmem_limit_bytes=60 * MIB, collective_id=1, has_side_effects=True
        ),
        cost_estimate=cost(2 * moved, 40 * moved),
    )(*split)


def weave(weight):
    rows = weight.shape[0]
    gap = jnp.zeros((rows, FF_PAD - FF), weight.dtype)
    parts = [jnp.concatenate([weight[:, i * FF : (i + 1) * FF], gap], 1) for i in range(2)]
    tiles = [
        parts[half][:, step * FF_TILE : (step + 1) * FF_TILE]
        for step in range(FF_STEPS)
        for half in range(2)
    ]
    return jnp.concatenate(tiles, axis=1)


def unweave(woven):
    tiles = [
        woven[:, (2 * step + half) * FF_TILE :][:, : min(FF_TILE, FF - step * FF_TILE)]
        for half in range(2)
        for step in range(FF_STEPS)
    ]
    return jnp.concatenate(tiles, axis=1)


def plan(seq_lengths, device, devices, micros):
    pair_cap = CAP // devices
    slots = devices * CHUNK_ROWS
    slot = jnp.arange(slots, dtype=jnp.int32)
    peer, inner = slot // CHUNK_ROWS, slot % CHUNK_ROWS
    rank, part = inner % pair_cap, inner // pair_cap
    micro = jnp.arange(MICRO, dtype=jnp.int32)
    mine = (micro % micros)[:, None] == part[None, :]
    seq = jnp.arange(seq_lengths.shape[1], dtype=jnp.int32)
    ahead = seq[None, :] < SEQ_DEV * peer[:, None]
    peer_start = jnp.sum(
        jnp.where(ahead[None], seq_lengths[:, None, :], 0), axis=2, dtype=jnp.int32
    )
    want = jnp.where(
        mine, (peer_start - device + devices - 1) // devices + rank[None, :], -1
    )
    own_seq = device * SEQ_DEV + jnp.arange(SEQ_DEV, dtype=jnp.int32)
    starts = jnp.sum(
        jnp.where(seq[None, None, :] < own_seq[None, :, None], seq_lengths[:, None, :], 0),
        axis=2,
        dtype=jnp.int32,
    )
    lengths = jnp.sum(
        jnp.where(seq[None, None, :] == own_seq[None, :, None], seq_lengths[:, None, :], 0),
        axis=2,
        dtype=jnp.int32,
    )
    first = (starts[:, :1] - peer[None, :] + devices - 1) // devices
    given = jnp.where(mine, (first + rank[None, :]) * devices + peer[None, :], -2)
    return want[:, None, :], starts, lengths, given[:, None, :]


def body(tokens, cotangent, seq_lengths, w_qkv, w_out, w_in, w_down, attn_gain, mlp_gain):
    group_size = lax.axis_size("grp")
    devices = lax.axis_size("rep") * group_size
    device = lax.axis_index("rep") * group_size + lax.axis_index("grp")
    micros = min(MICRO, max(1, CHUNK_ROWS * devices // CAP))
    both = ("rep", "grp")

    def swap(rows):
        return lax.all_to_all(rows, both, split_axis=0, concat_axis=0, tiled=True)

    def gather(rows):
        return lax.all_gather(rows, "grp", axis=0, tiled=True)

    near = group_size == SHARDS and devices == REPLICAS * SHARDS
    want, starts, lengths, given = plan(seq_lengths, device, devices, micros)
    token_rows = swap(pack_rows(tokens[:, :, 0], want, devices, micros))
    top_rows = swap(pack_rows(cotangent[:, :, 0], want, devices, micros))
    gains = lax.all_gather(jnp.stack([attn_gain, mlp_gain]), "grp", axis=1, tiled=True)
    gain_one = gains[:1].astype(F32)
    gain_two = gains[1:].astype(F32)
    full_qkv = gather(w_qkv)
    full_out = gather(w_out)
    full_in = gather(weave(w_in))
    full_down = gather(w_down)

    cosine, sine = rotary_tables(QKV_TILE)
    hidden, act_a = unpack_rows(
        token_rows, starts, lengths, given, gain_one, devices, micros, True
    )
    (top,) = unpack_rows(
        top_rows, starts, lengths, given, gain_one, devices, micros, False
    )
    qkv = qkv_rows(act_a, full_qkv, cosine, sine)
    attn_o, prob = attend(qkv, lengths)
    middle, act_b = middle_rows(attn_o, hidden, full_out, gain_two)
    layer_rows, grad_b, grad_in_w, grad_down_w = ffn(
        act_b, top, middle, full_in, full_down
    )
    layer_back = swap(repack_rows(layer_rows, starts, lengths, given, devices, micros))


    grad_mid, grad_o, grad_out_w, grad_gain_two = branch_back(
        grad_b, middle, top, attn_o, full_out, gain_two
    )
    grad_qkv_rows = attend_back(qkv, grad_o, prob, cosine[:, :LANES], sine[:, :LANES])
    grad_qkv_w = qkv_grad(act_a, grad_qkv_rows)
    grad_rows, grad_gain_one = input_back(
        grad_qkv_rows, full_qkv, hidden, grad_mid, gain_one
    )
    grad_back = swap(repack_rows(grad_rows, starts, lengths, given, devices, micros))
    parts = (grad_down_w, grad_in_w, grad_out_w, grad_qkv_w)
    if near:
        owned = reduce_all(parts)
    else:
        owned = [
            lax.psum(lax.psum_scatter(v, "grp", scatter_dimension=0, tiled=True), "rep")
            for v in parts
        ]
    grad_down, grad_in, grad_out, grad_qkv = (v.astype(F32) for v in owned)
    gain_parts = jnp.concatenate([grad_gain_one, grad_gain_two], axis=0)
    gain_parts = gain_parts.reshape(2, 1, group_size, -1)
    gain_parts = jnp.broadcast_to(
        gain_parts, (2, devices // group_size, *gain_parts.shape[2:])
    ).reshape(2, devices, -1)
    gain_sums = jnp.sum(
        lax.all_to_all(gain_parts, both, split_axis=1, concat_axis=1, tiled=True), axis=1
    )
    layer_out = spread_rows(layer_back, want, devices, micros)[:, :, None, :]
    grad_tokens = spread_rows(grad_back, want, devices, micros)[:, :, None, :]
    return (
        layer_out,
        grad_tokens,
        gain_sums[0],
        gain_sums[1],
        grad_qkv,
        grad_out,
        unweave(grad_in),
        grad_down,
    )


def solution(mesh):
    return jax.shard_map(
        body,
        mesh=mesh,
        in_specs=(
            P(None, None, ("rep", "grp"), None),
            P(None, None, ("rep", "grp"), None),
            P(),
            P("grp", None),
            P("grp", None),
            P("grp", None),
            P("grp", None),
            P("grp"),
            P("grp"),
        ),
        out_specs=(
            P(None, None, ("rep", "grp"), None),
            P(None, None, ("rep", "grp"), None),
            P("grp"),
            P("grp"),
            P("grp", None),
            P("grp", None),
            P("grp", None),
            P("grp", None),
        ),
        check_vma=False,
    )
```

```python
import functools
import math

import jax
import jax.numpy as jnp
import numpy as np
from jax import lax
from jax.experimental import pallas as pl
from jax.experimental.pallas import tpu as pltpu
from jax.sharding import PartitionSpec as P

D = 1024
HEADS = 16
HD = 64
FF = 2624
BLK = 128
MICRO = 4
SEQ_DEV = 2
CAP = 256
TOK_DEV = 192
ROWS = MICRO * CAP
BLOCKS = ROWS // BLK
PAIRS = HEADS // 2
LANES = 2 * HD

EPS = 1e-05
THETA = 160000.0
NEG = -1e30
ROOT_HALF = math.sqrt(0.5)
INV_ROOT_TWO_PI = 1.0 / math.sqrt(2.0 * math.pi)
SCALE = HD**-0.5

FF_TILE = 384
FF_STEPS = -(-FF // FF_TILE)
FF_PAD = FF_STEPS * FF_TILE
ROW_CHUNK = 256
CHUNK_ROWS = 16
SHARDS = 8
REPLICAS = 4
GAIN_ROWS = 8

F32 = jnp.float32
BF16 = jnp.bfloat16
MIB = 1 << 20


def dot(left, right, left_dim=1, right_dim=0):
    return lax.dot_general(
        left, right, (((left_dim,), (right_dim,)), ((), ())), preferred_element_type=F32
    )


def params(mib, steps=1):
    return pltpu.CompilerParams(
        vmem_limit_bytes=mib * MIB, dimension_semantics=("arbitrary",) * steps
    )


def cost(flops, moved, transcendentals=0):
    return pl.CostEstimate(
        flops=flops, bytes_accessed=moved, transcendentals=transcendentals
    )


def normed(values):
    center = values - jnp.mean(values, axis=-1, keepdims=True)
    inverse = lax.rsqrt(jnp.mean(center * center, axis=-1, keepdims=True) + EPS)
    return center * inverse, inverse


def norm_back(grad, normal, inverse):
    centred = grad - jnp.mean(grad, axis=-1, keepdims=True)
    return inverse * (centred - normal * jnp.mean(grad * normal, axis=-1, keepdims=True))


def rotary_tables():
    half = HD // 2
    frequency = np.float32(THETA) ** (-2.0 * np.arange(half, dtype=np.float32) / HD)
    angles = np.arange(BLK, dtype=np.float32)[:, None] * frequency.astype(np.float32)[None]
    cosine, sine = np.cos(angles), np.sin(angles)
    return (
        np.concatenate([cosine] * 4, axis=1).astype(np.float32),
        np.concatenate([-sine, sine] * 2, axis=1).astype(np.float32),
    )


def widen(table):
    return jnp.concatenate([table] * (QKV_TILE // LANES), axis=1)


def turned(values):
    axis = values.ndim - 1
    half = HD // 2
    width = values.shape[axis]
    lane = lax.broadcasted_iota(jnp.int32, values.shape, axis) % HD
    return jnp.where(
        lane < half,
        pltpu.roll(values, width - half, axis),
        pltpu.roll(values, half, axis),
    )


def position(devices):
    return lax.axis_index("rep") * (devices // lax.axis_size("rep")) + lax.axis_index("grp")


def length_sums(lengths_ref, chosen):
    return dot(
        lengths_ref[...].astype(F32).astype(BF16), chosen.astype(F32).astype(BF16)
    )


def slot_grid(sequences, devices):
    shape = (sequences, devices * CHUNK_ROWS)
    sequence = lax.broadcasted_iota(jnp.int32, shape, 0)
    slot = lax.broadcasted_iota(jnp.int32, shape, 1)
    inner = slot % CHUNK_ROWS
    pair_cap = CAP // devices
    return sequence, slot // CHUNK_ROWS, inner % pair_cap, inner // pair_cap


def ceil_div(value, count):
    return jnp.floor((value + (count - 0.5)) * (1.0 / count))


def sent_rows(lengths_ref, group, micros, devices):
    sequence, peer, rank, part = slot_grid(lengths_ref.shape[1], devices)
    starts = length_sums(lengths_ref, sequence < SEQ_DEV * peer)
    device = position(devices).astype(F32)
    wanted = ceil_div(starts - device, devices) + rank[:1].astype(F32)
    return pick_micros(wanted, part, group, micros, -1.0)


def pick_micros(values, part, group, micros, other):
    micro = lax.broadcasted_iota(jnp.int32, values.shape, 0)
    rows = []
    for step in range(micros):
        chosen = jnp.where(micro == group * micros + step, values, 0.0)
        row = jnp.sum(chosen, axis=0, keepdims=True)
        rows.append(jnp.where(part[:1] == step, row, other))
    return rows


def held_rows(lengths_ref, group, micros, devices):
    sequence, peer, rank, part = slot_grid(lengths_ref.shape[1], devices)
    device = position(devices)
    first = length_sums(lengths_ref, sequence < SEQ_DEV * device)
    source = peer[:1].astype(F32)
    given = (ceil_div(first - source, devices) + rank[:1].astype(F32)) * devices + source
    parts = [[None] * (CAP // BLK) for _ in range(micros)]
    for block in range(CAP // BLK):
        own = SEQ_DEV * device + block
        start = length_sums(lengths_ref, sequence < own)
        length = length_sums(lengths_ref, sequence == own)
        offsets = pick_micros(given - start, part, group, micros, -1.0)
        limits = pick_micros(length, part, group, micros, 0.0)
        for step in range(micros):
            place = lax.broadcasted_iota(jnp.int32, (BLK, part.shape[1]), 0).astype(F32)
            hit = (place == offsets[step]) & (place < limits[step])
            parts[step][block] = hit.astype(F32).astype(BF16)
    return jnp.concatenate([v for blocks in parts for v in blocks], axis=0)


def row_match(row):
    mine = lax.broadcasted_iota(jnp.int32, (TOK_DEV, row.shape[1]), 0).astype(F32)
    return (mine == row).astype(F32).astype(BF16)


def pack_kernel(micros, devices, lengths_ref, *refs):
    rows = sent_rows(lengths_ref, pl.program_id(0), micros, devices)
    picks = [row_match(row) for row in rows]
    count = len(refs) // 2
    for rows_ref, out_ref in zip(refs[:count], refs[count:]):
        total = None
        for step in range(micros):
            term = dot(picks[step], rows_ref[step], 0, 0)
            total = term if total is None else total + term
        out_ref[...] = total.astype(BF16).reshape(out_ref.shape)


def pack_rows(lengths, tables, devices, micros):
    groups = MICRO // micros
    slots = devices * CHUNK_ROWS
    count = len(tables)
    return pl.pallas_call(
        functools.partial(pack_kernel, micros, devices),
        grid=(groups,),
        in_specs=[
            pl.BlockSpec(lengths.shape, lambda g: (0, 0)),
            *[pl.BlockSpec((micros, TOK_DEV, D), lambda g: (g, 0, 0))] * count,
        ],
        out_specs=[
            pl.BlockSpec((devices, 1, CHUNK_ROWS, D), lambda g: (0, g, 0, 0))
        ]
        * count,
        out_shape=[jax.ShapeDtypeStruct((devices, groups, CHUNK_ROWS, D), BF16)] * count,
        compiler_params=params(48),
        cost_estimate=cost(
            2 * count * MICRO * TOK_DEV * slots * D, 4 * count * groups * slots * D
        ),
    )(lengths, *tables)


def spread_kernel(micros, devices, lengths_ref, back_ref, out_ref):
    arrived = back_ref[...].reshape(-1, D)
    rows = sent_rows(lengths_ref, pl.program_id(0), micros, devices)
    for step in range(micros):
        out_ref[step] = dot(row_match(rows[step]), arrived).astype(BF16)


def spread_rows(lengths, back, devices, micros):
    groups = MICRO // micros
    slots = devices * CHUNK_ROWS
    return pl.pallas_call(
        functools.partial(spread_kernel, micros, devices),
        grid=(groups,),
        in_specs=[
            pl.BlockSpec(lengths.shape, lambda g: (0, 0)),
            pl.BlockSpec((devices, 1, CHUNK_ROWS, D), lambda g: (0, g, 0, 0)),
        ],
        out_specs=pl.BlockSpec((micros, TOK_DEV, D), lambda g: (g, 0, 0)),
        out_shape=jax.ShapeDtypeStruct((MICRO, TOK_DEV, D), BF16),
        compiler_params=params(40),
        cost_estimate=cost(2 * MICRO * TOK_DEV * slots * D, 4 * groups * slots * D),
    )(lengths, back)


def unpack_kernel(
    micros, devices, lengths_ref, token_ref, top_ref, gain_ref, hidden_ref, act_ref, grad_ref
):
    pick = held_rows(lengths_ref, pl.program_id(0), micros, devices)
    rows = dot(pick, token_ref[...].reshape(-1, D))
    hidden_ref[...] = rows.astype(BF16)
    act_ref[...] = (normed(rows)[0] * gain_ref[...]).astype(BF16)
    grad_ref[...] = dot(pick, top_ref[...].reshape(-1, D)).astype(BF16)


def unpack_rows(lengths, tokens, top, gain, devices, micros):
    groups = MICRO // micros
    slots = devices * CHUNK_ROWS
    chunk = pl.BlockSpec((devices, 1, CHUNK_ROWS, D), lambda g: (0, g, 0, 0))
    return pl.pallas_call(
        functools.partial(unpack_kernel, micros, devices),
        grid=(groups,),
        in_specs=[
            pl.BlockSpec(lengths.shape, lambda g: (0, 0)),
            chunk,
            chunk,
            pl.BlockSpec((1, D), lambda g: (0, 0)),
        ],
        out_specs=[pl.BlockSpec((micros * CAP, D), lambda g: (g, 0))] * 3,
        out_shape=[jax.ShapeDtypeStruct((ROWS, D), BF16)] * 3,
        compiler_params=params(48),
        cost_estimate=cost(4 * ROWS * slots * D, 8 * groups * slots * D),
    )(lengths, tokens, top, gain)


def repack_kernel(micros, devices, lengths_ref, rows_ref, out_ref):
    pick = held_rows(lengths_ref, pl.program_id(0), micros, devices)
    out_ref[...] = dot(pick, rows_ref[...], 0, 0).astype(BF16).reshape(out_ref.shape)


def repack_rows(lengths, rows, devices, micros):
    groups = MICRO // micros
    slots = devices * CHUNK_ROWS
    return pl.pallas_call(
        functools.partial(repack_kernel, micros, devices),
        grid=(groups,),
        in_specs=[
            pl.BlockSpec(lengths.shape, lambda g: (0, 0)),
            pl.BlockSpec((micros * CAP, D), lambda g: (g, 0)),
        ],
        out_specs=pl.BlockSpec((devices, 1, CHUNK_ROWS, D), lambda g: (0, g, 0, 0)),
        out_shape=jax.ShapeDtypeStruct((devices, groups, CHUNK_ROWS, D), BF16),
        compiler_params=params(40),
        cost_estimate=cost(2 * ROWS * slots * D, 4 * groups * slots * D),
    )(lengths, rows)


QKV_TILE = 512


def qkv_kernel(act_ref, weight_ref, cos_ref, sin_ref, out_ref):
    packed = dot(act_ref[...], weight_ref[...])
    is_value = pl.program_id(0) >= 2 * D // QKV_TILE

    @pl.when(is_value)
    def _():
        out_ref[...] = packed.astype(BF16)

    @pl.when(jnp.logical_not(is_value))
    def _():
        split = packed.reshape(BLOCKS, BLK, QKV_TILE)
        spun = split * widen(cos_ref[...])[None] + turned(split) * widen(sin_ref[...])[None]
        out_ref[...] = spun.reshape(ROWS, QKV_TILE).astype(BF16)


def qkv_rows(act, weight, cosine, sine):
    return pl.pallas_call(
        qkv_kernel,
        grid=(3 * D // QKV_TILE,),
        in_specs=[
            pl.BlockSpec((ROWS, D), lambda j: (0, 0)),
            pl.BlockSpec((D, QKV_TILE), lambda j: (0, j)),
            pl.BlockSpec((BLK, LANES), lambda j: (0, 0)),
            pl.BlockSpec((BLK, LANES), lambda j: (0, 0)),
        ],
        out_specs=pl.BlockSpec((ROWS, QKV_TILE), lambda j: (0, j)),
        out_shape=jax.ShapeDtypeStruct((ROWS, 3 * D), BF16),
        compiler_params=params(40),
        cost_estimate=cost(2 * ROWS * D * 3 * D, 2 * (3 * D * D + ROWS * 4 * D)),
    )(act, weight, cosine, sine)


def head_masks(dtype):
    lane = lax.broadcasted_iota(jnp.int32, (BLK, LANES), 1)
    low = (lane < HD).astype(F32).astype(dtype)
    high = (lane >= HD).astype(F32).astype(dtype)
    return low, high


def attend_kernel(devices, length_ref, q_ref, k_ref, v_ref, out_ref, prob_ref):
    block = pl.program_id(0)
    low, high = head_masks(BF16)
    shape = (length_ref.shape[1], BLK)
    own = lax.broadcasted_iota(jnp.int32, shape, 0) == (
        SEQ_DEV * position(devices) + block % SEQ_DEV
    )
    lengths = length_sums(length_ref, own)
    micro = lax.broadcasted_iota(jnp.int32, lengths.shape, 0) == block // SEQ_DEV
    length = jnp.sum(jnp.where(micro, lengths, 0.0), axis=0, keepdims=True)
    valid = lax.broadcasted_iota(jnp.int32, (BLK, BLK), 1).astype(F32) < length
    for pair in range(PAIRS):
        lanes = slice(pair * LANES, (pair + 1) * LANES)
        query, key, value = q_ref[:, lanes], k_ref[:, lanes], v_ref[:, lanes]
        scores = dot(query, jnp.concatenate([key * low, key * high], axis=0), 1, 1)
        parts = []
        for head in range(2):
            score = scores[:, head * BLK : (head + 1) * BLK] * SCALE
            score = jnp.where(valid, score, NEG)
            expo = jnp.exp(score - jnp.max(score, axis=-1, keepdims=True))
            parts.append(expo / jnp.sum(expo, axis=-1, keepdims=True))
        prob = jnp.concatenate(parts, axis=1).astype(BF16)
        prob_ref[0, pair] = prob
        both = jnp.concatenate([value * low, value * high], axis=0)
        out_ref[:, lanes] = dot(prob, both).astype(BF16)


def attend(qkv, lengths, devices):
    return pl.pallas_call(
        functools.partial(attend_kernel, devices),
        grid=(BLOCKS,),
        in_specs=[
            pl.BlockSpec(lengths.shape, lambda b: (0, 0)),
            pl.BlockSpec((BLK, D), lambda b: (b, 0)),
            pl.BlockSpec((BLK, D), lambda b: (b, 1)),
            pl.BlockSpec((BLK, D), lambda b: (b, 2)),
        ],
        out_specs=[
            pl.BlockSpec((BLK, D), lambda b: (b, 0)),
            pl.BlockSpec((1, PAIRS, BLK, 2 * BLK), lambda b: (b, 0, 0, 0)),
        ],
        out_shape=[
            jax.ShapeDtypeStruct((ROWS, D), BF16),
            jax.ShapeDtypeStruct((BLOCKS, PAIRS, BLK, 2 * BLK), BF16),
        ],
        compiler_params=params(32),
        cost_estimate=cost(8 * ROWS * BLK * D, 2 * ROWS * 6 * D, ROWS * HEADS * BLK),
    )(lengths, qkv, qkv, qkv)


def attend_back_kernel(
    q_ref, k_ref, v_ref, grad_ref, prob_ref, cos_ref, sin_ref, out_ref
):
    low, high = head_masks(BF16)
    lane = lax.broadcasted_iota(jnp.int32, (BLK, LANES), 1)
    is_low = lane < HD
    cosine, sine = cos_ref[...], sin_ref[...]
    for pair in range(PAIRS):
        lanes = slice(pair * LANES, (pair + 1) * LANES)
        query, key, value = q_ref[:, lanes], k_ref[:, lanes], v_ref[:, lanes]
        grad, prob = grad_ref[:, lanes], prob_ref[0, pair]
        grad_v = dot(prob, grad, 0, 0)
        grad_v = jnp.where(is_low, grad_v[:BLK], grad_v[BLK:])
        grad_p = dot(grad, jnp.concatenate([value * low, value * high], axis=0), 1, 1)
        parts = []
        for head in range(2):
            keys = slice(head * BLK, (head + 1) * BLK)
            weight, slope = prob[:, keys].astype(F32), grad_p[:, keys]
            inner = jnp.sum(weight * slope, axis=-1, keepdims=True)
            parts.append(weight * (slope - inner))
        grad_s = jnp.concatenate(parts, axis=1).astype(BF16)
        both = jnp.concatenate([key * low, key * high], axis=0)
        grad_q = dot(grad_s, both) * SCALE
        grad_k = dot(grad_s, query, 0, 0)
        grad_k = jnp.where(is_low, grad_k[:BLK], grad_k[BLK:]) * SCALE
        start = pair * LANES
        out_ref[:, start : start + LANES] = (
            grad_q * cosine - turned(grad_q) * sine
        ).astype(BF16)
        out_ref[:, D + start : D + start + LANES] = (
            grad_k * cosine - turned(grad_k) * sine
        ).astype(BF16)
        out_ref[:, 2 * D + start : 2 * D + start + LANES] = grad_v.astype(BF16)


def attend_back(qkv, grad_o, prob, cosine, sine):
    return pl.pallas_call(
        attend_back_kernel,
        grid=(BLOCKS,),
        in_specs=[
            pl.BlockSpec((BLK, D), lambda b: (b, 0)),
            pl.BlockSpec((BLK, D), lambda b: (b, 1)),
            pl.BlockSpec((BLK, D), lambda b: (b, 2)),
            pl.BlockSpec((BLK, D), lambda b: (b, 0)),
            pl.BlockSpec((1, PAIRS, BLK, 2 * BLK), lambda b: (b, 0, 0, 0)),
            pl.BlockSpec((BLK, LANES), lambda b: (0, 0)),
            pl.BlockSpec((BLK, LANES), lambda b: (0, 0)),
        ],
        out_specs=pl.BlockSpec((BLK, 3 * D), lambda b: (b, 0)),
        out_shape=jax.ShapeDtypeStruct((ROWS, 3 * D), BF16),
        compiler_params=params(32),
        cost_estimate=cost(20 * ROWS * BLK * D, 2 * ROWS * 9 * D),
    )(qkv, qkv, qkv, grad_o, prob, cosine, sine)


def middle_kernel(attn_ref, hidden_ref, weight_ref, gain_ref, mid_ref, act_ref):
    middle = hidden_ref[...].astype(F32) + dot(attn_ref[...], weight_ref[...])
    mid_ref[...] = middle
    act_ref[...] = (normed(middle)[0] * gain_ref[...]).astype(BF16)


def middle_rows(attn_o, hidden, weight, gain):
    tile = pl.BlockSpec((ROW_CHUNK, D), lambda i: (i, 0))
    return pl.pallas_call(
        middle_kernel,
        grid=(ROWS // ROW_CHUNK,),
        in_specs=[
            tile,
            tile,
            pl.BlockSpec((D, D), lambda i: (0, 0)),
            pl.BlockSpec((1, D), lambda i: (0, 0)),
        ],
        out_specs=[tile, tile],
        out_shape=[
            jax.ShapeDtypeStruct((ROWS, D), F32),
            jax.ShapeDtypeStruct((ROWS, D), BF16),
        ],
        compiler_params=params(32),
        cost_estimate=cost(2 * ROWS * D * D, 2 * D * D + 10 * ROWS * D),
    )(attn_o, hidden, weight, gain)


def ffn_kernel(
    act_ref,
    top_ref,
    mid_ref,
    in_ref,
    down_ref,
    layer_ref,
    grad_b_ref,
    grad_in_ref,
    grad_down_ref,
    total,
    act_t,
    down_clean,
    kept_c,
    kept_gu,
):
    step = pl.program_id(0)

    @pl.when(step == 0)
    def _():
        total[...] = mid_ref[...]
        grad_b_ref[...] = jnp.zeros_like(grad_b_ref)
        act_t[...] = act_ref[...].T

    row = lax.broadcasted_iota(jnp.int32, (FF_TILE, D), 0) + step * FF_TILE
    down_clean[...] = jnp.where(row < FF, down_ref[...].astype(F32), 0.0).astype(BF16)

    def rows_step(index, carry):
        rows = pl.ds(pl.multiple_of(index * ROW_CHUNK, ROW_CHUNK), ROW_CHUNK)
        act, top = act_ref[rows, :], top_ref[rows, :]
        gate_up = dot(act, in_ref[...])
        gelu_in, linear = gate_up[:, :FF_TILE], gate_up[:, FF_TILE:]
        grad_c = dot(top, down_clean[...], 1, 1)
        phi = 0.5 * (1.0 + lax.erf(gelu_in * ROOT_HALF))
        gelu_out = gelu_in * phi
        slope = phi + gelu_in * (jnp.exp(-0.5 * gelu_in * gelu_in) * INV_ROOT_TWO_PI)
        act_c = (gelu_out * linear).astype(BF16)
        kept_c[rows, :] = act_c
        kept_gu[rows, :FF_TILE] = (grad_c * linear * slope).astype(BF16)
        kept_gu[rows, FF_TILE:] = (grad_c * gelu_out).astype(BF16)
        total[rows, :] += dot(act_c, down_clean[...])
        grad_b_ref[rows, :] += dot(kept_gu[rows, :], in_ref[...], 1, 1)
        return carry

    lax.fori_loop(0, ROWS // ROW_CHUNK, rows_step, 0)
    grad_in_ref[...] = dot(act_t[...], kept_gu[...]).astype(BF16)
    grad_down_ref[...] = dot(kept_c[...], top_ref[...], 0, 0).astype(BF16)

    @pl.when(step == FF_STEPS - 1)
    def _():
        layer_ref[...] = total[...].astype(BF16)


def ffn(act, top, middle, full_in, full_down):
    whole = pl.BlockSpec((ROWS, D), lambda j: (0, 0))
    tall = pl.BlockSpec((D, 2 * FF_TILE), lambda j: (0, j))
    wide = pl.BlockSpec((FF_TILE, D), lambda j: (j, 0))
    return pl.pallas_call(
        ffn_kernel,
        grid=(FF_STEPS,),
        in_specs=[
            whole,
            whole,
            whole,
            tall,
            wide,
        ],
        out_specs=[whole, whole, tall, wide],
        out_shape=[
            jax.ShapeDtypeStruct((ROWS, D), BF16),
            jax.ShapeDtypeStruct((ROWS, D), F32),
            jax.ShapeDtypeStruct((D, 2 * FF_PAD), BF16),
            jax.ShapeDtypeStruct((FF, D), BF16),
        ],
        scratch_shapes=[
            pltpu.VMEM((ROWS, D), F32),
            pltpu.VMEM((D, ROWS), BF16),
            pltpu.VMEM((FF_TILE, D), BF16),
            pltpu.VMEM((ROWS, FF_TILE), BF16),
            pltpu.VMEM((ROWS, 2 * FF_TILE), BF16),
        ],
        compiler_params=params(60),
        cost_estimate=cost(18 * ROWS * D * FF, 12 * D * FF, 2 * ROWS * FF),
    )(act, top, middle, full_in, full_down)


def branch_kernel(
    order_ref,
    grad_b_ref,
    mid_ref,
    top_ref,
    attn_ref,
    weight_ref,
    gain_ref,
    grad_mid_ref,
    grad_o_ref,
    grad_w_ref,
    grad_gain_ref,
    total,
):
    step = pl.program_id(0)

    @pl.when(step == 0)
    def _():
        total[...] = jnp.zeros_like(total)
        grad_gain_ref[...] = jnp.zeros_like(grad_gain_ref)

    grad_b = grad_b_ref[...]
    normal, inverse = normed(mid_ref[...])
    grad_gain_ref[...] += jnp.sum(grad_b * normal, axis=0, keepdims=True)
    grad_mid = top_ref[...].astype(F32) + norm_back(
        grad_b * gain_ref[...], normal, inverse
    )
    grad_mid_ref[...] = grad_mid
    grad_r = grad_mid.astype(BF16)
    grad_o_ref[...] = dot(grad_r, weight_ref[...], 1, 1).astype(BF16)
    total[...] += dot(attn_ref[...], grad_r, 0, 0)

    @pl.when(step == ROWS // ROW_CHUNK - 1)
    def _():
        grad_w_ref[...] = total[...].astype(BF16)


def branch_back(order, grad_b, middle, top, attn_o, weight, gain):
    tile = pl.BlockSpec((ROW_CHUNK, D), lambda i: (i, 0))
    square = pl.BlockSpec((D, D), lambda i: (0, 0))
    line = pl.BlockSpec((1, D), lambda i: (0, 0))
    return pl.pallas_call(
        branch_kernel,
        grid=(ROWS // ROW_CHUNK,),
        in_specs=[
            pl.BlockSpec(memory_space=pl.ANY),
            *[tile] * 4,
            square,
            line,
        ],
        out_specs=[tile, tile, square, line],
        out_shape=[
            jax.ShapeDtypeStruct((ROWS, D), F32),
            jax.ShapeDtypeStruct((ROWS, D), BF16),
            jax.ShapeDtypeStruct((D, D), BF16),
            jax.ShapeDtypeStruct((1, D), F32),
        ],
        scratch_shapes=[pltpu.VMEM((D, D), F32)],
        compiler_params=params(40),
        cost_estimate=cost(4 * ROWS * D * D, 4 * D * D + 18 * ROWS * D),
    )(order, grad_b, middle, top, attn_o, weight, gain)


def input_kernel(
    grad_qkv_ref,
    weight_ref,
    hidden_ref,
    grad_mid_ref,
    gain_ref,
    other_ref,
    out_ref,
    gains_ref,
    grad_gain,
):
    @pl.when(pl.program_id(0) == 0)
    def _():
        grad_gain[...] = jnp.zeros_like(grad_gain)

    grad_a = dot(grad_qkv_ref[...], weight_ref[...], 1, 1)
    normal, inverse = normed(hidden_ref[...].astype(F32))
    grad_gain[...] += jnp.sum(grad_a * normal, axis=0, keepdims=True)
    out_ref[...] = (
        grad_mid_ref[...] + norm_back(grad_a * gain_ref[...], normal, inverse)
    ).astype(BF16)

    @pl.when(pl.program_id(0) == ROWS // ROW_CHUNK - 1)
    def _():
        width = D // SHARDS
        for shard in range(SHARDS):
            lanes = slice(shard * width, (shard + 1) * width)
            for part, values in enumerate((grad_gain, other_ref)):
                gains_ref[shard, :, part * width : (part + 1) * width] = jnp.broadcast_to(
                    values[:, lanes], (GAIN_ROWS, width)
                )


def input_back(grad_qkv, weight, hidden, grad_mid, gain, other):
    tile = pl.BlockSpec((ROW_CHUNK, D), lambda i: (i, 0))
    line = pl.BlockSpec((1, D), lambda i: (0, 0))
    return pl.pallas_call(
        input_kernel,
        grid=(ROWS // ROW_CHUNK,),
        in_specs=[
            pl.BlockSpec((ROW_CHUNK, 3 * D), lambda i: (i, 0)),
            pl.BlockSpec((D, 3 * D), lambda i: (0, 0)),
            tile,
            tile,
            line,
            line,
        ],
        out_specs=[
            tile,
            pl.BlockSpec((SHARDS, GAIN_ROWS, 2 * D // SHARDS), lambda i: (0, 0, 0)),
        ],
        out_shape=[
            jax.ShapeDtypeStruct((ROWS, D), BF16),
            jax.ShapeDtypeStruct((SHARDS, GAIN_ROWS, 2 * D // SHARDS), F32),
        ],
        scratch_shapes=[pltpu.VMEM((1, D), F32)],
        compiler_params=params(40),
        cost_estimate=cost(6 * ROWS * D * D, 6 * D * D + 14 * ROWS * D),
    )(grad_qkv, weight, hidden, grad_mid, gain, other)


def qkv_grad_kernel(act_ref, grad_ref, out_ref, act_t):
    @pl.when(pl.program_id(0) == 0)
    def _():
        act_t[...] = act_ref[...].T

    out_ref[...] = dot(act_t[...], grad_ref[...]).astype(BF16)


def qkv_grad(act, grad_qkv):
    return pl.pallas_call(
        qkv_grad_kernel,
        grid=(3 * D // QKV_TILE,),
        in_specs=[
            pl.BlockSpec((ROWS, D), lambda j: (0, 0)),
            pl.BlockSpec((ROWS, QKV_TILE), lambda j: (0, j)),
        ],
        out_specs=pl.BlockSpec((D, QKV_TILE), lambda j: (0, j)),
        out_shape=jax.ShapeDtypeStruct((D, 3 * D), BF16),
        scratch_shapes=[pltpu.VMEM((D, ROWS), BF16)],
        compiler_params=params(32),
        cost_estimate=cost(6 * ROWS * D * D, 2 * (7 * D * D)),
    )(act, grad_qkv)


MESH = pl.DeviceIdType.MESH
REDUCE_CHUNKS = (
    (0, 0, 512),
    (0, 512, 512),
    (1, 0, 1792),
    (1, 1792, 1792),
    (1, 3584, 1792),
    (2, 0, 1024),
    (3, 0, 1536),
    (3, 1536, 1536),
    (4, 0, 256),
)
HOP_CORE, HOP_X, HOP_Y, HOP_XY, HOP_YX, HOP_IN, HOP_MID, HOP_OUT = range(8)


def place():
    rep, grp = lax.axis_index("rep"), lax.axis_index("grp")
    core, x, y = grp % 2, grp // 2 % 2, grp // 4
    return rep, grp, core, x, y, grp + 1 - 2 * core, grp + 2 - 4 * x, grp + 4 - 8 * y


def reduce_kernel(*refs):
    tensors, refs = refs[:5], refs[5:]
    outs, refs = refs[:5], refs[5:]
    chunks = len(REDUCE_CHUNKS)
    sums, from_core, from_near, from_cross, from_far = (
        refs[i * chunks : (i + 1) * chunks] for i in range(5)
    )
    load_sem, send_sem, recv_sem, store_sem = refs[5 * chunks :]
    rep, grp, core, x, y, by_core, by_x, by_y = place()
    is_middle = (rep == 1) | (rep == 2)
    inward, outward, across = 1 + rep // 2, 3 * (rep // 2), 3 - rep

    barrier = pltpu.get_barrier_semaphore()
    for near in (by_core, by_x, by_y):
        pl.semaphore_signal(barrier, device_id=(rep, near), device_id_type=MESH)

    @pl.when(is_middle)
    def _():
        pl.semaphore_signal(barrier, device_id=(across, grp), device_id_type=MESH)
        pl.semaphore_signal(barrier, device_id=(outward, grp), device_id_type=MESH)
        pl.semaphore_wait(barrier, 5)

    @pl.when(jnp.logical_not(is_middle))
    def _():
        pl.semaphore_signal(barrier, device_id=(inward, grp), device_id_type=MESH)
        pl.semaphore_wait(barrier, 4)

    def hop(chunk, which):
        tensor, start, width = REDUCE_CHUNKS[chunk]
        half = width // 2
        left, right, columns = pl.ds(0, half), pl.ds(half, half), pl.ds(start, width)
        total, far = sums[chunk], from_far[chunk]
        near, cross = from_near[chunk], from_cross[chunk]
        if which == HOP_CORE:
            source, target = tensors[tensor].at[:, :, 1 - core, :, columns], from_core[chunk]
        elif which == HOP_X:
            source, target = total.at[:, 1 - x, :, left], near.at[0]
        elif which == HOP_Y:
            source, target = total.at[1 - y, :, :, right], near.at[1]
        elif which == HOP_XY:
            source, target = total.at[1 - y, x, :, left], cross.at[0]
        elif which == HOP_YX:
            source, target = total.at[y, 1 - x, :, right], cross.at[1]
        elif which == HOP_IN:
            source, target = total.at[y, x], far.at[0]
        elif which == HOP_MID:
            source, target = total.at[y, x], far.at[1]
        else:
            source, target = far.at[0], outs[tensor].at[:, columns]
        to_rep = (rep, rep, rep, rep, rep, inward, across, outward)[which]
        to_grp = (by_core, by_x, by_y, by_y, by_x, grp, grp, grp)[which]
        return pltpu.make_async_remote_copy(
            src_ref=source,
            dst_ref=target,
            send_sem=send_sem.at[chunk, which],
            recv_sem=recv_sem.at[chunk, which],
            device_id=(to_rep, to_grp),
            device_id_type=MESH,
        )

    def load(chunk):
        tensor, start, width = REDUCE_CHUNKS[chunk]
        return pltpu.make_async_copy(
            tensors[tensor].at[:, :, core, :, pl.ds(start, width)],
            sums[chunk],
            load_sem.at[chunk],
        )

    def store(chunk):
        tensor, start, width = REDUCE_CHUNKS[chunk]
        return pltpu.make_async_copy(
            from_far[chunk].at[0],
            outs[tensor].at[:, pl.ds(start, width)],
            store_sem.at[chunk],
        )

    def add(one, other):
        return (one.astype(F32) + other.astype(F32)).astype(one.dtype)

    def after_core(chunk):
        load(chunk).wait()
        hop(chunk, HOP_CORE).wait_recv()
        total = sums[chunk]

        def plane(index, carry):
            row, column = index // 2, index % 2
            total[row, column] = add(total[row, column], from_core[chunk][row, column])
            return carry

        lax.fori_loop(0, 4, plane, 0)
        hop(chunk, HOP_X).start()
        hop(chunk, HOP_Y).start()

    def after_near(chunk):
        half = REDUCE_CHUNKS[chunk][2] // 2
        hop(chunk, HOP_X).wait_recv()
        hop(chunk, HOP_Y).wait_recv()
        total, near = sums[chunk], from_near[chunk]

        def plane(index, carry):
            total[index, x, :, :half] = add(total[index, x, :, :half], near[0, index])
            total[y, index, :, half:] = add(total[y, index, :, half:], near[1, index])
            return carry

        lax.fori_loop(0, 2, plane, 0)
        hop(chunk, HOP_XY).start()
        hop(chunk, HOP_YX).start()

    def after_cross(chunk):
        half = REDUCE_CHUNKS[chunk][2] // 2
        hop(chunk, HOP_XY).wait_recv()
        hop(chunk, HOP_YX).wait_recv()
        total, cross = sums[chunk], from_cross[chunk]
        total[y, x, :, :half] = add(total[y, x, :, :half], cross[0])
        total[y, x, :, half:] = add(total[y, x, :, half:], cross[1])

        @pl.when(jnp.logical_not(is_middle))
        def _():
            hop(chunk, HOP_IN).start()

    def after_in(chunk):
        @pl.when(is_middle)
        def _():
            hop(chunk, HOP_IN).wait_recv()
            total = sums[chunk]
            total[y, x] = add(total[y, x], from_far[chunk][0])
            hop(chunk, HOP_MID).start()

    def after_middle(chunk):
        @pl.when(is_middle)
        def _():
            hop(chunk, HOP_MID).wait_recv()
            far = from_far[chunk]
            far[0] = add(sums[chunk][y, x], far[1])
            hop(chunk, HOP_OUT).start()
            store(chunk).start()

    for chunk in range(chunks):
        load(chunk).start()
        hop(chunk, HOP_CORE).start()
    stages = (after_core, after_near, after_cross, after_in, after_middle)
    for step in range(chunks + len(stages) - 1):
        for late, stage in enumerate(stages):
            if 0 <= step - late < chunks:
                stage(step - late)
    for chunk in range(chunks):
        for which in (HOP_CORE, HOP_X, HOP_Y, HOP_XY, HOP_YX):
            hop(chunk, which).wait_send()

    @pl.when(is_middle)
    def _():
        for chunk in range(chunks):
            hop(chunk, HOP_MID).wait_send()
            hop(chunk, HOP_OUT).wait_send()
            store(chunk).wait()

    @pl.when(jnp.logical_not(is_middle))
    def _():
        for chunk in range(chunks):
            hop(chunk, HOP_IN).wait_send()
            hop(chunk, HOP_OUT).wait_recv()


def reduce_all(parts):
    split = [part.reshape(2, 2, 2, -1, part.shape[-1]) for part in parts]
    kinds = [(split[t].dtype, split[t].shape[3], width) for t, _, width in REDUCE_CHUNKS]
    anywhere = pl.BlockSpec(memory_space=pl.ANY)
    chunks = len(REDUCE_CHUNKS)
    moved = sum(v.size for v in split)
    return pl.pallas_call(
        reduce_kernel,
        in_specs=[anywhere] * len(parts),
        out_specs=[anywhere] * len(parts),
        out_shape=[jax.ShapeDtypeStruct(v.shape[3:], v.dtype) for v in split],
        scratch_shapes=[
            *[pltpu.VMEM((2, 2, r, w), t) for t, r, w in kinds],
            *[pltpu.VMEM((2, 2, r, w), t) for t, r, w in kinds],
            *[pltpu.VMEM((2, 2, r, w // 2), t) for t, r, w in kinds],
            *[pltpu.VMEM((2, r, w // 2), t) for t, r, w in kinds],
            *[pltpu.VMEM((2, r, w), t) for t, r, w in kinds],
            pltpu.SemaphoreType.DMA((chunks,)),
            pltpu.SemaphoreType.DMA((chunks, 8)),
            pltpu.SemaphoreType.DMA((chunks, 8)),
            pltpu.SemaphoreType.DMA((chunks,)),
        ],
        compiler_params=pltpu.CompilerParams(
            vmem_limit_bytes=60 * MIB, collective_id=1, has_side_effects=True
        ),
        cost_estimate=cost(2 * moved, 40 * moved),
    )(*split)


WAY_X, WAY_Y, WAY_CORE, WAY_CORE_X, WAY_CORE_Y = range(5)
WAY_XY, WAY_YX, WAY_CORE_XY, WAY_CORE_YX = range(5, 9)


def gather_kernel(devices, *refs):
    shards, refs = refs[:4], refs[4:]
    gain, sends, refs = refs[0], refs[1:3], refs[3:]
    fulls, refs = refs[:4], refs[4:]
    gains, lands, refs = refs[0], refs[1:3], refs[3:]
    local_sem, way_send, way_recv, gain_send, gain_recv, row_send, row_recv = refs
    rep, grp, core, x, y, by_core, by_x, by_y = place()
    by_xy = by_x + by_y - grp
    other = by_core - grp
    device = rep * SHARDS + grp

    def peer(step):
        return lax.rem(device + step, devices)

    def mesh_id(index):
        return (index // SHARDS, lax.rem(index, SHARDS))

    barrier = pltpu.get_barrier_semaphore()

    def greet(step, carry):
        pl.semaphore_signal(barrier, device_id=mesh_id(peer(step)), device_id_type=MESH)
        return carry

    lax.fori_loop(1, devices, greet, 0)
    pl.semaphore_wait(barrier, devices - 1)

    def way(which, tensor):
        full, width = fulls[tensor], shards[tensor].shape[1]
        left, right = pl.ds(0, width // 2), pl.ds(width // 2, width // 2)
        own = shards[tensor]
        source, slot, landing, part, to = {
            WAY_X: (own, grp, by_x, None, by_x),
            WAY_Y: (own, grp, by_y, None, by_y),
            WAY_CORE: (own, grp, by_core, None, by_core),
            WAY_CORE_X: (None, by_x, by_x + other, None, by_core),
            WAY_CORE_Y: (None, by_y, by_y + other, None, by_core),
            WAY_XY: (None, by_x, by_xy, left, by_y),
            WAY_YX: (None, by_y, by_xy, right, by_x),
            WAY_CORE_XY: (None, by_xy, by_xy + other, left, by_core),
            WAY_CORE_YX: (None, by_xy, by_xy + other, right, by_core),
        }[which]

        def view(index):
            return full.at[index] if part is None else full.at[index, :, part]

        def copy(source, target):
            return pltpu.make_async_remote_copy(
                src_ref=source,
                dst_ref=target,
                send_sem=way_send.at[tensor, which],
                recv_sem=way_recv.at[tensor, which],
                device_id=(rep, to),
                device_id_type=MESH,
            )

        def start():
            copy(view(slot) if source is None else source, view(slot)).start()

        def arrive():
            copy(view(landing), view(landing)).wait_recv()

        def sent():
            copy(view(slot) if source is None else source, view(slot)).wait_send()

        return start, arrive, sent

    def start(tensor, *ways):
        for which in ways:
            way(which, tensor)[0]()

    def arrive(tensor, *ways):
        for which in ways:
            way(which, tensor)[1]()

    def gain_copy(step, slot):
        to = lax.rem(grp + step, SHARDS)
        return pltpu.make_async_remote_copy(
            src_ref=gain,
            dst_ref=gains.at[slot],
            send_sem=gain_send.at[step],
            recv_sem=gain_recv.at[step],
            device_id=(rep, to),
            device_id_type=MESH,
        )

    def row_copy(which, step, source, slot, to):
        return pltpu.make_async_remote_copy(
            src_ref=sends[which].at[source],
            dst_ref=lands[which].at[slot],
            send_sem=row_send.at[which, step],
            recv_sem=row_recv.at[which, step],
            device_id=mesh_id(to),
            device_id_type=MESH,
        )

    def send_rows(which):
        def one(step, carry):
            row_copy(which, step, peer(step), device, peer(step)).start()
            return carry

        lax.fori_loop(1, devices, one, 0)

    def land_rows(which):
        def one(step, carry):
            source = lax.rem(device + devices - step, devices)
            row_copy(which, step, peer(step), source, peer(step)).wait_recv()
            row_copy(which, step, peer(step), device, peer(step)).wait_send()
            return carry

        lax.fori_loop(1, devices, one, 0)

    def local(index, source, target):
        return pltpu.make_async_copy(source, target, local_sem.at[index])

    keeps = [local(i, shards[i], fulls[i].at[grp]) for i in range(4)]
    keeps.append(local(4, gain, gains.at[grp]))
    keeps += [local(5 + i, sends[i].at[device], lands[i].at[device]) for i in range(2)]

    for step in range(1, SHARDS):
        gain_copy(step, grp).start()
    start(3, WAY_X, WAY_Y, WAY_CORE)
    send_rows(0)
    for tensor in (2, 1, 0):
        start(tensor, WAY_X, WAY_Y, WAY_CORE)
    send_rows(1)
    for keep in keeps:
        keep.start()
    order = (3, 2, 1, 0)
    for late in range(len(order) + 1):
        if late < len(order):
            tensor = order[late]
            arrive(tensor, WAY_X)
            start(tensor, WAY_XY, WAY_CORE_X)
            arrive(tensor, WAY_Y)
            start(tensor, WAY_YX, WAY_CORE_Y)
        if late:
            tensor = order[late - 1]
            arrive(tensor, WAY_XY)
            start(tensor, WAY_CORE_XY)
            arrive(tensor, WAY_YX)
            start(tensor, WAY_CORE_YX)
    for tensor in order:
        arrive(tensor, WAY_CORE, WAY_CORE_X, WAY_CORE_Y, WAY_CORE_XY, WAY_CORE_YX)
    for step in range(1, SHARDS):
        gain_copy(step, lax.rem(grp + SHARDS - step, SHARDS)).wait_recv()
        gain_copy(step, grp).wait_send()
    for which in range(2):
        land_rows(which)
    for tensor in order:
        for which in range(9):
            way(which, tensor)[2]()
    for keep in keeps:
        keep.wait()


def gather_all(shards, gain, sends, devices):
    anywhere = pl.BlockSpec(memory_space=pl.ANY)
    moved = SHARDS * sum(v.size for v in shards) + sum(v.size for v in sends)
    dma = pltpu.SemaphoreType.DMA
    out = [
        *[jax.ShapeDtypeStruct((SHARDS, *v.shape), v.dtype) for v in (*shards, gain)],
        *[jax.ShapeDtypeStruct(v.shape, v.dtype) for v in sends],
    ]
    return pl.pallas_call(
        functools.partial(gather_kernel, devices),
        in_specs=[anywhere] * 7,
        out_specs=[anywhere] * 7,
        out_shape=out,
        scratch_shapes=[
            dma((7,)),
            dma((4, 9)),
            dma((4, 9)),
            dma((SHARDS,)),
            dma((SHARDS,)),
            dma((2, devices)),
            dma((2, devices)),
        ],
        compiler_params=pltpu.CompilerParams(collective_id=0, has_side_effects=True),
        cost_estimate=cost(0, 16 * moved),
    )(*shards, gain, *sends)


def weave(weight):
    rows = weight.shape[0]
    gap = jnp.zeros((rows, FF_PAD - FF), weight.dtype)
    parts = [jnp.concatenate([weight[:, i * FF : (i + 1) * FF], gap], 1) for i in range(2)]
    tiles = [
        parts[half][:, step * FF_TILE : (step + 1) * FF_TILE]
        for step in range(FF_STEPS)
        for half in range(2)
    ]
    return jnp.concatenate(tiles, axis=1)


def unweave(woven):
    tiles = [
        woven[:, (2 * step + half) * FF_TILE :][:, : min(FF_TILE, FF - step * FF_TILE)]
        for half in range(2)
        for step in range(FF_STEPS)
    ]
    return jnp.concatenate(tiles, axis=1)


def body(tokens, cotangent, seq_lengths, w_qkv, w_out, w_in, w_down, attn_gain, mlp_gain):
    group_size = lax.axis_size("grp")
    devices = lax.axis_size("rep") * group_size
    device = lax.axis_index("rep") * group_size + lax.axis_index("grp")
    micros = min(MICRO, max(1, CHUNK_ROWS * devices // CAP))
    both = ("rep", "grp")

    def swap(rows):
        return lax.all_to_all(rows, both, split_axis=0, concat_axis=0, tiled=True)

    near = group_size == SHARDS and devices == REPLICAS * SHARDS
    sends = pack_rows(
        seq_lengths, (tokens[:, :, 0], cotangent[:, :, 0]), devices, micros
    )
    gains = jnp.stack([attn_gain, mlp_gain])
    shards = (w_down, weave(w_in), w_out, w_qkv)
    if near:
        gain = jnp.pad(gains, ((0, CHUNK_ROWS - 2), (0, 0)))
        *full, gains, token_rows, top_rows = gather_all(shards, gain, sends, devices)
        full = [v.reshape(-1, v.shape[-1]) for v in full]
        gains = jnp.swapaxes(gains[:, :2], 0, 1).reshape(2, D)
    else:
        token_rows, top_rows = (swap(v) for v in sends)
        full = [lax.all_gather(v, "grp", axis=0, tiled=True) for v in shards]
        gains = lax.all_gather(gains, "grp", axis=1, tiled=True)
    full_down, full_in, full_out, full_qkv = full
    gain_one = gains[:1].astype(F32)
    gain_two = gains[1:].astype(F32)

    cosine, sine = rotary_tables()
    hidden, act_a, top = unpack_rows(
        seq_lengths, token_rows, top_rows, gain_one, devices, micros
    )
    qkv = qkv_rows(act_a, full_qkv, cosine, sine)
    attn_o, prob = attend(qkv, seq_lengths, devices)
    middle, act_b = middle_rows(attn_o, hidden, full_out, gain_two)
    layer_rows, grad_b, grad_in_w, grad_down_w = ffn(act_b, top, middle, full_in, full_down)
    layer_send = repack_rows(seq_lengths, layer_rows, devices, micros)
    layer_back = swap(layer_send)
    grad_mid, grad_o, grad_out_w, grad_gain_two = branch_back(
        layer_send, grad_b, middle, top, attn_o, full_out, gain_two
    )
    grad_qkv_rows = attend_back(qkv, grad_o, prob, cosine, sine)
    grad_qkv_w = qkv_grad(act_a, grad_qkv_rows)
    grad_rows, gain_parts = input_back(
        grad_qkv_rows, full_qkv, hidden, grad_mid, gain_one, grad_gain_two
    )
    grad_back = swap(repack_rows(seq_lengths, grad_rows, devices, micros))
    parts = (grad_down_w, grad_in_w, grad_out_w, grad_qkv_w)
    if near:
        *owned, gain_sums = reduce_all((*parts, gain_parts))
        gain_sums = gain_sums[0].reshape(2, -1)
    else:
        owned = [
            lax.psum(lax.psum_scatter(v, "grp", scatter_dimension=0, tiled=True), "rep")
            for v in parts
        ]
        gain_parts = gain_parts[:, 0].reshape(SHARDS, 2, -1).swapaxes(0, 1).reshape(2, D)
        gain_sums = lax.psum(
            lax.psum_scatter(gain_parts, "grp", scatter_dimension=1, tiled=True), "rep"
        )
    grad_down, grad_in, grad_out, grad_qkv = (v.astype(F32) for v in owned)
    layer_out = spread_rows(seq_lengths, layer_back, devices, micros)[:, :, None, :]
    grad_tokens = spread_rows(seq_lengths, grad_back, devices, micros)[:, :, None, :]
    return (
        layer_out,
        grad_tokens,
        gain_sums[0],
        gain_sums[1],
        grad_qkv,
        grad_out,
        unweave(grad_in),
        grad_down,
    )


def solution(mesh):
    return jax.shard_map(
        body,
        mesh=mesh,
        in_specs=(
            P(None, None, ("rep", "grp"), None),
            P(None, None, ("rep", "grp"), None),
            P(),
            P("grp", None),
            P("grp", None),
            P("grp", None),
            P("grp", None),
            P("grp"),
            P("grp"),
        ),
        out_specs=(
            P(None, None, ("rep", "grp"), None),
            P(None, None, ("rep", "grp"), None),
            P("grp"),
            P("grp"),
            P("grp", None),
            P("grp", None),
            P("grp", None),
            P("grp", None),
        ),
        check_vma=False,
    )
```

```python
import functools
import math

import jax
import jax.numpy as jnp
import numpy as np
from jax import lax
from jax.experimental import pallas as pl
from jax.experimental.pallas import tpu as pltpu
from jax.sharding import PartitionSpec as P

D = 1024
HEADS = 16
HD = 64
FF = 2624
BLK = 128
MICRO = 4
SEQ_DEV = 2
CAP = 256
TOK_DEV = 192
ROWS = MICRO * CAP
BLOCKS = ROWS // BLK
PAIRS = HEADS // 2
LANES = 2 * HD

EPS = 1e-05
THETA = 160000.0
NEG = -1e30
ROOT_HALF = math.sqrt(0.5)
INV_ROOT_TWO_PI = 1.0 / math.sqrt(2.0 * math.pi)
SCALE = HD**-0.5

FF_TILE = 384
FF_STEPS = -(-FF // FF_TILE)
FF_PAD = FF_STEPS * FF_TILE
ROW_CHUNK = 256
CHUNK_ROWS = 16
SHARDS = 8
REPLICAS = 4
GAIN_ROWS = 8

F32 = jnp.float32
BF16 = jnp.bfloat16
MIB = 1 << 20


def dot(left, right, left_dim=1, right_dim=0):
    return lax.dot_general(
        left, right, (((left_dim,), (right_dim,)), ((), ())), preferred_element_type=F32
    )


def params(mib, steps=1):
    return pltpu.CompilerParams(
        vmem_limit_bytes=mib * MIB, dimension_semantics=("arbitrary",) * steps
    )


def cost(flops, moved, transcendentals=0):
    return pl.CostEstimate(
        flops=flops, bytes_accessed=moved, transcendentals=transcendentals
    )


def normed(values):
    center = values - jnp.mean(values, axis=-1, keepdims=True)
    inverse = lax.rsqrt(jnp.mean(center * center, axis=-1, keepdims=True) + EPS)
    return center * inverse, inverse


def norm_back(grad, normal, inverse):
    centred = grad - jnp.mean(grad, axis=-1, keepdims=True)
    return inverse * (centred - normal * jnp.mean(grad * normal, axis=-1, keepdims=True))


def rotary_tables():
    half = HD // 2
    frequency = np.float32(THETA) ** (-2.0 * np.arange(half, dtype=np.float32) / HD)
    angles = np.arange(BLK, dtype=np.float32)[:, None] * frequency.astype(np.float32)[None]
    cosine, sine = np.cos(angles), np.sin(angles)
    return (
        np.concatenate([cosine] * 4, axis=1).astype(np.float32),
        np.concatenate([-sine, sine] * 2, axis=1).astype(np.float32),
    )


def widen(table):
    return jnp.concatenate([table] * (QKV_TILE // LANES), axis=1)


def turned(values):
    axis = values.ndim - 1
    half = HD // 2
    width = values.shape[axis]
    lane = lax.broadcasted_iota(jnp.int32, values.shape, axis) % HD
    return jnp.where(
        lane < half,
        pltpu.roll(values, width - half, axis),
        pltpu.roll(values, half, axis),
    )


def position(devices):
    return lax.axis_index("rep") * (devices // lax.axis_size("rep")) + lax.axis_index("grp")


def length_sums(lengths_ref, chosen):
    return dot(
        lengths_ref[...].astype(F32).astype(BF16), chosen.astype(F32).astype(BF16)
    )


def slot_grid(sequences, devices):
    shape = (sequences, devices * CHUNK_ROWS)
    sequence = lax.broadcasted_iota(jnp.int32, shape, 0)
    slot = lax.broadcasted_iota(jnp.int32, shape, 1)
    inner = slot % CHUNK_ROWS
    pair_cap = CAP // devices
    return sequence, slot // CHUNK_ROWS, inner % pair_cap, inner // pair_cap


def ceil_div(value, count):
    return jnp.floor((value + (count - 0.5)) * (1.0 / count))


def sent_rows(lengths_ref, group, micros, devices):
    sequence, peer, rank, part = slot_grid(lengths_ref.shape[1], devices)
    starts = length_sums(lengths_ref, sequence < SEQ_DEV * peer)
    device = position(devices).astype(F32)
    wanted = ceil_div(starts - device, devices) + rank[:1].astype(F32)
    return pick_micros(wanted, part, group, micros, -1.0)


def pick_micros(values, part, group, micros, other):
    micro = lax.broadcasted_iota(jnp.int32, values.shape, 0)
    rows = []
    for step in range(micros):
        chosen = jnp.where(micro == group * micros + step, values, 0.0)
        row = jnp.sum(chosen, axis=0, keepdims=True)
        rows.append(jnp.where(part[:1] == step, row, other))
    return rows


def held_rows(lengths_ref, group, micros, devices):
    sequence, peer, rank, part = slot_grid(lengths_ref.shape[1], devices)
    device = position(devices)
    first = length_sums(lengths_ref, sequence < SEQ_DEV * device)
    source = peer[:1].astype(F32)
    given = (ceil_div(first - source, devices) + rank[:1].astype(F32)) * devices + source
    parts = [[None] * (CAP // BLK) for _ in range(micros)]
    for block in range(CAP // BLK):
        own = SEQ_DEV * device + block
        start = length_sums(lengths_ref, sequence < own)
        length = length_sums(lengths_ref, sequence == own)
        offsets = pick_micros(given - start, part, group, micros, -1.0)
        limits = pick_micros(length, part, group, micros, 0.0)
        for step in range(micros):
            place = lax.broadcasted_iota(jnp.int32, (BLK, part.shape[1]), 0).astype(F32)
            hit = (place == offsets[step]) & (place < limits[step])
            parts[step][block] = hit.astype(F32).astype(BF16)
    return jnp.concatenate([v for blocks in parts for v in blocks], axis=0)


def row_match(row):
    mine = lax.broadcasted_iota(jnp.int32, (TOK_DEV, row.shape[1]), 0).astype(F32)
    return (mine == row).astype(F32).astype(BF16)


def pack_kernel(micros, devices, lengths_ref, *refs):
    rows = sent_rows(lengths_ref, pl.program_id(0), micros, devices)
    picks = [row_match(row) for row in rows]
    count = len(refs) // 2
    for rows_ref, out_ref in zip(refs[:count], refs[count:]):
        total = None
        for step in range(micros):
            term = dot(picks[step], rows_ref[step], 0, 0)
            total = term if total is None else total + term
        out_ref[...] = total.astype(BF16).reshape(out_ref.shape)


def pack_rows(lengths, tables, devices, micros):
    groups = MICRO // micros
    slots = devices * CHUNK_ROWS
    count = len(tables)
    return pl.pallas_call(
        functools.partial(pack_kernel, micros, devices),
        grid=(groups,),
        in_specs=[
            pl.BlockSpec(lengths.shape, lambda g: (0, 0)),
            *[pl.BlockSpec((micros, TOK_DEV, D), lambda g: (g, 0, 0))] * count,
        ],
        out_specs=[
            pl.BlockSpec((devices, 1, CHUNK_ROWS, D), lambda g: (0, g, 0, 0))
        ]
        * count,
        out_shape=[jax.ShapeDtypeStruct((devices, groups, CHUNK_ROWS, D), BF16)] * count,
        compiler_params=params(48),
        cost_estimate=cost(
            2 * count * MICRO * TOK_DEV * slots * D, 4 * count * groups * slots * D
        ),
    )(lengths, *tables)


def spread_kernel(micros, devices, lengths_ref, back_ref, out_ref):
    arrived = back_ref[...].reshape(-1, D)
    rows = sent_rows(lengths_ref, pl.program_id(0), micros, devices)
    for step in range(micros):
        out_ref[step] = dot(row_match(rows[step]), arrived).astype(BF16)


def spread_rows(lengths, back, devices, micros):
    groups = MICRO // micros
    slots = devices * CHUNK_ROWS
    return pl.pallas_call(
        functools.partial(spread_kernel, micros, devices),
        grid=(groups,),
        in_specs=[
            pl.BlockSpec(lengths.shape, lambda g: (0, 0)),
            pl.BlockSpec((devices, 1, CHUNK_ROWS, D), lambda g: (0, g, 0, 0)),
        ],
        out_specs=pl.BlockSpec((micros, TOK_DEV, D), lambda g: (g, 0, 0)),
        out_shape=jax.ShapeDtypeStruct((MICRO, TOK_DEV, D), BF16),
        compiler_params=params(40),
        cost_estimate=cost(2 * MICRO * TOK_DEV * slots * D, 4 * groups * slots * D),
    )(lengths, back)


def unpack_kernel(
    micros, devices, lengths_ref, token_ref, top_ref, gain_ref, hidden_ref, act_ref, grad_ref
):
    pick = held_rows(lengths_ref, pl.program_id(0), micros, devices)
    rows = dot(pick, token_ref[...].reshape(-1, D))
    hidden_ref[...] = rows.astype(BF16)
    act_ref[...] = (normed(rows)[0] * gain_ref[...]).astype(BF16)
    grad_ref[...] = dot(pick, top_ref[...].reshape(-1, D)).astype(BF16)


def unpack_rows(lengths, tokens, top, gain, devices, micros):
    groups = MICRO // micros
    slots = devices * CHUNK_ROWS
    chunk = pl.BlockSpec((devices, 1, CHUNK_ROWS, D), lambda g: (0, g, 0, 0))
    return pl.pallas_call(
        functools.partial(unpack_kernel, micros, devices),
        grid=(groups,),
        in_specs=[
            pl.BlockSpec(lengths.shape, lambda g: (0, 0)),
            chunk,
            chunk,
            pl.BlockSpec((1, D), lambda g: (0, 0)),
        ],
        out_specs=[pl.BlockSpec((micros * CAP, D), lambda g: (g, 0))] * 3,
        out_shape=[jax.ShapeDtypeStruct((ROWS, D), BF16)] * 3,
        compiler_params=params(48),
        cost_estimate=cost(4 * ROWS * slots * D, 8 * groups * slots * D),
    )(lengths, tokens, top, gain)


def repack_kernel(micros, devices, lengths_ref, rows_ref, out_ref):
    pick = held_rows(lengths_ref, pl.program_id(0), micros, devices)
    out_ref[...] = dot(pick, rows_ref[...], 0, 0).astype(BF16).reshape(out_ref.shape)


def repack_rows(lengths, rows, devices, micros):
    groups = MICRO // micros
    slots = devices * CHUNK_ROWS
    return pl.pallas_call(
        functools.partial(repack_kernel, micros, devices),
        grid=(groups,),
        in_specs=[
            pl.BlockSpec(lengths.shape, lambda g: (0, 0)),
            pl.BlockSpec((micros * CAP, D), lambda g: (g, 0)),
        ],
        out_specs=pl.BlockSpec((devices, 1, CHUNK_ROWS, D), lambda g: (0, g, 0, 0)),
        out_shape=jax.ShapeDtypeStruct((devices, groups, CHUNK_ROWS, D), BF16),
        compiler_params=params(40),
        cost_estimate=cost(2 * ROWS * slots * D, 4 * groups * slots * D),
    )(lengths, rows)


QKV_TILE = 512


def qkv_kernel(act_ref, weight_ref, cos_ref, sin_ref, out_ref):
    packed = dot(act_ref[...], weight_ref[...])
    is_value = pl.program_id(0) >= 2 * D // QKV_TILE

    @pl.when(is_value)
    def _():
        out_ref[...] = packed.astype(BF16)

    @pl.when(jnp.logical_not(is_value))
    def _():
        split = packed.reshape(BLOCKS, BLK, QKV_TILE)
        spun = split * widen(cos_ref[...])[None] + turned(split) * widen(sin_ref[...])[None]
        out_ref[...] = spun.reshape(ROWS, QKV_TILE).astype(BF16)


def qkv_rows(act, weight, cosine, sine):
    return pl.pallas_call(
        qkv_kernel,
        grid=(3 * D // QKV_TILE,),
        in_specs=[
            pl.BlockSpec((ROWS, D), lambda j: (0, 0)),
            pl.BlockSpec((D, QKV_TILE), lambda j: (0, j)),
            pl.BlockSpec((BLK, LANES), lambda j: (0, 0)),
            pl.BlockSpec((BLK, LANES), lambda j: (0, 0)),
        ],
        out_specs=pl.BlockSpec((ROWS, QKV_TILE), lambda j: (0, j)),
        out_shape=jax.ShapeDtypeStruct((ROWS, 3 * D), BF16),
        compiler_params=params(40),
        cost_estimate=cost(2 * ROWS * D * 3 * D, 2 * (3 * D * D + ROWS * 4 * D)),
    )(act, weight, cosine, sine)


def head_masks(dtype):
    lane = lax.broadcasted_iota(jnp.int32, (BLK, LANES), 1)
    low = (lane < HD).astype(F32).astype(dtype)
    high = (lane >= HD).astype(F32).astype(dtype)
    return low, high


def attend_kernel(devices, length_ref, q_ref, k_ref, v_ref, out_ref, prob_ref):
    block = pl.program_id(0)
    low, high = head_masks(BF16)
    shape = (length_ref.shape[1], BLK)
    own = lax.broadcasted_iota(jnp.int32, shape, 0) == (
        SEQ_DEV * position(devices) + block % SEQ_DEV
    )
    lengths = length_sums(length_ref, own)
    micro = lax.broadcasted_iota(jnp.int32, lengths.shape, 0) == block // SEQ_DEV
    length = jnp.sum(jnp.where(micro, lengths, 0.0), axis=0, keepdims=True)
    valid = lax.broadcasted_iota(jnp.int32, (BLK, BLK), 1).astype(F32) < length
    for pair in range(PAIRS):
        lanes = slice(pair * LANES, (pair + 1) * LANES)
        query, key, value = q_ref[:, lanes], k_ref[:, lanes], v_ref[:, lanes]
        scores = dot(query, jnp.concatenate([key * low, key * high], axis=0), 1, 1)
        parts = []
        for head in range(2):
            score = scores[:, head * BLK : (head + 1) * BLK] * SCALE
            score = jnp.where(valid, score, NEG)
            expo = jnp.exp(score - jnp.max(score, axis=-1, keepdims=True))
            parts.append(expo / jnp.sum(expo, axis=-1, keepdims=True))
        prob = jnp.concatenate(parts, axis=1).astype(BF16)
        prob_ref[0, pair] = prob
        both = jnp.concatenate([value * low, value * high], axis=0)
        out_ref[:, lanes] = dot(prob, both).astype(BF16)


def attend(qkv, lengths, devices):
    return pl.pallas_call(
        functools.partial(attend_kernel, devices),
        grid=(BLOCKS,),
        in_specs=[
            pl.BlockSpec(lengths.shape, lambda b: (0, 0)),
            pl.BlockSpec((BLK, D), lambda b: (b, 0)),
            pl.BlockSpec((BLK, D), lambda b: (b, 1)),
            pl.BlockSpec((BLK, D), lambda b: (b, 2)),
        ],
        out_specs=[
            pl.BlockSpec((BLK, D), lambda b: (b, 0)),
            pl.BlockSpec((1, PAIRS, BLK, 2 * BLK), lambda b: (b, 0, 0, 0)),
        ],
        out_shape=[
            jax.ShapeDtypeStruct((ROWS, D), BF16),
            jax.ShapeDtypeStruct((BLOCKS, PAIRS, BLK, 2 * BLK), BF16),
        ],
        compiler_params=params(32),
        cost_estimate=cost(8 * ROWS * BLK * D, 2 * ROWS * 6 * D, ROWS * HEADS * BLK),
    )(lengths, qkv, qkv, qkv)


def attend_back_kernel(
    q_ref, k_ref, v_ref, grad_ref, prob_ref, cos_ref, sin_ref, out_ref
):
    for pair in range(PAIRS):
        start = pair * LANES
        lanes = slice(start, start + LANES)
        results = attend_back_pair(
            q_ref[:, lanes],
            k_ref[:, lanes],
            v_ref[:, lanes],
            grad_ref[:, lanes],
            prob_ref[0, pair],
            cos_ref[...],
            sin_ref[...],
        )
        for part, result in enumerate(results):
            out_ref[:, part * D + start : part * D + start + LANES] = result


def attend_back(qkv, grad_o, prob, cosine, sine):
    return pl.pallas_call(
        attend_back_kernel,
        grid=(BLOCKS,),
        in_specs=[
            pl.BlockSpec((BLK, D), lambda b: (b, 0)),
            pl.BlockSpec((BLK, D), lambda b: (b, 1)),
            pl.BlockSpec((BLK, D), lambda b: (b, 2)),
            pl.BlockSpec((BLK, D), lambda b: (b, 0)),
            pl.BlockSpec((1, PAIRS, BLK, 2 * BLK), lambda b: (b, 0, 0, 0)),
            pl.BlockSpec((BLK, LANES), lambda b: (0, 0)),
            pl.BlockSpec((BLK, LANES), lambda b: (0, 0)),
        ],
        out_specs=pl.BlockSpec((BLK, 3 * D), lambda b: (b, 0)),
        out_shape=jax.ShapeDtypeStruct((ROWS, 3 * D), BF16),
        compiler_params=params(32),
        cost_estimate=cost(20 * ROWS * BLK * D, 2 * ROWS * 9 * D),
    )(qkv, qkv, qkv, grad_o, prob, cosine, sine)


def middle_kernel(attn_ref, hidden_ref, weight_ref, gain_ref, mid_ref, act_ref):
    middle = hidden_ref[...].astype(F32) + dot(attn_ref[...], weight_ref[...])
    mid_ref[...] = middle
    act_ref[...] = (normed(middle)[0] * gain_ref[...]).astype(BF16)


def middle_rows(attn_o, hidden, weight, gain):
    tile = pl.BlockSpec((ROW_CHUNK, D), lambda i: (i, 0))
    return pl.pallas_call(
        middle_kernel,
        grid=(ROWS // ROW_CHUNK,),
        in_specs=[
            tile,
            tile,
            pl.BlockSpec((D, D), lambda i: (0, 0)),
            pl.BlockSpec((1, D), lambda i: (0, 0)),
        ],
        out_specs=[tile, tile],
        out_shape=[
            jax.ShapeDtypeStruct((ROWS, D), F32),
            jax.ShapeDtypeStruct((ROWS, D), BF16),
        ],
        compiler_params=params(32),
        cost_estimate=cost(2 * ROWS * D * D, 2 * D * D + 10 * ROWS * D),
    )(attn_o, hidden, weight, gain)


def ffn_kernel(
    act_ref,
    top_ref,
    mid_ref,
    in_ref,
    down_ref,
    layer_ref,
    grad_b_ref,
    grad_in_ref,
    grad_down_ref,
    total,
    act_t,
    down_clean,
    kept_c,
    kept_gu,
):
    step = pl.program_id(0)

    @pl.when(step == 0)
    def _():
        total[...] = mid_ref[...]
        grad_b_ref[...] = jnp.zeros_like(grad_b_ref)
        act_t[...] = act_ref[...].T

    row = lax.broadcasted_iota(jnp.int32, (FF_TILE, D), 0) + step * FF_TILE
    down_clean[...] = jnp.where(row < FF, down_ref[...].astype(F32), 0.0).astype(BF16)

    def rows_step(index, carry):
        rows = pl.ds(pl.multiple_of(index * ROW_CHUNK, ROW_CHUNK), ROW_CHUNK)
        act, top = act_ref[rows, :], top_ref[rows, :]
        gate_up = dot(act, in_ref[...])
        gelu_in, linear = gate_up[:, :FF_TILE], gate_up[:, FF_TILE:]
        grad_c = dot(top, down_clean[...], 1, 1)
        phi = 0.5 * (1.0 + lax.erf(gelu_in * ROOT_HALF))
        gelu_out = gelu_in * phi
        slope = phi + gelu_in * (jnp.exp(-0.5 * gelu_in * gelu_in) * INV_ROOT_TWO_PI)
        act_c = (gelu_out * linear).astype(BF16)
        kept_c[rows, :] = act_c
        kept_gu[rows, :FF_TILE] = (grad_c * linear * slope).astype(BF16)
        kept_gu[rows, FF_TILE:] = (grad_c * gelu_out).astype(BF16)
        total[rows, :] += dot(act_c, down_clean[...])
        grad_b_ref[rows, :] += dot(kept_gu[rows, :], in_ref[...], 1, 1)
        return carry

    lax.fori_loop(0, ROWS // ROW_CHUNK, rows_step, 0)
    grad_in_ref[...] = dot(act_t[...], kept_gu[...]).astype(BF16)
    grad_down_ref[...] = dot(kept_c[...], top_ref[...], 0, 0).astype(BF16)

    @pl.when(step == FF_STEPS - 1)
    def _():
        layer_ref[...] = total[...].astype(BF16)


def ffn(act, top, middle, full_in, full_down):
    whole = pl.BlockSpec((ROWS, D), lambda j: (0, 0))
    tall = pl.BlockSpec((D, 2 * FF_TILE), lambda j: (0, j))
    wide = pl.BlockSpec((FF_TILE, D), lambda j: (j, 0))
    return pl.pallas_call(
        ffn_kernel,
        grid=(FF_STEPS,),
        in_specs=[
            whole,
            whole,
            whole,
            tall,
            wide,
        ],
        out_specs=[whole, whole, tall, wide],
        out_shape=[
            jax.ShapeDtypeStruct((ROWS, D), BF16),
            jax.ShapeDtypeStruct((ROWS, D), F32),
            jax.ShapeDtypeStruct((D, 2 * FF_PAD), BF16),
            jax.ShapeDtypeStruct((FF, D), BF16),
        ],
        scratch_shapes=[
            pltpu.VMEM((ROWS, D), F32),
            pltpu.VMEM((D, ROWS), BF16),
            pltpu.VMEM((FF_TILE, D), BF16),
            pltpu.VMEM((ROWS, FF_TILE), BF16),
            pltpu.VMEM((ROWS, 2 * FF_TILE), BF16),
        ],
        compiler_params=params(60),
        cost_estimate=cost(18 * ROWS * D * FF, 12 * D * FF, 2 * ROWS * FF),
    )(act, top, middle, full_in, full_down)


def branch_kernel(
    order_ref,
    grad_b_ref,
    mid_ref,
    top_ref,
    attn_ref,
    weight_ref,
    gain_ref,
    grad_mid_ref,
    grad_o_ref,
    grad_w_ref,
    grad_gain_ref,
    total,
):
    step = pl.program_id(0)

    @pl.when(step == 0)
    def _():
        total[...] = jnp.zeros_like(total)
        grad_gain_ref[...] = jnp.zeros_like(grad_gain_ref)

    grad_b = grad_b_ref[...]
    normal, inverse = normed(mid_ref[...])
    grad_gain_ref[...] += jnp.sum(grad_b * normal, axis=0, keepdims=True)
    grad_mid = top_ref[...].astype(F32) + norm_back(
        grad_b * gain_ref[...], normal, inverse
    )
    grad_mid_ref[...] = grad_mid
    grad_r = grad_mid.astype(BF16)
    grad_o_ref[...] = dot(grad_r, weight_ref[...], 1, 1).astype(BF16)
    total[...] += dot(attn_ref[...], grad_r, 0, 0)

    @pl.when(step == ROWS // ROW_CHUNK - 1)
    def _():
        grad_w_ref[...] = total[...].astype(BF16)


def branch_back(order, grad_b, middle, top, attn_o, weight, gain):
    tile = pl.BlockSpec((ROW_CHUNK, D), lambda i: (i, 0))
    square = pl.BlockSpec((D, D), lambda i: (0, 0))
    line = pl.BlockSpec((1, D), lambda i: (0, 0))
    return pl.pallas_call(
        branch_kernel,
        grid=(ROWS // ROW_CHUNK,),
        in_specs=[
            pl.BlockSpec(memory_space=pl.ANY),
            *[tile] * 4,
            square,
            line,
        ],
        out_specs=[tile, tile, square, line],
        out_shape=[
            jax.ShapeDtypeStruct((ROWS, D), F32),
            jax.ShapeDtypeStruct((ROWS, D), BF16),
            jax.ShapeDtypeStruct((D, D), BF16),
            jax.ShapeDtypeStruct((1, D), F32),
        ],
        scratch_shapes=[pltpu.VMEM((D, D), F32)],
        compiler_params=params(40),
        cost_estimate=cost(4 * ROWS * D * D, 4 * D * D + 18 * ROWS * D),
    )(order, grad_b, middle, top, attn_o, weight, gain)


def input_kernel(
    grad_qkv_ref,
    weight_ref,
    hidden_ref,
    grad_mid_ref,
    gain_ref,
    other_ref,
    out_ref,
    gains_ref,
    grad_gain,
):
    @pl.when(pl.program_id(0) == 0)
    def _():
        grad_gain[...] = jnp.zeros_like(grad_gain)

    grad_a = dot(grad_qkv_ref[...], weight_ref[...], 1, 1)
    normal, inverse = normed(hidden_ref[...].astype(F32))
    grad_gain[...] += jnp.sum(grad_a * normal, axis=0, keepdims=True)
    out_ref[...] = (
        grad_mid_ref[...] + norm_back(grad_a * gain_ref[...], normal, inverse)
    ).astype(BF16)

    @pl.when(pl.program_id(0) == ROWS // ROW_CHUNK - 1)
    def _():
        width = D // SHARDS
        for shard in range(SHARDS):
            lanes = slice(shard * width, (shard + 1) * width)
            for part, values in enumerate((grad_gain, other_ref)):
                gains_ref[shard, :, part * width : (part + 1) * width] = jnp.broadcast_to(
                    values[:, lanes], (GAIN_ROWS, width)
                )


def input_back(grad_qkv, weight, hidden, grad_mid, gain, other):
    tile = pl.BlockSpec((ROW_CHUNK, D), lambda i: (i, 0))
    line = pl.BlockSpec((1, D), lambda i: (0, 0))
    return pl.pallas_call(
        input_kernel,
        grid=(ROWS // ROW_CHUNK,),
        in_specs=[
            pl.BlockSpec((ROW_CHUNK, 3 * D), lambda i: (i, 0)),
            pl.BlockSpec((D, 3 * D), lambda i: (0, 0)),
            tile,
            tile,
            line,
            line,
        ],
        out_specs=[
            tile,
            pl.BlockSpec((SHARDS, GAIN_ROWS, 2 * D // SHARDS), lambda i: (0, 0, 0)),
        ],
        out_shape=[
            jax.ShapeDtypeStruct((ROWS, D), BF16),
            jax.ShapeDtypeStruct((SHARDS, GAIN_ROWS, 2 * D // SHARDS), F32),
        ],
        scratch_shapes=[pltpu.VMEM((1, D), F32)],
        compiler_params=params(40),
        cost_estimate=cost(6 * ROWS * D * D, 6 * D * D + 14 * ROWS * D),
    )(grad_qkv, weight, hidden, grad_mid, gain, other)


def qkv_grad_kernel(act_ref, grad_ref, out_ref, act_t):
    @pl.when(pl.program_id(0) == 0)
    def _():
        act_t[...] = act_ref[...].T

    out_ref[...] = dot(act_t[...], grad_ref[...]).astype(BF16)


def qkv_grad(act, grad_qkv):
    return pl.pallas_call(
        qkv_grad_kernel,
        grid=(3 * D // QKV_TILE,),
        in_specs=[
            pl.BlockSpec((ROWS, D), lambda j: (0, 0)),
            pl.BlockSpec((ROWS, QKV_TILE), lambda j: (0, j)),
        ],
        out_specs=pl.BlockSpec((D, QKV_TILE), lambda j: (0, j)),
        out_shape=jax.ShapeDtypeStruct((D, 3 * D), BF16),
        scratch_shapes=[pltpu.VMEM((D, ROWS), BF16)],
        compiler_params=params(32),
        cost_estimate=cost(6 * ROWS * D * D, 2 * (7 * D * D)),
    )(act, grad_qkv)


MESH = pl.DeviceIdType.MESH
EARLY_CHUNKS = (
    (0, 0, 512),
    (0, 512, 512),
    *[(1, i * 768, 768) for i in range(7)],
    (2, 0, 1024),
)
LATE_CHUNKS = (
    (3, 0, 768),
    (3, 768, 768),
    (3, 1536, 768),
    (3, 2304, 512),
    (4, 0, 256),
    (3, 2816, 256),
)
REDUCE_CHUNKS = EARLY_CHUNKS + LATE_CHUNKS
HOP_CORE, HOP_X, HOP_Y, HOP_XY, HOP_YX, HOP_IN, HOP_MID, HOP_OUT = range(8)


def place():
    rep, grp = lax.axis_index("rep"), lax.axis_index("grp")
    core, x, y = grp % 2, grp // 2 % 2, grp // 4
    return rep, grp, core, x, y, grp + 1 - 2 * core, grp + 2 - 4 * x, grp + 4 - 8 * y


def mesh_id(index):
    return (index // SHARDS, lax.rem(index, SHARDS))


def greet_all(devices):
    device = position(devices)
    barrier = pltpu.get_barrier_semaphore()

    def greet(step, carry):
        to = mesh_id(lax.rem(device + step, devices))
        pl.semaphore_signal(barrier, device_id=to, device_id_type=MESH)
        return carry

    lax.fori_loop(1, devices, greet, 0)
    pl.semaphore_wait(barrier, devices - 1)


def row_exchange(send, land, local_sem, send_sem, recv_sem, devices):
    device = position(devices)

    def copy(step, slot):
        to = lax.rem(device + step, devices)
        return pltpu.make_async_remote_copy(
            src_ref=send(to),
            dst_ref=land(slot),
            send_sem=send_sem.at[step],
            recv_sem=recv_sem.at[step],
            device_id=mesh_id(to),
            device_id_type=MESH,
        )

    def keep():
        return pltpu.make_async_copy(send(device), land(device), local_sem)

    def start():
        def one(step, carry):
            copy(step, device).start()
            return carry

        keep().start()
        lax.fori_loop(1, devices, one, 0)

    def finish():
        def one(step, carry):
            copy(step, lax.rem(device + devices - step, devices)).wait_recv()
            copy(step, device).wait_send()
            return carry

        lax.fori_loop(1, devices, one, 0)
        keep().wait()

    return start, finish


def reduction(table, tensors, outs, refs):
    chunks = len(table)
    sums, from_core, from_near, from_cross, from_far = (
        refs[i * chunks : (i + 1) * chunks] for i in range(5)
    )
    load_sem, send_sem, recv_sem, store_sem = refs[5 * chunks :]
    rep, grp, core, x, y, by_core, by_x, by_y = place()
    is_middle = (rep == 1) | (rep == 2)
    inward, outward, across = 1 + rep // 2, 3 * (rep // 2), 3 - rep

    def hop(chunk, which):
        tensor, start, width = table[chunk]
        half = width // 2
        left, right, columns = pl.ds(0, half), pl.ds(half, half), pl.ds(start, width)
        total, far = sums[chunk], from_far[chunk]
        near, cross = from_near[chunk], from_cross[chunk]
        if which == HOP_CORE:
            source, target = tensors[tensor].at[:, :, 1 - core, :, columns], from_core[chunk]
        elif which == HOP_X:
            source, target = total.at[:, 1 - x, :, left], near.at[0]
        elif which == HOP_Y:
            source, target = total.at[1 - y, :, :, right], near.at[1]
        elif which == HOP_XY:
            source, target = total.at[1 - y, x, :, left], cross.at[0]
        elif which == HOP_YX:
            source, target = total.at[y, 1 - x, :, right], cross.at[1]
        elif which == HOP_IN:
            source, target = total.at[y, x], far.at[0]
        elif which == HOP_MID:
            source, target = total.at[y, x], far.at[1]
        else:
            source, target = far.at[0], outs[tensor].at[:, columns]
        to_rep = (rep, rep, rep, rep, rep, inward, across, outward)[which]
        to_grp = (by_core, by_x, by_y, by_y, by_x, grp, grp, grp)[which]
        return pltpu.make_async_remote_copy(
            src_ref=source,
            dst_ref=target,
            send_sem=send_sem.at[chunk, which],
            recv_sem=recv_sem.at[chunk, which],
            device_id=(to_rep, to_grp),
            device_id_type=MESH,
        )

    def load(chunk):
        tensor, start, width = table[chunk]
        return pltpu.make_async_copy(
            tensors[tensor].at[:, :, core, :, pl.ds(start, width)],
            sums[chunk],
            load_sem.at[chunk],
        )

    def store(chunk):
        tensor, start, width = table[chunk]
        return pltpu.make_async_copy(
            from_far[chunk].at[0],
            outs[tensor].at[:, pl.ds(start, width)],
            store_sem.at[chunk],
        )

    def add(one, other):
        return (one.astype(F32) + other.astype(F32)).astype(one.dtype)

    def after_core(chunk):
        load(chunk).wait()
        hop(chunk, HOP_CORE).wait_recv()
        total = sums[chunk]

        def plane(index, carry):
            row, column = index // 2, index % 2
            total[row, column] = add(total[row, column], from_core[chunk][row, column])
            return carry

        lax.fori_loop(0, 4, plane, 0)
        hop(chunk, HOP_X).start()
        hop(chunk, HOP_Y).start()

    def after_near(chunk):
        half = table[chunk][2] // 2
        hop(chunk, HOP_X).wait_recv()
        hop(chunk, HOP_Y).wait_recv()
        total, near = sums[chunk], from_near[chunk]

        def plane(index, carry):
            total[index, x, :, :half] = add(total[index, x, :, :half], near[0, index])
            total[y, index, :, half:] = add(total[y, index, :, half:], near[1, index])
            return carry

        lax.fori_loop(0, 2, plane, 0)
        hop(chunk, HOP_XY).start()
        hop(chunk, HOP_YX).start()

    def after_cross(chunk):
        half = table[chunk][2] // 2
        hop(chunk, HOP_XY).wait_recv()
        hop(chunk, HOP_YX).wait_recv()
        total, cross = sums[chunk], from_cross[chunk]
        total[y, x, :, :half] = add(total[y, x, :, :half], cross[0])
        total[y, x, :, half:] = add(total[y, x, :, half:], cross[1])

        @pl.when(jnp.logical_not(is_middle))
        def _():
            hop(chunk, HOP_IN).start()

    def after_in(chunk):
        @pl.when(is_middle)
        def _():
            hop(chunk, HOP_IN).wait_recv()
            total = sums[chunk]
            total[y, x] = add(total[y, x], from_far[chunk][0])
            hop(chunk, HOP_MID).start()

    def after_middle(chunk):
        @pl.when(is_middle)
        def _():
            hop(chunk, HOP_MID).wait_recv()
            far = from_far[chunk]
            far[0] = add(sums[chunk][y, x], far[1])
            hop(chunk, HOP_OUT).start()
            store(chunk).start()

    def start(some):
        for chunk in some:
            load(chunk).start()
            hop(chunk, HOP_CORE).start()

    stages = (after_core, after_near, after_cross, after_in, after_middle)

    def one_step(step):
        for late, stage in enumerate(stages):
            if 0 <= step - late < chunks:
                stage(step - late)

    steps = [functools.partial(one_step, i) for i in range(chunks + len(stages) - 1)]

    def finish():
        for chunk in range(chunks):
            for which in (HOP_CORE, HOP_X, HOP_Y, HOP_XY, HOP_YX):
                hop(chunk, which).wait_send()

        @pl.when(is_middle)
        def _():
            for chunk in range(chunks):
                hop(chunk, HOP_MID).wait_send()
                hop(chunk, HOP_OUT).wait_send()
                store(chunk).wait()

        @pl.when(jnp.logical_not(is_middle))
        def _():
            for chunk in range(chunks):
                hop(chunk, HOP_IN).wait_send()
                hop(chunk, HOP_OUT).wait_recv()

    return start, steps, finish


def reduction_scratch(table, split):
    kinds = [(split[t].dtype, split[t].shape[3], width) for t, _, width in table]
    dma = pltpu.SemaphoreType.DMA
    return [
        *[pltpu.VMEM((2, 2, r, w), t) for t, r, w in kinds],
        *[pltpu.VMEM((2, 2, r, w), t) for t, r, w in kinds],
        *[pltpu.VMEM((2, 2, r, w // 2), t) for t, r, w in kinds],
        *[pltpu.VMEM((2, r, w // 2), t) for t, r, w in kinds],
        *[pltpu.VMEM((2, r, w), t) for t, r, w in kinds],
        dma((len(table),)),
        dma((len(table), 8)),
        dma((len(table), 8)),
        dma((len(table),)),
    ]


def split_shards(parts):
    return [part.reshape(2, 2, 2, -1, part.shape[-1]) for part in parts]


def attend_back_pair(query, key, value, grad, prob, cosine, sine):
    low, high = head_masks(BF16)
    is_low = lax.broadcasted_iota(jnp.int32, (BLK, LANES), 1) < HD
    grad_v = dot(prob, grad, 0, 0)
    grad_v = jnp.where(is_low, grad_v[:BLK], grad_v[BLK:])
    grad_p = dot(grad, jnp.concatenate([value * low, value * high], axis=0), 1, 1)
    parts = []
    for head in range(2):
        keys = slice(head * BLK, (head + 1) * BLK)
        weight, slope = prob[:, keys].astype(F32), grad_p[:, keys]
        inner = jnp.sum(weight * slope, axis=-1, keepdims=True)
        parts.append(weight * (slope - inner))
    grad_s = jnp.concatenate(parts, axis=1).astype(BF16)
    both = jnp.concatenate([key * low, key * high], axis=0)
    grad_q = dot(grad_s, both) * SCALE
    grad_k = dot(grad_s, query, 0, 0)
    grad_k = jnp.where(is_low, grad_k[:BLK], grad_k[BLK:]) * SCALE
    return (
        (grad_q * cosine - turned(grad_q) * sine).astype(BF16),
        (grad_k * cosine - turned(grad_k) * sine).astype(BF16),
        grad_v.astype(BF16),
    )


FEATURES = D // SHARDS
SOME_ROWS = 128


def interleave(steps, pieces, ahead):
    for piece in pieces[:ahead]:
        piece()
    pieces = pieces[ahead:]
    done = 0
    for index, step in enumerate(steps):
        step()
        upto = -(-len(pieces) * (index + 1) // len(steps))
        for piece in pieces[done:upto]:
            piece()
        done = upto


def return_kernel(devices, micros, *refs):
    groups = MICRO // micros
    early = refs[:3]
    send, lengths_ref, qkv_ref, prob_ref, grad_o_ref, act_ref, hidden_ref = refs[3:10]
    mid_ref, weight_ref, gain_ref, other_ref, cos_ref, sin_ref = refs[10:16]
    outs, layer_land, grad_land, grad_w_ref, gains_ref = refs[16:21], *refs[21:25]
    wide, grads, block_prob, block_grad, act_part, w_part = refs[25:31]
    row_hidden, row_mid, kept, packed, grad_gain, gain_parts = refs[31:37]
    wide_sem, block_sem, act_sem, w_sem, row_sem, gain_sem = refs[37:43]
    layer_sems, grad_sems, refs = refs[43:46], refs[46:49], refs[49:]
    tensors = (*early, grad_w_ref, gains_ref)
    start, steps, finish = reduction(REDUCE_CHUNKS, tensors, outs, refs)
    start_layer, finish_layer = row_exchange(
        lambda to: send.at[to], lambda slot: layer_land.at[slot], *layer_sems, devices
    )
    exchanges = [
        row_exchange(
            lambda to, group=group: packed.at[group, to],
            lambda slot, group=group: grad_land.at[slot, group],
            *[sem.at[group] for sem in grad_sems],
            devices,
        )
        for group in range(groups)
    ]
    copy = pltpu.make_async_copy

    def block_loads(block):
        slot = block % 2
        rows = pl.ds(block * BLK, BLK)
        return (
            copy(prob_ref.at[block], block_prob.at[slot], block_sem.at[slot, 0]),
            copy(grad_o_ref.at[rows], block_grad.at[slot], block_sem.at[slot, 1]),
        )

    def act_load(part):
        columns = pl.ds(part * FEATURES, FEATURES)
        return copy(act_ref.at[:, columns], act_part.at[part % 2], act_sem.at[part % 2])

    def w_store(part):
        target = grad_w_ref.at[part // 4, part // 2 % 2, part % 2]
        return copy(w_part.at[part % 2], target, w_sem.at[part % 2])

    def row_loads(part):
        slot = part % 2
        rows = pl.ds(part * SOME_ROWS, SOME_ROWS)
        return (
            copy(hidden_ref.at[rows], row_hidden.at[slot], row_sem.at[slot, 0]),
            copy(mid_ref.at[rows], row_mid.at[slot], row_sem.at[slot, 1]),
        )

    load_qkv = copy(qkv_ref, wide, wide_sem.at[0])
    load_weight = copy(weight_ref, wide, wide_sem.at[1])

    def attend_piece(block):
        if block == 0:
            load_qkv.wait()
        for load in block_loads(block):
            load.wait()
        if block + 1 < BLOCKS:
            for load in block_loads(block + 1):
                load.start()
        slot = block % 2
        rows = slice(block * BLK, (block + 1) * BLK)

        def two(index, carry):
            for inner in range(2):
                pair = index * 2 + inner
                base = pl.multiple_of(pair * LANES, LANES)
                columns = [
                    pl.ds(pl.multiple_of(part * D + base, LANES), LANES) for part in range(3)
                ]
                results = attend_back_pair(
                    *[wide[rows, c] for c in columns],
                    block_grad[slot, :, pl.ds(base, LANES)],
                    block_prob[slot, pair],
                    cos_ref[...],
                    sin_ref[...],
                )
                for c, result in zip(columns, results):
                    grads[rows, c] = result
            return carry

        lax.fori_loop(0, PAIRS // 2, two, 0)
        if block == BLOCKS - 1:
            load_weight.start()
            act_load(0).start()

    def weight_piece(part):
        act_load(part).wait()
        if part + 1 < SHARDS:
            act_load(part + 1).start()
        if part >= 2:
            w_store(part - 2).wait()
        act_t = act_part[part % 2].T
        for third in range(3):
            columns = slice(third * D, (third + 1) * D)
            w_part[part % 2, :, columns] = dot(act_t, grads[:, columns]).astype(BF16)
        w_store(part).start()
        if part == SHARDS - 1:
            w_store(part - 1).wait()
            w_store(part).wait()
            start([i for i, c in enumerate(REDUCE_CHUNKS) if c[0] == 3])
            for load in row_loads(0):
                load.start()

    def row_piece(part):
        if part == 0:
            load_weight.wait()
            grad_gain[...] = jnp.zeros_like(grad_gain)
        for load in row_loads(part):
            load.wait()
        if part + 1 < BLOCKS:
            for load in row_loads(part + 1):
                load.start()
        slot = part % 2
        rows = slice(part * SOME_ROWS, (part + 1) * SOME_ROWS)
        grad_a = dot(grads[rows, :], wide[...], 1, 1)
        normal, inverse = normed(row_hidden[slot].astype(F32))
        grad_gain[...] += jnp.sum(grad_a * normal, axis=0, keepdims=True)
        each = BLOCKS // groups
        inner = slice(part % each * SOME_ROWS, (part % each + 1) * SOME_ROWS)
        kept[inner] = (
            row_mid[slot] + norm_back(grad_a * gain_ref[...], normal, inverse)
        ).astype(BF16)
        if part % each == each - 1:
            group = part // each
            pick = held_rows(lengths_ref, group, micros, devices)
            packed[group] = (
                dot(pick, kept[...], 0, 0).astype(BF16).reshape(packed.shape[1:])
            )
            exchanges[group][0]()

    def gain_piece():
        width = D // SHARDS
        for shard in range(SHARDS):
            columns = slice(shard * width, (shard + 1) * width)
            for part, values in enumerate((grad_gain, other_ref)):
                gain_parts[shard // 4, shard // 2 % 2, shard % 2, :, part * width : (part + 1) * width] = (
                    jnp.broadcast_to(values[:, columns], (GAIN_ROWS, width))
                )
        keep = copy(gain_parts, gains_ref, gain_sem)
        keep.start()
        keep.wait()
        start([i for i, c in enumerate(REDUCE_CHUNKS) if c[0] == 4])

    greet_all(devices)
    load_qkv.start()
    for load in block_loads(0):
        load.start()
    start(range(len(EARLY_CHUNKS)))
    start_layer()
    pieces = [
        *[functools.partial(attend_piece, i) for i in range(BLOCKS)],
        *[functools.partial(weight_piece, i) for i in range(SHARDS)],
        *[functools.partial(row_piece, i) for i in range(BLOCKS)],
        gain_piece,
    ]
    count = len(EARLY_CHUNKS)
    interleave(steps[:count], pieces, 2)
    for step in steps[count:]:
        step()
    finish()
    finish_layer()
    for exchange in exchanges:
        exchange[1]()


def return_all(
    parts,
    send,
    lengths,
    qkv,
    prob,
    grad_o,
    act,
    hidden,
    grad_mid,
    weight,
    gain,
    other,
    tables,
    devices,
    micros,
):
    early = split_shards(parts)
    groups = MICRO // micros
    rows = D // SHARDS
    split = [
        *early,
        jax.ShapeDtypeStruct((2, 2, 2, rows, 3 * D), BF16),
        jax.ShapeDtypeStruct((2, 2, 2, GAIN_ROWS, 2 * rows), F32),
    ]
    anywhere = pl.BlockSpec(memory_space=pl.ANY)
    inside = pl.BlockSpec(memory_space=pltpu.VMEM)
    dma = pltpu.SemaphoreType.DMA
    *owned, layer_back, grad_back, _, _ = pl.pallas_call(
        functools.partial(return_kernel, devices, micros),
        in_specs=[
            *[anywhere] * 4,
            inside,
            *[anywhere] * 7,
            *[inside] * 4,
        ],
        out_specs=[anywhere] * 9,
        out_shape=[
            *[jax.ShapeDtypeStruct(v.shape[3:], v.dtype) for v in split],
            jax.ShapeDtypeStruct(send.shape, send.dtype),
            jax.ShapeDtypeStruct(send.shape, send.dtype),
            *split[3:],
        ],
        scratch_shapes=[
            pltpu.VMEM((ROWS, 3 * D), BF16),
            pltpu.VMEM((ROWS, 3 * D), BF16),
            pltpu.VMEM((2, PAIRS, BLK, 2 * BLK), BF16),
            pltpu.VMEM((2, BLK, D), BF16),
            pltpu.VMEM((2, ROWS, FEATURES), BF16),
            pltpu.VMEM((2, FEATURES, 3 * D), BF16),
            pltpu.VMEM((2, SOME_ROWS, D), BF16),
            pltpu.VMEM((2, SOME_ROWS, D), F32),
            pltpu.VMEM((ROWS // groups, D), BF16),
            pltpu.VMEM((groups, devices, CHUNK_ROWS, D), BF16),
            pltpu.VMEM((1, D), F32),
            pltpu.VMEM((2, 2, 2, GAIN_ROWS, 2 * rows), F32),
            dma((2,)),
            dma((2, 2)),
            dma((2,)),
            dma((2,)),
            dma((2, 2)),
            dma,
            dma,
            dma((devices,)),
            dma((devices,)),
            dma((groups,)),
            dma((groups, devices)),
            dma((groups, devices)),
            *reduction_scratch(REDUCE_CHUNKS, split),
        ],
        compiler_params=pltpu.CompilerParams(
            vmem_limit_bytes=63 * MIB, collective_id=1, has_side_effects=True
        ),
        cost_estimate=cost(16 * ROWS * D * D, 600 * MIB),
    )(
        *early,
        send,
        lengths,
        qkv,
        prob,
        grad_o,
        act,
        hidden,
        grad_mid,
        weight,
        gain,
        other,
        *tables,
    )
    return (*owned, layer_back, grad_back)


WAY_X, WAY_Y, WAY_CORE, WAY_CORE_X, WAY_CORE_Y = range(5)
WAY_XY, WAY_YX, WAY_CORE_XY, WAY_CORE_YX = range(5, 9)


def gather_kernel(devices, *refs):
    shards, refs = refs[:4], refs[4:]
    gain, sends, refs = refs[0], refs[1:3], refs[3:]
    fulls, refs = refs[:4], refs[4:]
    gains, lands, refs = refs[0], refs[1:3], refs[3:]
    local_sem, way_send, way_recv, gain_send, gain_recv, row_send, row_recv = refs
    rep, grp, core, x, y, by_core, by_x, by_y = place()
    by_xy = by_x + by_y - grp
    other = by_core - grp
    device = rep * SHARDS + grp

    def peer(step):
        return lax.rem(device + step, devices)

    def mesh_id(index):
        return (index // SHARDS, lax.rem(index, SHARDS))

    barrier = pltpu.get_barrier_semaphore()

    def greet(step, carry):
        pl.semaphore_signal(barrier, device_id=mesh_id(peer(step)), device_id_type=MESH)
        return carry

    lax.fori_loop(1, devices, greet, 0)
    pl.semaphore_wait(barrier, devices - 1)

    def way(which, tensor):
        full, width = fulls[tensor], shards[tensor].shape[1]
        left, right = pl.ds(0, width // 2), pl.ds(width // 2, width // 2)
        own = shards[tensor]
        source, slot, landing, part, to = {
            WAY_X: (own, grp, by_x, None, by_x),
            WAY_Y: (own, grp, by_y, None, by_y),
            WAY_CORE: (own, grp, by_core, None, by_core),
            WAY_CORE_X: (None, by_x, by_x + other, None, by_core),
            WAY_CORE_Y: (None, by_y, by_y + other, None, by_core),
            WAY_XY: (None, by_x, by_xy, left, by_y),
            WAY_YX: (None, by_y, by_xy, right, by_x),
            WAY_CORE_XY: (None, by_xy, by_xy + other, left, by_core),
            WAY_CORE_YX: (None, by_xy, by_xy + other, right, by_core),
        }[which]

        def view(index):
            return full.at[index] if part is None else full.at[index, :, part]

        def copy(source, target):
            return pltpu.make_async_remote_copy(
                src_ref=source,
                dst_ref=target,
                send_sem=way_send.at[tensor, which],
                recv_sem=way_recv.at[tensor, which],
                device_id=(rep, to),
                device_id_type=MESH,
            )

        def start():
            copy(view(slot) if source is None else source, view(slot)).start()

        def arrive():
            copy(view(landing), view(landing)).wait_recv()

        def sent():
            copy(view(slot) if source is None else source, view(slot)).wait_send()

        return start, arrive, sent

    def start(tensor, *ways):
        for which in ways:
            way(which, tensor)[0]()

    def arrive(tensor, *ways):
        for which in ways:
            way(which, tensor)[1]()

    def gain_copy(step, slot):
        to = lax.rem(grp + step, SHARDS)
        return pltpu.make_async_remote_copy(
            src_ref=gain,
            dst_ref=gains.at[slot],
            send_sem=gain_send.at[step],
            recv_sem=gain_recv.at[step],
            device_id=(rep, to),
            device_id_type=MESH,
        )

    def row_copy(which, step, source, slot, to):
        return pltpu.make_async_remote_copy(
            src_ref=sends[which].at[source],
            dst_ref=lands[which].at[slot],
            send_sem=row_send.at[which, step],
            recv_sem=row_recv.at[which, step],
            device_id=mesh_id(to),
            device_id_type=MESH,
        )

    def send_rows(which):
        def one(step, carry):
            row_copy(which, step, peer(step), device, peer(step)).start()
            return carry

        lax.fori_loop(1, devices, one, 0)

    def land_rows(which):
        def one(step, carry):
            source = lax.rem(device + devices - step, devices)
            row_copy(which, step, peer(step), source, peer(step)).wait_recv()
            row_copy(which, step, peer(step), device, peer(step)).wait_send()
            return carry

        lax.fori_loop(1, devices, one, 0)

    def local(index, source, target):
        return pltpu.make_async_copy(source, target, local_sem.at[index])

    keeps = [local(i, shards[i], fulls[i].at[grp]) for i in range(4)]
    keeps.append(local(4, gain, gains.at[grp]))
    keeps += [local(5 + i, sends[i].at[device], lands[i].at[device]) for i in range(2)]

    for step in range(1, SHARDS):
        gain_copy(step, grp).start()
    start(3, WAY_X, WAY_Y, WAY_CORE)
    send_rows(0)
    for tensor in (2, 1, 0):
        start(tensor, WAY_X, WAY_Y, WAY_CORE)
    send_rows(1)
    for keep in keeps:
        keep.start()
    order = (3, 2, 1, 0)
    for late in range(len(order) + 1):
        if late < len(order):
            tensor = order[late]
            arrive(tensor, WAY_X)
            start(tensor, WAY_XY, WAY_CORE_X)
            arrive(tensor, WAY_Y)
            start(tensor, WAY_YX, WAY_CORE_Y)
        if late:
            tensor = order[late - 1]
            arrive(tensor, WAY_XY)
            start(tensor, WAY_CORE_XY)
            arrive(tensor, WAY_YX)
            start(tensor, WAY_CORE_YX)
    for tensor in order:
        arrive(tensor, WAY_CORE, WAY_CORE_X, WAY_CORE_Y, WAY_CORE_XY, WAY_CORE_YX)
    for step in range(1, SHARDS):
        gain_copy(step, lax.rem(grp + SHARDS - step, SHARDS)).wait_recv()
        gain_copy(step, grp).wait_send()
    for which in range(2):
        land_rows(which)
    for tensor in order:
        for which in range(9):
            way(which, tensor)[2]()
    for keep in keeps:
        keep.wait()


def gather_all(shards, gain, sends, devices):
    anywhere = pl.BlockSpec(memory_space=pl.ANY)
    moved = SHARDS * sum(v.size for v in shards) + sum(v.size for v in sends)
    dma = pltpu.SemaphoreType.DMA
    out = [
        *[jax.ShapeDtypeStruct((SHARDS, *v.shape), v.dtype) for v in (*shards, gain)],
        *[jax.ShapeDtypeStruct(v.shape, v.dtype) for v in sends],
    ]
    return pl.pallas_call(
        functools.partial(gather_kernel, devices),
        in_specs=[anywhere] * 7,
        out_specs=[anywhere] * 7,
        out_shape=out,
        scratch_shapes=[
            dma((7,)),
            dma((4, 9)),
            dma((4, 9)),
            dma((SHARDS,)),
            dma((SHARDS,)),
            dma((2, devices)),
            dma((2, devices)),
        ],
        compiler_params=pltpu.CompilerParams(collective_id=0, has_side_effects=True),
        cost_estimate=cost(0, 16 * moved),
    )(*shards, gain, *sends)


def weave(weight):
    rows = weight.shape[0]
    gap = jnp.zeros((rows, FF_PAD - FF), weight.dtype)
    parts = [jnp.concatenate([weight[:, i * FF : (i + 1) * FF], gap], 1) for i in range(2)]
    tiles = [
        parts[half][:, step * FF_TILE : (step + 1) * FF_TILE]
        for step in range(FF_STEPS)
        for half in range(2)
    ]
    return jnp.concatenate(tiles, axis=1)


def unweave(woven):
    tiles = [
        woven[:, (2 * step + half) * FF_TILE :][:, : min(FF_TILE, FF - step * FF_TILE)]
        for half in range(2)
        for step in range(FF_STEPS)
    ]
    return jnp.concatenate(tiles, axis=1)


def body(tokens, cotangent, seq_lengths, w_qkv, w_out, w_in, w_down, attn_gain, mlp_gain):
    group_size = lax.axis_size("grp")
    devices = lax.axis_size("rep") * group_size
    device = lax.axis_index("rep") * group_size + lax.axis_index("grp")
    micros = min(MICRO, max(1, CHUNK_ROWS * devices // CAP))
    both = ("rep", "grp")

    def swap(rows):
        return lax.all_to_all(rows, both, split_axis=0, concat_axis=0, tiled=True)

    near = group_size == SHARDS and devices == REPLICAS * SHARDS
    sends = pack_rows(
        seq_lengths, (tokens[:, :, 0], cotangent[:, :, 0]), devices, micros
    )
    gains = jnp.stack([attn_gain, mlp_gain])
    shards = (w_down, weave(w_in), w_out, w_qkv)
    if near:
        gain = jnp.pad(gains, ((0, CHUNK_ROWS - 2), (0, 0)))
        *full, gains, token_rows, top_rows = gather_all(shards, gain, sends, devices)
        full = [v.reshape(-1, v.shape[-1]) for v in full]
        gains = jnp.swapaxes(gains[:, :2], 0, 1).reshape(2, D)
    else:
        token_rows, top_rows = (swap(v) for v in sends)
        full = [lax.all_gather(v, "grp", axis=0, tiled=True) for v in shards]
        gains = lax.all_gather(gains, "grp", axis=1, tiled=True)
    full_down, full_in, full_out, full_qkv = full
    gain_one = gains[:1].astype(F32)
    gain_two = gains[1:].astype(F32)

    cosine, sine = rotary_tables()
    hidden, act_a, top = unpack_rows(
        seq_lengths, token_rows, top_rows, gain_one, devices, micros
    )
    qkv = qkv_rows(act_a, full_qkv, cosine, sine)
    attn_o, prob = attend(qkv, seq_lengths, devices)
    middle, act_b = middle_rows(attn_o, hidden, full_out, gain_two)
    layer_rows, grad_b, grad_in_w, grad_down_w = ffn(act_b, top, middle, full_in, full_down)
    layer_send = repack_rows(seq_lengths, layer_rows, devices, micros)
    grad_mid, grad_o, grad_out_w, grad_gain_two = branch_back(
        layer_send, grad_b, middle, top, attn_o, full_out, gain_two
    )
    if near:
        grad_down, grad_in, grad_out, grad_qkv, gain_sums, layer_back, grad_back = return_all(
            (grad_down_w, grad_in_w, grad_out_w),
            layer_send,
            seq_lengths,
            qkv,
            prob,
            grad_o,
            act_a,
            hidden,
            grad_mid,
            full_qkv,
            gain_one,
            grad_gain_two,
            (cosine, sine),
            devices,
            micros,
        )
        gain_sums = gain_sums[0].reshape(2, -1)
    else:
        layer_back = swap(layer_send)
        grad_qkv_rows = attend_back(qkv, grad_o, prob, cosine, sine)
        grad_qkv_w = qkv_grad(act_a, grad_qkv_rows)
        grad_rows, gain_parts = input_back(
            grad_qkv_rows, full_qkv, hidden, grad_mid, gain_one, grad_gain_two
        )
        grad_back = swap(repack_rows(seq_lengths, grad_rows, devices, micros))
        grad_down, grad_in, grad_out, grad_qkv = (
            lax.psum(lax.psum_scatter(v, "grp", scatter_dimension=0, tiled=True), "rep")
            for v in (grad_down_w, grad_in_w, grad_out_w, grad_qkv_w)
        )
        gain_parts = gain_parts[:, 0].reshape(SHARDS, 2, -1).swapaxes(0, 1).reshape(2, D)
        gain_sums = lax.psum(
            lax.psum_scatter(gain_parts, "grp", scatter_dimension=1, tiled=True), "rep"
        )
    grad_down, grad_in, grad_out, grad_qkv = (
        v.astype(F32) for v in (grad_down, grad_in, grad_out, grad_qkv)
    )
    layer_out = spread_rows(seq_lengths, layer_back, devices, micros)[:, :, None, :]
    grad_tokens = spread_rows(seq_lengths, grad_back, devices, micros)[:, :, None, :]
    return (
        layer_out,
        grad_tokens,
        gain_sums[0],
        gain_sums[1],
        grad_qkv,
        grad_out,
        unweave(grad_in),
        grad_down,
    )


def solution(mesh):
    return jax.shard_map(
        body,
        mesh=mesh,
        in_specs=(
            P(None, None, ("rep", "grp"), None),
            P(None, None, ("rep", "grp"), None),
            P(),
            P("grp", None),
            P("grp", None),
            P("grp", None),
            P("grp", None),
            P("grp"),
            P("grp"),
        ),
        out_specs=(
            P(None, None, ("rep", "grp"), None),
            P(None, None, ("rep", "grp"), None),
            P("grp"),
            P("grp"),
            P("grp", None),
            P("grp", None),
            P("grp", None),
            P("grp", None),
        ),
        check_vma=False,
    )
```

```python
import functools
import math

import jax
import jax.numpy as jnp
import numpy as np
from jax import lax
from jax.experimental import pallas as pl
from jax.experimental.pallas import tpu as pltpu
from jax.sharding import PartitionSpec as P

D = 1024
HEADS = 16
HD = 64
FF = 2624
BLK = 128
MICRO = 4
SEQ_DEV = 2
CAP = 256
TOK_DEV = 192
ROWS = MICRO * CAP
BLOCKS = ROWS // BLK
PAIRS = HEADS // 2
LANES = 2 * HD

EPS = 1e-05
THETA = 160000.0
NEG = -1e30
ROOT_HALF = math.sqrt(0.5)
INV_ROOT_TWO_PI = 1.0 / math.sqrt(2.0 * math.pi)
SCALE = HD**-0.5

FF_TILE = 384
ROW_CHUNK = 256
CHUNK_ROWS = 16
SHARDS = 8
REPLICAS = 4
GAIN_ROWS = 8

F32 = jnp.float32
BF16 = jnp.bfloat16
MIB = 1 << 20


def dot(left, right, left_dim=1, right_dim=0):
    return lax.dot_general(
        left, right, (((left_dim,), (right_dim,)), ((), ())), preferred_element_type=F32
    )


def params(mib, steps=1):
    return pltpu.CompilerParams(
        vmem_limit_bytes=mib * MIB, dimension_semantics=("arbitrary",) * steps
    )


def cost(flops, moved, transcendentals=0):
    return pl.CostEstimate(
        flops=flops, bytes_accessed=moved, transcendentals=transcendentals
    )


def normed(values):
    center = values - jnp.mean(values, axis=-1, keepdims=True)
    inverse = lax.rsqrt(jnp.mean(center * center, axis=-1, keepdims=True) + EPS)
    return center * inverse, inverse


def norm_back(grad, normal, inverse):
    centred = grad - jnp.mean(grad, axis=-1, keepdims=True)
    return inverse * (centred - normal * jnp.mean(grad * normal, axis=-1, keepdims=True))


def rotary_tables():
    half = HD // 2
    frequency = np.float32(THETA) ** (-2.0 * np.arange(half, dtype=np.float32) / HD)
    angles = np.arange(BLK, dtype=np.float32)[:, None] * frequency.astype(np.float32)[None]
    cosine, sine = np.cos(angles), np.sin(angles)
    return (
        np.concatenate([cosine] * 4, axis=1).astype(np.float32),
        np.concatenate([-sine, sine] * 2, axis=1).astype(np.float32),
    )


def widen(table):
    return jnp.concatenate([table] * (QKV_TILE // LANES), axis=1)


def turned(values):
    axis = values.ndim - 1
    half = HD // 2
    width = values.shape[axis]
    lane = lax.broadcasted_iota(jnp.int32, values.shape, axis) % HD
    return jnp.where(
        lane < half,
        pltpu.roll(values, width - half, axis),
        pltpu.roll(values, half, axis),
    )


def position(devices):
    return lax.axis_index("rep") * (devices // lax.axis_size("rep")) + lax.axis_index("grp")


def length_sums(lengths_ref, chosen):
    return dot(
        lengths_ref[...].astype(F32).astype(BF16), chosen.astype(F32).astype(BF16)
    )


def slot_grid(sequences, devices):
    shape = (sequences, devices * CHUNK_ROWS)
    sequence = lax.broadcasted_iota(jnp.int32, shape, 0)
    slot = lax.broadcasted_iota(jnp.int32, shape, 1)
    inner = slot % CHUNK_ROWS
    pair_cap = CAP // devices
    return sequence, slot // CHUNK_ROWS, inner % pair_cap, inner // pair_cap


def ceil_div(value, count):
    return jnp.floor((value + (count - 0.5)) * (1.0 / count))


def sent_rows(lengths_ref, group, micros, devices):
    sequence, peer, rank, part = slot_grid(lengths_ref.shape[1], devices)
    starts = length_sums(lengths_ref, sequence < SEQ_DEV * peer)
    device = position(devices).astype(F32)
    wanted = ceil_div(starts - device, devices) + rank[:1].astype(F32)
    return pick_micros(wanted, part, group, micros, -1.0)


def pick_micros(values, part, group, micros, other):
    micro = lax.broadcasted_iota(jnp.int32, values.shape, 0)
    rows = []
    for step in range(micros):
        chosen = jnp.where(micro == group * micros + step, values, 0.0)
        row = jnp.sum(chosen, axis=0, keepdims=True)
        rows.append(jnp.where(part[:1] == step, row, other))
    return rows


def held_rows(lengths_ref, group, micros, devices):
    sequence, peer, rank, part = slot_grid(lengths_ref.shape[1], devices)
    device = position(devices)
    first = length_sums(lengths_ref, sequence < SEQ_DEV * device)
    source = peer[:1].astype(F32)
    given = (ceil_div(first - source, devices) + rank[:1].astype(F32)) * devices + source
    parts = [[None] * (CAP // BLK) for _ in range(micros)]
    for block in range(CAP // BLK):
        own = SEQ_DEV * device + block
        start = length_sums(lengths_ref, sequence < own)
        length = length_sums(lengths_ref, sequence == own)
        offsets = pick_micros(given - start, part, group, micros, -1.0)
        limits = pick_micros(length, part, group, micros, 0.0)
        for step in range(micros):
            place = lax.broadcasted_iota(jnp.int32, (BLK, part.shape[1]), 0).astype(F32)
            hit = (place == offsets[step]) & (place < limits[step])
            parts[step][block] = hit.astype(F32).astype(BF16)
    return jnp.concatenate([v for blocks in parts for v in blocks], axis=0)


def row_match(row):
    mine = lax.broadcasted_iota(jnp.int32, (TOK_DEV, row.shape[1]), 0).astype(F32)
    return (mine == row).astype(F32).astype(BF16)


def pack_kernel(micros, devices, lengths_ref, *refs):
    rows = sent_rows(lengths_ref, pl.program_id(0), micros, devices)
    picks = [row_match(row) for row in rows]
    count = len(refs) // 2
    for rows_ref, out_ref in zip(refs[:count], refs[count:]):
        total = None
        for step in range(micros):
            term = dot(picks[step], rows_ref[step], 0, 0)
            total = term if total is None else total + term
        out_ref[...] = total.astype(BF16).reshape(out_ref.shape)


def pack_rows(lengths, tables, devices, micros):
    groups = MICRO // micros
    slots = devices * CHUNK_ROWS
    count = len(tables)
    return pl.pallas_call(
        functools.partial(pack_kernel, micros, devices),
        grid=(groups,),
        in_specs=[
            pl.BlockSpec(lengths.shape, lambda g: (0, 0)),
            *[pl.BlockSpec((micros, TOK_DEV, D), lambda g: (g, 0, 0))] * count,
        ],
        out_specs=[
            pl.BlockSpec((devices, 1, CHUNK_ROWS, D), lambda g: (0, g, 0, 0))
        ]
        * count,
        out_shape=[jax.ShapeDtypeStruct((devices, groups, CHUNK_ROWS, D), BF16)] * count,
        compiler_params=params(48),
        cost_estimate=cost(
            2 * count * MICRO * TOK_DEV * slots * D, 4 * count * groups * slots * D
        ),
    )(lengths, *tables)


def spread_kernel(micros, devices, lengths_ref, back_ref, out_ref):
    arrived = back_ref[...].reshape(-1, D)
    rows = sent_rows(lengths_ref, pl.program_id(0), micros, devices)
    for step in range(micros):
        out_ref[step] = dot(row_match(rows[step]), arrived).astype(BF16)


def spread_rows(lengths, back, devices, micros):
    groups = MICRO // micros
    slots = devices * CHUNK_ROWS
    return pl.pallas_call(
        functools.partial(spread_kernel, micros, devices),
        grid=(groups,),
        in_specs=[
            pl.BlockSpec(lengths.shape, lambda g: (0, 0)),
            pl.BlockSpec((devices, 1, CHUNK_ROWS, D), lambda g: (0, g, 0, 0)),
        ],
        out_specs=pl.BlockSpec((micros, TOK_DEV, D), lambda g: (g, 0, 0)),
        out_shape=jax.ShapeDtypeStruct((MICRO, TOK_DEV, D), BF16),
        compiler_params=params(40),
        cost_estimate=cost(2 * MICRO * TOK_DEV * slots * D, 4 * groups * slots * D),
    )(lengths, back)


def unpack_kernel(
    micros, devices, lengths_ref, token_ref, top_ref, gain_ref, hidden_ref, act_ref, grad_ref
):
    pick = held_rows(lengths_ref, pl.program_id(0), micros, devices)
    rows = dot(pick, token_ref[...].reshape(-1, D))
    hidden_ref[...] = rows.astype(BF16)
    act_ref[...] = (normed(rows)[0] * gain_ref[...]).astype(BF16)
    grad_ref[...] = dot(pick, top_ref[...].reshape(-1, D)).astype(BF16)


def unpack_rows(lengths, tokens, top, gain, devices, micros):
    groups = MICRO // micros
    slots = devices * CHUNK_ROWS
    chunk = pl.BlockSpec((devices, 1, CHUNK_ROWS, D), lambda g: (0, g, 0, 0))
    return pl.pallas_call(
        functools.partial(unpack_kernel, micros, devices),
        grid=(groups,),
        in_specs=[
            pl.BlockSpec(lengths.shape, lambda g: (0, 0)),
            chunk,
            chunk,
            pl.BlockSpec((1, D), lambda g: (0, 0)),
        ],
        out_specs=[pl.BlockSpec((micros * CAP, D), lambda g: (g, 0))] * 3,
        out_shape=[jax.ShapeDtypeStruct((ROWS, D), BF16)] * 3,
        compiler_params=params(48),
        cost_estimate=cost(4 * ROWS * slots * D, 8 * groups * slots * D),
    )(lengths, tokens, top, gain)


def repack_kernel(micros, devices, lengths_ref, rows_ref, out_ref):
    pick = held_rows(lengths_ref, pl.program_id(0), micros, devices)
    out_ref[...] = dot(pick, rows_ref[...], 0, 0).astype(BF16).reshape(out_ref.shape)


def repack_rows(lengths, rows, devices, micros):
    groups = MICRO // micros
    slots = devices * CHUNK_ROWS
    return pl.pallas_call(
        functools.partial(repack_kernel, micros, devices),
        grid=(groups,),
        in_specs=[
            pl.BlockSpec(lengths.shape, lambda g: (0, 0)),
            pl.BlockSpec((micros * CAP, D), lambda g: (g, 0)),
        ],
        out_specs=pl.BlockSpec((devices, 1, CHUNK_ROWS, D), lambda g: (0, g, 0, 0)),
        out_shape=jax.ShapeDtypeStruct((devices, groups, CHUNK_ROWS, D), BF16),
        compiler_params=params(40),
        cost_estimate=cost(2 * ROWS * slots * D, 4 * groups * slots * D),
    )(lengths, rows)


QKV_TILE = 512


def qkv_kernel(act_ref, weight_ref, cos_ref, sin_ref, out_ref):
    packed = dot(act_ref[...], weight_ref[...])
    is_value = pl.program_id(0) >= 2 * D // QKV_TILE

    @pl.when(is_value)
    def _():
        out_ref[...] = packed.astype(BF16)

    @pl.when(jnp.logical_not(is_value))
    def _():
        split = packed.reshape(BLOCKS, BLK, QKV_TILE)
        spun = split * widen(cos_ref[...])[None] + turned(split) * widen(sin_ref[...])[None]
        out_ref[...] = spun.reshape(ROWS, QKV_TILE).astype(BF16)


def qkv_rows(act, weight, cosine, sine):
    return pl.pallas_call(
        qkv_kernel,
        grid=(3 * D // QKV_TILE,),
        in_specs=[
            pl.BlockSpec((ROWS, D), lambda j: (0, 0)),
            pl.BlockSpec((D, QKV_TILE), lambda j: (0, j)),
            pl.BlockSpec((BLK, LANES), lambda j: (0, 0)),
            pl.BlockSpec((BLK, LANES), lambda j: (0, 0)),
        ],
        out_specs=pl.BlockSpec((ROWS, QKV_TILE), lambda j: (0, j)),
        out_shape=jax.ShapeDtypeStruct((ROWS, 3 * D), BF16),
        compiler_params=params(40),
        cost_estimate=cost(2 * ROWS * D * 3 * D, 2 * (3 * D * D + ROWS * 4 * D)),
    )(act, weight, cosine, sine)


def head_masks(dtype):
    lane = lax.broadcasted_iota(jnp.int32, (BLK, LANES), 1)
    low = (lane < HD).astype(F32).astype(dtype)
    high = (lane >= HD).astype(F32).astype(dtype)
    return low, high


def attend_pair(query, key, value, valid):
    low, high = head_masks(BF16)
    scores = dot(query, jnp.concatenate([key * low, key * high], axis=0), 1, 1)
    parts = []
    for head in range(2):
        score = scores[:, head * BLK : (head + 1) * BLK] * SCALE
        score = jnp.where(valid, score, NEG)
        expo = jnp.exp(score - jnp.max(score, axis=-1, keepdims=True))
        parts.append(expo / jnp.sum(expo, axis=-1, keepdims=True))
    prob = jnp.concatenate(parts, axis=1).astype(BF16)
    both = jnp.concatenate([value * low, value * high], axis=0)
    return dot(prob, both).astype(BF16), prob


def block_lengths(length_ref, block, devices):
    shape = (length_ref.shape[1], BLK)
    own = lax.broadcasted_iota(jnp.int32, shape, 0) == (
        SEQ_DEV * position(devices) + block
    )
    return length_sums(length_ref, own)


def key_mask(length):
    return lax.broadcasted_iota(jnp.int32, (BLK, BLK), 1).astype(F32) < length


def attend_kernel(devices, length_ref, q_ref, k_ref, v_ref, out_ref, prob_ref):
    block = pl.program_id(0)
    lengths = block_lengths(length_ref, block % SEQ_DEV, devices)
    micro = lax.broadcasted_iota(jnp.int32, lengths.shape, 0) == block // SEQ_DEV
    valid = key_mask(jnp.sum(jnp.where(micro, lengths, 0.0), axis=0, keepdims=True))
    for pair in range(PAIRS):
        lanes = slice(pair * LANES, (pair + 1) * LANES)
        out_ref[:, lanes], prob_ref[0, pair] = attend_pair(
            q_ref[:, lanes], k_ref[:, lanes], v_ref[:, lanes], valid
        )


def attend(qkv, lengths, devices):
    return pl.pallas_call(
        functools.partial(attend_kernel, devices),
        grid=(BLOCKS,),
        in_specs=[
            pl.BlockSpec(lengths.shape, lambda b: (0, 0)),
            pl.BlockSpec((BLK, D), lambda b: (b, 0)),
            pl.BlockSpec((BLK, D), lambda b: (b, 1)),
            pl.BlockSpec((BLK, D), lambda b: (b, 2)),
        ],
        out_specs=[
            pl.BlockSpec((BLK, D), lambda b: (b, 0)),
            pl.BlockSpec((1, PAIRS, BLK, 2 * BLK), lambda b: (b, 0, 0, 0)),
        ],
        out_shape=[
            jax.ShapeDtypeStruct((ROWS, D), BF16),
            jax.ShapeDtypeStruct((BLOCKS, PAIRS, BLK, 2 * BLK), BF16),
        ],
        compiler_params=params(32),
        cost_estimate=cost(8 * ROWS * BLK * D, 2 * ROWS * 6 * D, ROWS * HEADS * BLK),
    )(lengths, qkv, qkv, qkv)


def attend_back_kernel(
    q_ref, k_ref, v_ref, grad_ref, prob_ref, cos_ref, sin_ref, out_ref
):
    for pair in range(PAIRS):
        start = pair * LANES
        lanes = slice(start, start + LANES)
        results = attend_back_pair(
            q_ref[:, lanes],
            k_ref[:, lanes],
            v_ref[:, lanes],
            grad_ref[:, lanes],
            prob_ref[0, pair],
            cos_ref[...],
            sin_ref[...],
        )
        for part, result in enumerate(results):
            out_ref[:, part * D + start : part * D + start + LANES] = result


def attend_back(qkv, grad_o, prob, cosine, sine):
    return pl.pallas_call(
        attend_back_kernel,
        grid=(BLOCKS,),
        in_specs=[
            pl.BlockSpec((BLK, D), lambda b: (b, 0)),
            pl.BlockSpec((BLK, D), lambda b: (b, 1)),
            pl.BlockSpec((BLK, D), lambda b: (b, 2)),
            pl.BlockSpec((BLK, D), lambda b: (b, 0)),
            pl.BlockSpec((1, PAIRS, BLK, 2 * BLK), lambda b: (b, 0, 0, 0)),
            pl.BlockSpec((BLK, LANES), lambda b: (0, 0)),
            pl.BlockSpec((BLK, LANES), lambda b: (0, 0)),
        ],
        out_specs=pl.BlockSpec((BLK, 3 * D), lambda b: (b, 0)),
        out_shape=jax.ShapeDtypeStruct((ROWS, 3 * D), BF16),
        compiler_params=params(32),
        cost_estimate=cost(20 * ROWS * BLK * D, 2 * ROWS * 9 * D),
    )(qkv, qkv, qkv, grad_o, prob, cosine, sine)


def middle_kernel(attn_ref, hidden_ref, weight_ref, gain_ref, mid_ref, act_ref):
    middle = hidden_ref[...].astype(F32) + dot(attn_ref[...], weight_ref[...])
    mid_ref[...] = middle
    act_ref[...] = (normed(middle)[0] * gain_ref[...]).astype(BF16)


def middle_rows(attn_o, hidden, weight, gain):
    tile = pl.BlockSpec((ROW_CHUNK, D), lambda i: (i, 0))
    return pl.pallas_call(
        middle_kernel,
        grid=(ROWS // ROW_CHUNK,),
        in_specs=[
            tile,
            tile,
            pl.BlockSpec((D, D), lambda i: (0, 0)),
            pl.BlockSpec((1, D), lambda i: (0, 0)),
        ],
        out_specs=[tile, tile],
        out_shape=[
            jax.ShapeDtypeStruct((ROWS, D), F32),
            jax.ShapeDtypeStruct((ROWS, D), BF16),
        ],
        compiler_params=params(32),
        cost_estimate=cost(2 * ROWS * D * D, 2 * D * D + 10 * ROWS * D),
    )(attn_o, hidden, weight, gain)


def ffn_kernel(
    act_ref,
    top_ref,
    mid_ref,
    in_ref,
    down_ref,
    layer_ref,
    grad_b_ref,
    grad_in_ref,
    grad_down_ref,
    total,
    act_t,
    kept_c,
    kept_gu,
):
    step = pl.program_id(0)

    @pl.when(step == 0)
    def _():
        total[...] = mid_ref[...]
        grad_b_ref[...] = jnp.zeros_like(grad_b_ref)
        act_t[...] = act_ref[...].T

    def rows_step(index, carry):
        rows = pl.ds(pl.multiple_of(index * ROW_CHUNK, ROW_CHUNK), ROW_CHUNK)
        act, top = act_ref[rows, :], top_ref[rows, :]
        gate_up = dot(act, in_ref[...])
        gelu_in, linear = gate_up[:, :FF_TILE], gate_up[:, FF_TILE:]
        grad_c = dot(top, down_ref[...], 1, 1)
        phi = 0.5 * (1.0 + lax.erf(gelu_in * ROOT_HALF))
        gelu_out = gelu_in * phi
        slope = phi + gelu_in * (jnp.exp(-0.5 * gelu_in * gelu_in) * INV_ROOT_TWO_PI)
        act_c = (gelu_out * linear).astype(BF16)
        kept_c[rows, :] = act_c
        kept_gu[rows, :FF_TILE] = (grad_c * linear * slope).astype(BF16)
        kept_gu[rows, FF_TILE:] = (grad_c * gelu_out).astype(BF16)
        total[rows, :] += dot(act_c, down_ref[...])
        grad_b_ref[rows, :] += dot(kept_gu[rows, :], in_ref[...], 1, 1)
        return carry

    lax.fori_loop(0, ROWS // ROW_CHUNK, rows_step, 0)
    grad_in_ref[...] = dot(act_t[...], kept_gu[...]).astype(BF16)
    grad_down_ref[...] = dot(kept_c[...], top_ref[...], 0, 0).astype(BF16)

    @pl.when(step == pl.num_programs(0) - 1)
    def _():
        layer_ref[...] = total[...].astype(BF16)


def ffn(act, top, middle, full_in, full_down):
    whole = pl.BlockSpec((ROWS, D), lambda j: (0, 0))
    tall = pl.BlockSpec((D, 2 * FF_TILE), lambda j: (0, j))
    wide = pl.BlockSpec((FF_TILE, D), lambda j: (j, 0))
    return pl.pallas_call(
        ffn_kernel,
        grid=(full_down.shape[0] // FF_TILE,),
        in_specs=[
            whole,
            whole,
            whole,
            tall,
            wide,
        ],
        out_specs=[whole, whole, tall, wide],
        out_shape=[
            jax.ShapeDtypeStruct((ROWS, D), BF16),
            jax.ShapeDtypeStruct((ROWS, D), F32),
            jax.ShapeDtypeStruct(full_in.shape, BF16),
            jax.ShapeDtypeStruct(full_down.shape, BF16),
        ],
        scratch_shapes=[
            pltpu.VMEM((ROWS, D), F32),
            pltpu.VMEM((D, ROWS), BF16),
            pltpu.VMEM((ROWS, FF_TILE), BF16),
            pltpu.VMEM((ROWS, 2 * FF_TILE), BF16),
        ],
        compiler_params=params(60),
        cost_estimate=cost(18 * ROWS * D * FF, 12 * D * FF, 2 * ROWS * FF),
    )(act, top, middle, full_in, full_down)


def branch_kernel(
    order_ref,
    grad_b_ref,
    mid_ref,
    top_ref,
    attn_ref,
    weight_ref,
    gain_ref,
    grad_mid_ref,
    grad_o_ref,
    grad_w_ref,
    grad_gain_ref,
    total,
):
    step = pl.program_id(0)

    @pl.when(step == 0)
    def _():
        total[...] = jnp.zeros_like(total)
        grad_gain_ref[...] = jnp.zeros_like(grad_gain_ref)

    grad_b = grad_b_ref[...]
    normal, inverse = normed(mid_ref[...])
    grad_gain_ref[...] += jnp.sum(grad_b * normal, axis=0, keepdims=True)
    grad_mid = top_ref[...].astype(F32) + norm_back(
        grad_b * gain_ref[...], normal, inverse
    )
    grad_mid_ref[...] = grad_mid
    grad_r = grad_mid.astype(BF16)
    grad_o_ref[...] = dot(grad_r, weight_ref[...], 1, 1).astype(BF16)
    total[...] += dot(attn_ref[...], grad_r, 0, 0)

    @pl.when(step == ROWS // ROW_CHUNK - 1)
    def _():
        grad_w_ref[...] = total[...].astype(BF16)


def branch_back(order, grad_b, middle, top, attn_o, weight, gain):
    tile = pl.BlockSpec((ROW_CHUNK, D), lambda i: (i, 0))
    square = pl.BlockSpec((D, D), lambda i: (0, 0))
    line = pl.BlockSpec((1, D), lambda i: (0, 0))
    return pl.pallas_call(
        branch_kernel,
        grid=(ROWS // ROW_CHUNK,),
        in_specs=[
            pl.BlockSpec(memory_space=pl.ANY),
            *[tile] * 4,
            square,
            line,
        ],
        out_specs=[tile, tile, square, line],
        out_shape=[
            jax.ShapeDtypeStruct((ROWS, D), F32),
            jax.ShapeDtypeStruct((ROWS, D), BF16),
            jax.ShapeDtypeStruct((D, D), BF16),
            jax.ShapeDtypeStruct((1, D), F32),
        ],
        scratch_shapes=[pltpu.VMEM((D, D), F32)],
        compiler_params=params(40),
        cost_estimate=cost(4 * ROWS * D * D, 4 * D * D + 18 * ROWS * D),
    )(order, grad_b, middle, top, attn_o, weight, gain)


def input_kernel(
    grad_qkv_ref,
    weight_ref,
    hidden_ref,
    grad_mid_ref,
    gain_ref,
    other_ref,
    out_ref,
    gains_ref,
    grad_gain,
):
    @pl.when(pl.program_id(0) == 0)
    def _():
        grad_gain[...] = jnp.zeros_like(grad_gain)

    grad_a = dot(grad_qkv_ref[...], weight_ref[...], 1, 1)
    normal, inverse = normed(hidden_ref[...].astype(F32))
    grad_gain[...] += jnp.sum(grad_a * normal, axis=0, keepdims=True)
    out_ref[...] = (
        grad_mid_ref[...] + norm_back(grad_a * gain_ref[...], normal, inverse)
    ).astype(BF16)

    @pl.when(pl.program_id(0) == ROWS // ROW_CHUNK - 1)
    def _():
        width = D // SHARDS
        for shard in range(SHARDS):
            lanes = slice(shard * width, (shard + 1) * width)
            for part, values in enumerate((grad_gain, other_ref)):
                gains_ref[shard, :, part * width : (part + 1) * width] = jnp.broadcast_to(
                    values[:, lanes], (GAIN_ROWS, width)
                )


def input_back(grad_qkv, weight, hidden, grad_mid, gain, other):
    tile = pl.BlockSpec((ROW_CHUNK, D), lambda i: (i, 0))
    line = pl.BlockSpec((1, D), lambda i: (0, 0))
    return pl.pallas_call(
        input_kernel,
        grid=(ROWS // ROW_CHUNK,),
        in_specs=[
            pl.BlockSpec((ROW_CHUNK, 3 * D), lambda i: (i, 0)),
            pl.BlockSpec((D, 3 * D), lambda i: (0, 0)),
            tile,
            tile,
            line,
            line,
        ],
        out_specs=[
            tile,
            pl.BlockSpec((SHARDS, GAIN_ROWS, 2 * D // SHARDS), lambda i: (0, 0, 0)),
        ],
        out_shape=[
            jax.ShapeDtypeStruct((ROWS, D), BF16),
            jax.ShapeDtypeStruct((SHARDS, GAIN_ROWS, 2 * D // SHARDS), F32),
        ],
        scratch_shapes=[pltpu.VMEM((1, D), F32)],
        compiler_params=params(40),
        cost_estimate=cost(6 * ROWS * D * D, 6 * D * D + 14 * ROWS * D),
    )(grad_qkv, weight, hidden, grad_mid, gain, other)


def qkv_grad_kernel(act_ref, grad_ref, out_ref, act_t):
    @pl.when(pl.program_id(0) == 0)
    def _():
        act_t[...] = act_ref[...].T

    out_ref[...] = dot(act_t[...], grad_ref[...]).astype(BF16)


def qkv_grad(act, grad_qkv):
    return pl.pallas_call(
        qkv_grad_kernel,
        grid=(3 * D // QKV_TILE,),
        in_specs=[
            pl.BlockSpec((ROWS, D), lambda j: (0, 0)),
            pl.BlockSpec((ROWS, QKV_TILE), lambda j: (0, j)),
        ],
        out_specs=pl.BlockSpec((D, QKV_TILE), lambda j: (0, j)),
        out_shape=jax.ShapeDtypeStruct((D, 3 * D), BF16),
        scratch_shapes=[pltpu.VMEM((D, ROWS), BF16)],
        compiler_params=params(32),
        cost_estimate=cost(6 * ROWS * D * D, 2 * (7 * D * D)),
    )(act, grad_qkv)


MESH = pl.DeviceIdType.MESH
EARLY_CHUNKS = (
    (0, 0, 512),
    (0, 512, 512),
    *[(1, i * 768, 768) for i in range(7)],
    (2, 0, 1024),
)
LATE_CHUNKS = (
    (3, 0, 768),
    (3, 768, 768),
    (3, 1536, 768),
    (3, 2304, 512),
    (4, 0, 256),
    (3, 2816, 256),
)
REDUCE_CHUNKS = EARLY_CHUNKS + LATE_CHUNKS
HOP_CORE, HOP_X, HOP_Y, HOP_XY, HOP_YX, HOP_IN, HOP_MID, HOP_OUT = range(8)


def place():
    rep, grp = lax.axis_index("rep"), lax.axis_index("grp")
    core, x, y = grp % 2, grp // 2 % 2, grp // 4
    return rep, grp, core, x, y, grp + 1 - 2 * core, grp + 2 - 4 * x, grp + 4 - 8 * y


def mesh_id(index):
    return (index // SHARDS, lax.rem(index, SHARDS))


def greet_all(devices):
    device = position(devices)
    barrier = pltpu.get_barrier_semaphore()

    def greet(step, carry):
        to = mesh_id(lax.rem(device + step, devices))
        pl.semaphore_signal(barrier, device_id=to, device_id_type=MESH)
        return carry

    lax.fori_loop(1, devices, greet, 0)
    pl.semaphore_wait(barrier, devices - 1)


def row_exchange(send, land, local_sem, send_sem, recv_sem, devices):
    device = position(devices)

    def copy(step, slot):
        to = lax.rem(device + step, devices)
        return pltpu.make_async_remote_copy(
            src_ref=send(to),
            dst_ref=land(slot),
            send_sem=send_sem.at[step],
            recv_sem=recv_sem.at[step],
            device_id=mesh_id(to),
            device_id_type=MESH,
        )

    def keep():
        return pltpu.make_async_copy(send(device), land(device), local_sem)

    def start():
        def one(step, carry):
            copy(step, device).start()
            return carry

        keep().start()
        lax.fori_loop(1, devices, one, 0)

    def finish():
        def one(step, carry):
            copy(step, lax.rem(device + devices - step, devices)).wait_recv()
            copy(step, device).wait_send()
            return carry

        lax.fori_loop(1, devices, one, 0)
        keep().wait()

    return start, finish


def reduction(table, tensors, outs, refs):
    chunks = len(table)
    sums, from_core, from_near, from_cross, from_far = (
        refs[i * chunks : (i + 1) * chunks] for i in range(5)
    )
    load_sem, send_sem, recv_sem, store_sem = refs[5 * chunks :]
    rep, grp, core, x, y, by_core, by_x, by_y = place()
    is_middle = (rep == 1) | (rep == 2)
    inward, outward, across = 1 + rep // 2, 3 * (rep // 2), 3 - rep

    def hop(chunk, which):
        tensor, start, width = table[chunk]
        half = width // 2
        left, right, columns = pl.ds(0, half), pl.ds(half, half), pl.ds(start, width)
        total, far = sums[chunk], from_far[chunk]
        near, cross = from_near[chunk], from_cross[chunk]
        if which == HOP_CORE:
            source, target = tensors[tensor].at[:, :, 1 - core, :, columns], from_core[chunk]
        elif which == HOP_X:
            source, target = total.at[:, 1 - x, :, left], near.at[0]
        elif which == HOP_Y:
            source, target = total.at[1 - y, :, :, right], near.at[1]
        elif which == HOP_XY:
            source, target = total.at[1 - y, x, :, left], cross.at[0]
        elif which == HOP_YX:
            source, target = total.at[y, 1 - x, :, right], cross.at[1]
        elif which == HOP_IN:
            source, target = total.at[y, x], far.at[0]
        elif which == HOP_MID:
            source, target = total.at[y, x], far.at[1]
        else:
            source, target = far.at[0], outs[tensor].at[:, columns]
        to_rep = (rep, rep, rep, rep, rep, inward, across, outward)[which]
        to_grp = (by_core, by_x, by_y, by_y, by_x, grp, grp, grp)[which]
        return pltpu.make_async_remote_copy(
            src_ref=source,
            dst_ref=target,
            send_sem=send_sem.at[chunk, which],
            recv_sem=recv_sem.at[chunk, which],
            device_id=(to_rep, to_grp),
            device_id_type=MESH,
        )

    def load(chunk):
        tensor, start, width = table[chunk]
        return pltpu.make_async_copy(
            tensors[tensor].at[:, :, core, :, pl.ds(start, width)],
            sums[chunk],
            load_sem.at[chunk],
        )

    def store(chunk):
        tensor, start, width = table[chunk]
        return pltpu.make_async_copy(
            from_far[chunk].at[0],
            outs[tensor].at[:, pl.ds(start, width)],
            store_sem.at[chunk],
        )

    def add(one, other):
        return (one.astype(F32) + other.astype(F32)).astype(one.dtype)

    def after_core(chunk):
        load(chunk).wait()
        hop(chunk, HOP_CORE).wait_recv()
        total = sums[chunk]

        def plane(index, carry):
            row, column = index // 2, index % 2
            total[row, column] = add(total[row, column], from_core[chunk][row, column])
            return carry

        lax.fori_loop(0, 4, plane, 0)
        hop(chunk, HOP_X).start()
        hop(chunk, HOP_Y).start()

    def after_near(chunk):
        half = table[chunk][2] // 2
        hop(chunk, HOP_X).wait_recv()
        hop(chunk, HOP_Y).wait_recv()
        total, near = sums[chunk], from_near[chunk]

        def plane(index, carry):
            total[index, x, :, :half] = add(total[index, x, :, :half], near[0, index])
            total[y, index, :, half:] = add(total[y, index, :, half:], near[1, index])
            return carry

        lax.fori_loop(0, 2, plane, 0)
        hop(chunk, HOP_XY).start()
        hop(chunk, HOP_YX).start()

    def after_cross(chunk):
        half = table[chunk][2] // 2
        hop(chunk, HOP_XY).wait_recv()
        hop(chunk, HOP_YX).wait_recv()
        total, cross = sums[chunk], from_cross[chunk]
        total[y, x, :, :half] = add(total[y, x, :, :half], cross[0])
        total[y, x, :, half:] = add(total[y, x, :, half:], cross[1])

        @pl.when(jnp.logical_not(is_middle))
        def _():
            hop(chunk, HOP_IN).start()

    def after_in(chunk):
        @pl.when(is_middle)
        def _():
            hop(chunk, HOP_IN).wait_recv()
            total = sums[chunk]
            total[y, x] = add(total[y, x], from_far[chunk][0])
            hop(chunk, HOP_MID).start()

    def after_middle(chunk):
        @pl.when(is_middle)
        def _():
            hop(chunk, HOP_MID).wait_recv()
            far = from_far[chunk]
            far[0] = add(sums[chunk][y, x], far[1])
            hop(chunk, HOP_OUT).start()
            store(chunk).start()

    def start(some):
        for chunk in some:
            load(chunk).start()
            hop(chunk, HOP_CORE).start()

    stages = (after_core, after_near, after_cross, after_in, after_middle)

    def one_step(step):
        for late, stage in enumerate(stages):
            if 0 <= step - late < chunks:
                stage(step - late)

    steps = [functools.partial(one_step, i) for i in range(chunks + len(stages) - 1)]

    def finish():
        for chunk in range(chunks):
            for which in (HOP_CORE, HOP_X, HOP_Y, HOP_XY, HOP_YX):
                hop(chunk, which).wait_send()

        @pl.when(is_middle)
        def _():
            for chunk in range(chunks):
                hop(chunk, HOP_MID).wait_send()
                hop(chunk, HOP_OUT).wait_send()
                store(chunk).wait()

        @pl.when(jnp.logical_not(is_middle))
        def _():
            for chunk in range(chunks):
                hop(chunk, HOP_IN).wait_send()
                hop(chunk, HOP_OUT).wait_recv()

    return start, steps, finish


def reduction_scratch(table, split):
    kinds = [(split[t].dtype, split[t].shape[3], width) for t, _, width in table]
    dma = pltpu.SemaphoreType.DMA
    return [
        *[pltpu.VMEM((2, 2, r, w), t) for t, r, w in kinds],
        *[pltpu.VMEM((2, 2, r, w), t) for t, r, w in kinds],
        *[pltpu.VMEM((2, 2, r, w // 2), t) for t, r, w in kinds],
        *[pltpu.VMEM((2, r, w // 2), t) for t, r, w in kinds],
        *[pltpu.VMEM((2, r, w), t) for t, r, w in kinds],
        dma((len(table),)),
        dma((len(table), 8)),
        dma((len(table), 8)),
        dma((len(table),)),
    ]


def split_shards(parts):
    return [part.reshape(2, 2, 2, -1, part.shape[-1]) for part in parts]


def attend_back_pair(query, key, value, grad, prob, cosine, sine):
    low, high = head_masks(BF16)
    is_low = lax.broadcasted_iota(jnp.int32, (BLK, LANES), 1) < HD
    grad_v = dot(prob, grad, 0, 0)
    grad_v = jnp.where(is_low, grad_v[:BLK], grad_v[BLK:])
    grad_p = dot(grad, jnp.concatenate([value * low, value * high], axis=0), 1, 1)
    parts = []
    for head in range(2):
        keys = slice(head * BLK, (head + 1) * BLK)
        weight, slope = prob[:, keys].astype(F32), grad_p[:, keys]
        inner = jnp.sum(weight * slope, axis=-1, keepdims=True)
        parts.append(weight * (slope - inner))
    grad_s = jnp.concatenate(parts, axis=1).astype(BF16)
    both = jnp.concatenate([key * low, key * high], axis=0)
    grad_q = dot(grad_s, both) * SCALE
    grad_k = dot(grad_s, query, 0, 0)
    grad_k = jnp.where(is_low, grad_k[:BLK], grad_k[BLK:]) * SCALE
    return (
        (grad_q * cosine - turned(grad_q) * sine).astype(BF16),
        (grad_k * cosine - turned(grad_k) * sine).astype(BF16),
        grad_v.astype(BF16),
    )


FEATURES = D // SHARDS
SOME_ROWS = 256
ROW_PIECES = ROWS // SOME_ROWS


def interleave(steps, pieces, ahead):
    for piece in pieces[:ahead]:
        piece()
    pieces = pieces[ahead:]
    done = 0
    for index, step in enumerate(steps):
        step()
        upto = -(-len(pieces) * (index + 1) // len(steps))
        for piece in pieces[done:upto]:
            piece()
        done = upto


def return_kernel(devices, micros, *refs):
    groups = MICRO // micros
    early = refs[:3]
    send, lengths_ref, qkv_ref, prob_ref, grad_o_ref, act_ref, hidden_ref = refs[3:10]
    mid_ref, weight_ref, gain_ref, other_ref, cos_ref, sin_ref = refs[10:16]
    outs, layer_land, grad_land, grad_w_ref, gains_ref = refs[16:21], *refs[21:25]
    wide, grads, block_prob, block_grad, act_part, w_part = refs[25:31]
    row_hidden, row_mid, kept, packed, grad_gain, gain_parts = refs[31:37]
    wide_sem, block_sem, act_sem, w_sem, row_sem, gain_sem = refs[37:43]
    layer_sems, grad_sems, refs = refs[43:46], refs[46:49], refs[49:]
    tensors = (*early, grad_w_ref, gains_ref)
    start, steps, finish = reduction(REDUCE_CHUNKS, tensors, outs, refs)
    start_layer, finish_layer = row_exchange(
        lambda to: send.at[to], lambda slot: layer_land.at[slot], *layer_sems, devices
    )
    exchanges = [
        row_exchange(
            lambda to, group=group: packed.at[group, to],
            lambda slot, group=group: grad_land.at[slot, group],
            *[sem.at[group] for sem in grad_sems],
            devices,
        )
        for group in range(groups)
    ]
    copy = pltpu.make_async_copy

    def block_loads(block):
        slot = block % 2
        rows = pl.ds(block * BLK, BLK)
        return (
            copy(prob_ref.at[block], block_prob.at[slot], block_sem.at[slot, 0]),
            copy(grad_o_ref.at[rows], block_grad.at[slot], block_sem.at[slot, 1]),
        )

    def act_load(part):
        columns = pl.ds(part * FEATURES, FEATURES)
        return copy(act_ref.at[:, columns], act_part.at[part % 2], act_sem.at[part % 2])

    def w_store(part):
        target = grad_w_ref.at[part // 4, part // 2 % 2, part % 2]
        return copy(w_part, target, w_sem)

    def row_loads(part):
        rows = pl.ds(part * SOME_ROWS, SOME_ROWS)
        return (
            copy(hidden_ref.at[rows], row_hidden, row_sem.at[0]),
            copy(mid_ref.at[rows], row_mid, row_sem.at[1]),
        )

    load_qkv = copy(qkv_ref, wide, wide_sem.at[0])
    load_weight = copy(weight_ref, wide, wide_sem.at[1])

    def attend_piece(block):
        if block == 0:
            load_qkv.wait()
        for load in block_loads(block):
            load.wait()
        if block + 1 < BLOCKS:
            for load in block_loads(block + 1):
                load.start()
        slot = block % 2
        rows = slice(block * BLK, (block + 1) * BLK)

        def two(index, carry):
            for inner in range(4):
                pair = index * 4 + inner
                base = pl.multiple_of(pair * LANES, LANES)
                columns = [
                    pl.ds(pl.multiple_of(part * D + base, LANES), LANES) for part in range(3)
                ]
                results = attend_back_pair(
                    *[wide[rows, c] for c in columns],
                    block_grad[slot, :, pl.ds(base, LANES)],
                    block_prob[slot, pair],
                    cos_ref[...],
                    sin_ref[...],
                )
                for c, result in zip(columns, results):
                    grads[rows, c] = result
            return carry

        lax.fori_loop(0, PAIRS // 4, two, 0)
        if block == BLOCKS - 1:
            load_weight.start()
            act_load(0).start()

    def weight_piece(part):
        act_load(part).wait()
        if part + 1 < SHARDS:
            act_load(part + 1).start()
        act_t = act_part[part % 2].T
        if part:
            w_store(part - 1).wait()
        for third in range(3):
            columns = slice(third * D, (third + 1) * D)
            w_part[:, columns] = dot(act_t, grads[:, columns]).astype(BF16)
        w_store(part).start()
        if part == SHARDS - 1:
            w_store(part).wait()
            start([i for i, c in enumerate(REDUCE_CHUNKS) if c[0] == 3])
            for load in row_loads(0):
                load.start()

    def row_piece(part):
        if part == 0:
            load_weight.wait()
            grad_gain[...] = jnp.zeros_like(grad_gain)
        for load in row_loads(part):
            load.wait()
        rows = slice(part * SOME_ROWS, (part + 1) * SOME_ROWS)
        grad_a = dot(grads[rows, :], wide[...], 1, 1)
        normal, inverse = normed(row_hidden[...].astype(F32))
        grad_gain[...] += jnp.sum(grad_a * normal, axis=0, keepdims=True)
        each = ROW_PIECES // groups
        inner = slice(part % each * SOME_ROWS, (part % each + 1) * SOME_ROWS)
        kept[inner] = (
            row_mid[...] + norm_back(grad_a * gain_ref[...], normal, inverse)
        ).astype(BF16)
        if part + 1 < ROW_PIECES:
            for load in row_loads(part + 1):
                load.start()
        if part % each == each - 1:
            group = part // each
            pick = held_rows(lengths_ref, group, micros, devices)
            packed[group] = (
                dot(pick, kept[...], 0, 0).astype(BF16).reshape(packed.shape[1:])
            )
            exchanges[group][0]()

    def gain_piece():
        width = D // SHARDS
        for shard in range(SHARDS):
            columns = slice(shard * width, (shard + 1) * width)
            for part, values in enumerate((grad_gain, other_ref)):
                gain_parts[shard // 4, shard // 2 % 2, shard % 2, :, part * width : (part + 1) * width] = (
                    jnp.broadcast_to(values[:, columns], (GAIN_ROWS, width))
                )
        keep = copy(gain_parts, gains_ref, gain_sem)
        keep.start()
        keep.wait()
        start([i for i, c in enumerate(REDUCE_CHUNKS) if c[0] == 4])

    greet_all(devices)
    load_qkv.start()
    for load in block_loads(0):
        load.start()
    start(range(len(EARLY_CHUNKS)))
    start_layer()
    pieces = [
        *[functools.partial(attend_piece, i) for i in range(BLOCKS)],
        *[functools.partial(weight_piece, i) for i in range(SHARDS)],
        *[functools.partial(row_piece, i) for i in range(ROW_PIECES)],
        gain_piece,
    ]
    count = len(EARLY_CHUNKS)
    interleave(steps[:count], pieces, 2)
    for step in steps[count:]:
        step()
    finish()
    finish_layer()
    for exchange in exchanges:
        exchange[1]()


def return_all(
    parts,
    send,
    lengths,
    qkv,
    prob,
    grad_o,
    act,
    hidden,
    grad_mid,
    weight,
    gain,
    other,
    tables,
    devices,
    micros,
):
    early = split_shards(parts)
    groups = MICRO // micros
    rows = D // SHARDS
    split = [
        *early,
        jax.ShapeDtypeStruct((2, 2, 2, rows, 3 * D), BF16),
        jax.ShapeDtypeStruct((2, 2, 2, GAIN_ROWS, 2 * rows), F32),
    ]
    anywhere = pl.BlockSpec(memory_space=pl.ANY)
    inside = pl.BlockSpec(memory_space=pltpu.VMEM)
    dma = pltpu.SemaphoreType.DMA
    *owned, layer_back, grad_back, _, _ = pl.pallas_call(
        functools.partial(return_kernel, devices, micros),
        in_specs=[
            *[anywhere] * 4,
            inside,
            *[anywhere] * 7,
            *[inside] * 4,
        ],
        out_specs=[anywhere] * 9,
        out_shape=[
            *[jax.ShapeDtypeStruct(v.shape[3:], v.dtype) for v in split],
            jax.ShapeDtypeStruct(send.shape, send.dtype),
            jax.ShapeDtypeStruct(send.shape, send.dtype),
            *split[3:],
        ],
        scratch_shapes=[
            pltpu.VMEM((ROWS, 3 * D), BF16),
            pltpu.VMEM((ROWS, 3 * D), BF16),
            pltpu.VMEM((2, PAIRS, BLK, 2 * BLK), BF16),
            pltpu.VMEM((2, BLK, D), BF16),
            pltpu.VMEM((2, ROWS, FEATURES), BF16),
            pltpu.VMEM((FEATURES, 3 * D), BF16),
            pltpu.VMEM((SOME_ROWS, D), BF16),
            pltpu.VMEM((SOME_ROWS, D), F32),
            pltpu.VMEM((ROWS // groups, D), BF16),
            pltpu.VMEM((groups, devices, CHUNK_ROWS, D), BF16),
            pltpu.VMEM((1, D), F32),
            pltpu.VMEM((2, 2, 2, GAIN_ROWS, 2 * rows), F32),
            dma((2,)),
            dma((2, 2)),
            dma((2,)),
            dma,
            dma((2,)),
            dma,
            dma,
            dma((devices,)),
            dma((devices,)),
            dma((groups,)),
            dma((groups, devices)),
            dma((groups, devices)),
            *reduction_scratch(REDUCE_CHUNKS, split),
        ],
        compiler_params=pltpu.CompilerParams(
            vmem_limit_bytes=63 * MIB, collective_id=1, has_side_effects=True
        ),
        cost_estimate=cost(16 * ROWS * D * D, 600 * MIB),
    )(
        *early,
        send,
        lengths,
        qkv,
        prob,
        grad_o,
        act,
        hidden,
        grad_mid,
        weight,
        gain,
        other,
        *tables,
    )
    return (*owned, layer_back, grad_back)


WAY_X, WAY_Y, WAY_CORE, WAY_CORE_X, WAY_CORE_Y = range(5)
WAY_XY, WAY_YX, WAY_CORE_XY, WAY_CORE_YX = range(5, 9)


GATHER_CHUNKS = (
    (0, 0, 1536),
    (0, 1536, 1536),
    (1, 0, 1024),
    (2, 0, 768),
    (3, 0, 512),
    (3, 512, 512),
    *[(2, i * 768, 768) for i in range(1, 7)],
)
OUT_CHUNK = 2
FF_CHUNKS = (3, 6, 7, 8, 9, 10, 11)
AHEAD = 3


def gathering(table, shards, fulls, keep_sem, send_sem, recv_sem):
    rep, grp, core, x, y, by_core, by_x, by_y = place()
    by_xy = by_x + by_y - grp
    other = by_core - grp

    def view(chunk, slot, half=None):
        tensor, start, width = table[chunk]
        rows = shards[tensor].shape[0]
        if half is not None:
            start, width = start + half * (width // 2), width // 2
        first = pl.multiple_of(slot * rows, rows)
        return fulls[tensor].at[pl.ds(first, rows), pl.ds(start, width)]

    def own(chunk):
        tensor, start, width = table[chunk]
        return shards[tensor].at[:, pl.ds(start, width)]

    def way(chunk, which):
        slot, landing, half, to = {
            WAY_X: (grp, by_x, None, by_x),
            WAY_Y: (grp, by_y, None, by_y),
            WAY_CORE: (grp, by_core, None, by_core),
            WAY_CORE_X: (by_x, by_x + other, None, by_core),
            WAY_CORE_Y: (by_y, by_y + other, None, by_core),
            WAY_XY: (by_x, by_xy, 0, by_y),
            WAY_YX: (by_y, by_xy, 1, by_x),
            WAY_CORE_XY: (by_xy, by_xy + other, 0, by_core),
            WAY_CORE_YX: (by_xy, by_xy + other, 1, by_core),
        }[which]
        from_own = which in (WAY_X, WAY_Y, WAY_CORE)

        def copy(source, target):
            return pltpu.make_async_remote_copy(
                src_ref=source,
                dst_ref=target,
                send_sem=send_sem.at[chunk, which],
                recv_sem=recv_sem.at[chunk, which],
                device_id=(rep, to),
                device_id_type=MESH,
            )

        source = own(chunk) if from_own else view(chunk, slot, half)
        here = view(chunk, landing, half)
        return (
            lambda: copy(source, view(chunk, slot, half)).start(),
            lambda: copy(here, here).wait_recv(),
            lambda: copy(source, view(chunk, slot, half)).wait_send(),
        )

    def keep(chunk):
        return pltpu.make_async_copy(own(chunk), view(chunk, grp), keep_sem.at[chunk])

    def start(chunk, *ways):
        for which in ways:
            way(chunk, which)[0]()

    def arrive(chunk, *ways):
        for which in ways:
            way(chunk, which)[1]()

    def first(chunk):
        start(chunk, WAY_X, WAY_Y, WAY_CORE)
        keep(chunk).start()

    def forward(chunk):
        arrive(chunk, WAY_X)
        start(chunk, WAY_XY, WAY_CORE_X)
        arrive(chunk, WAY_Y)
        start(chunk, WAY_YX, WAY_CORE_Y)

    def last(chunk):
        arrive(chunk, WAY_XY)
        start(chunk, WAY_CORE_XY)
        arrive(chunk, WAY_YX)
        start(chunk, WAY_CORE_YX)

    def complete(chunk):
        keep(chunk).wait()
        arrive(chunk, WAY_CORE, WAY_CORE_X, WAY_CORE_Y, WAY_CORE_XY, WAY_CORE_YX)

    def sent(chunk):
        for which in range(9):
            way(chunk, which)[2]()

    return first, forward, last, complete, sent


def forward_kernel(devices, micros, *refs):
    groups = MICRO // micros
    lengths_ref, gain_shard, cos_ref, sin_ref, token_send, top_send = refs[:6]
    w_qkv_ref, w_out_ref, w_in_ref, w_down_ref = refs[6:10]
    gain_rows, gain_grad, hidden_out, act_out, qkv_out, prob_out = refs[10:16]
    attn_out, mid_out, layer_out, grad_mid_out, grad_in_out, grad_down_out = refs[16:22]
    weight_out, grad_o_out, grad_out_out, refs = *refs[22:25], refs[25:]
    weight, full_out, full_in, full_down, token_land, top_land, gain_land = refs[:7]
    picks, act_b, act_t, top, total, grad_b = refs[7:13]
    s_hidden, s_act, s_qkv, s_prob, s_attn, s_mid, s_in, s_down = refs[13:21]
    raw_in, own_in = refs[21:23]
    store_sem, gain_sem, gain_send, gain_recv = refs[23:27]
    row_sems, refs = refs[27:30], refs[30:]
    shards = (w_qkv_ref, w_out_ref, own_in, w_down_ref)
    fulls = (weight, full_out, full_in, full_down)
    first, forward, last, complete, sent = gathering(GATHER_CHUNKS, shards, fulls, *refs)
    rep, grp = lax.axis_index("rep"), lax.axis_index("grp")
    chunks = len(GATHER_CHUNKS)
    slots = devices * CHUNK_ROWS

    def exchange(send, land, group, index):
        return row_exchange(
            lambda to: send.at[to, group],
            lambda slot: land.at[slot, group],
            *[sem.at[index] for sem in row_sems],
            devices,
        )

    token_swaps = [exchange(token_send, token_land, g, g) for g in range(groups)]
    top_swaps = [exchange(top_send, top_land, g, groups + g) for g in range(groups)]

    def gain_copy(step, slot):
        return pltpu.make_async_remote_copy(
            src_ref=gain_shard,
            dst_ref=gain_land.at[slot],
            send_sem=gain_send.at[step],
            recv_sem=gain_recv.at[step],
            device_id=(rep, lax.rem(grp + step, SHARDS)),
            device_id_type=MESH,
        )

    pending = {}

    def free(name):
        if name in pending:
            pending.pop(name).wait()

    def put(name, source, target):
        index = ("hidden", "act", "qkv", "prob", "attn", "mid", "in", "down", "late", "layer", "far", "o", "w")
        copy = pltpu.make_async_copy(source, target, store_sem.at[index.index(name)])
        copy.start()
        pending[name] = copy

    def tick(step):
        if step < chunks:
            forward(step)
            if step + AHEAD < chunks:
                first(step + AHEAD)
        if 0 < step <= chunks:
            last(step - 1)

    def gain_row(part):
        table = gain_land[...].astype(F32)
        return jnp.concatenate([table[s, part : part + 1] for s in range(SHARDS)], axis=1)

    def micro_rows(micro):
        return slice(micro * CAP, (micro + 1) * CAP)

    def qkv_piece(micro):
        group, rows = micro // micros, micro_rows(micro)
        for name in ("hidden", "act", "qkv"):
            free(name)
        values = dot(picks[rows, :], token_land[:, group].reshape(slots, D))
        s_hidden[...] = values.astype(BF16)
        act = (normed(values)[0] * gain_rows[0:1, :]).astype(BF16)
        s_act[...] = act
        for step in range(3 * D // QKV_TILE):
            lanes = slice(step * QKV_TILE, (step + 1) * QKV_TILE)
            packed = dot(act, weight[:, lanes])
            if step < 2 * D // QKV_TILE:
                split = packed.reshape(CAP // BLK, BLK, QKV_TILE)
                split = (
                    split * widen(cos_ref[...])[None]
                    + turned(split) * widen(sin_ref[...])[None]
                )
                packed = split.reshape(CAP, QKV_TILE)
            s_qkv[:, lanes] = packed.astype(BF16)
        put("hidden", s_hidden, hidden_out.at[rows])
        put("act", s_act, act_out.at[rows])
        put("qkv", s_qkv, qkv_out.at[rows])

    def attend_piece(micro):
        free("prob")
        free("attn")

        def one(block, carry):
            rows = pl.ds(pl.multiple_of(block * BLK, BLK), BLK)
            lengths = block_lengths(lengths_ref, block, devices)
            valid = key_mask(lengths[micro : micro + 1])
            for pair in range(PAIRS):
                columns = [
                    slice(part * D + pair * LANES, part * D + (pair + 1) * LANES)
                    for part in range(3)
                ]
                context, prob = attend_pair(*[s_qkv[rows, c] for c in columns], valid)
                s_attn[rows, columns[0]] = context
                s_prob[block, pair] = prob
            return carry

        lax.fori_loop(0, SEQ_DEV, one, 0)

    def middle_piece(micro):
        rows = micro_rows(micro)
        free("mid")
        middle = s_hidden[...].astype(F32) + dot(s_attn[...], full_out[...])
        s_mid[...] = middle
        total[rows, :] = middle
        act_b[rows, :] = (normed(middle)[0] * gain_rows[1:2, :]).astype(BF16)
        put("prob", s_prob, prob_out.at[pl.ds(micro * SEQ_DEV, SEQ_DEV)])
        put("attn", s_attn, attn_out.at[rows])
        put("mid", s_mid, mid_out.at[rows])

    def top_piece(micro):
        group, rows = micro // micros, micro_rows(micro)
        values = dot(picks[rows, :], top_land[:, group].reshape(slots, D))
        top[rows, :] = values.astype(BF16)

    def ff_views(step):
        return (
            slice(step * 2 * FF_TILE, (step + 1) * 2 * FF_TILE),
            slice(step * FF_TILE, (step + 1) * FF_TILE),
            step % 2 * 3 * FF_TILE,
        )

    def ff_forward(step):
        both, hidden, base = ff_views(step)
        gate_up = dot(act_b[...], full_in[:, both])
        gelu_in, linear = gate_up[:, :FF_TILE], gate_up[:, FF_TILE:]
        phi = 0.5 * (1.0 + lax.erf(gelu_in * ROOT_HALF))
        gelu_out = gelu_in * phi
        slope = phi + gelu_in * (jnp.exp(-0.5 * gelu_in * gelu_in) * INV_ROOT_TWO_PI)
        act_c = (gelu_out * linear).astype(BF16)
        weight[:, base : base + FF_TILE] = (linear * slope).astype(BF16)
        weight[:, base + FF_TILE : base + 2 * FF_TILE] = gelu_out.astype(BF16)
        weight[:, base + 2 * FF_TILE : base + 3 * FF_TILE] = act_c
        total[...] += dot(act_c, full_down[hidden, :])

    def ff_backward(step):
        both, hidden, base = ff_views(step)
        kept = slice(6 * FF_TILE, 8 * FF_TILE)
        grad_c = dot(top[...], full_down[hidden, :], 1, 1)
        for part in range(2):
            factor = weight[:, base + part * FF_TILE : base + (part + 1) * FF_TILE]
            start = (6 + part) * FF_TILE
            weight[:, start : start + FF_TILE] = (grad_c * factor.astype(F32)).astype(BF16)
        grad_b[...] += dot(weight[:, kept], full_in[:, both], 1, 1)
        s_in[...] = dot(act_t[...], weight[:, kept]).astype(BF16)
        act_c = weight[:, base + 2 * FF_TILE : base + 3 * FF_TILE]
        s_down[...] = dot(act_c, top[...], 0, 0).astype(BF16)

    raw_load = pltpu.make_async_copy(w_in_ref, raw_in, store_sem.at[12])
    raw_load.start()
    greet_all(devices)
    gain_keep = pltpu.make_async_copy(gain_shard, gain_land.at[grp], gain_sem)
    gain_keep.start()
    for step in range(1, SHARDS):
        gain_copy(step, grp).start()
    token_swaps[0][0]()
    first(0)
    first(1)
    for swap in token_swaps[1:]:
        swap[0]()
    first(2)
    raw_load.wait()
    weave_inside(raw_in, own_in)
    for group in range(groups):
        rows = slice(group * micros * CAP, (group + 1) * micros * CAP)
        picks[rows, :] = held_rows(lengths_ref, group, micros, devices)
    grad_b[...] = jnp.zeros_like(grad_b)
    for step in range(3):
        tick(step)
    gain_keep.wait()
    for step in range(1, SHARDS):
        gain_copy(step, lax.rem(grp + SHARDS - step, SHARDS)).wait_recv()
        gain_copy(step, grp).wait_send()
    for part in range(2):
        gain_rows[part : part + 1, :] = gain_row(part)
    for swap in token_swaps:
        swap[1]()
    for swap in top_swaps:
        swap[0]()
    complete(0)
    complete(1)
    put("late", weight, weight_out)
    for micro in range(MICRO):
        qkv_piece(micro)
        tick(3 + micro)
        attend_piece(micro)
        if micro == 0:
            complete(OUT_CHUNK)
        middle_piece(micro)
    act_t[...] = act_b[...].T
    for chunk in (4, 5):
        complete(chunk)
    free("late")
    for chunk in range(2):
        sent(chunk)
    steps = len(FF_CHUNKS)
    for step in range(2):
        if step:
            tick(7)
        complete(FF_CHUNKS[step])
        ff_forward(step)
    for swap in top_swaps:
        swap[1]()
    for micro in range(MICRO):
        top_piece(micro)
    for step in range(steps):
        if step + 2 < steps:
            tick(8 + step)
            complete(FF_CHUNKS[step + 2])
        free("in")
        free("down")
        ff_backward(step)
        if step + 2 < steps:
            ff_forward(step + 2)
        both, hidden, _ = ff_views(step)
        put("in", s_in, grad_in_out.at[:, both])
        put("down", s_down, grad_down_out.at[hidden])
    free("attn")
    free("mid")
    load_attn = pltpu.make_async_copy(attn_out, act_b, store_sem.at[13])
    load_mid = pltpu.make_async_copy(mid_out, total, store_sem.at[14])
    load_attn.start()
    for group in range(groups):
        rows = slice(group * micros * CAP, (group + 1) * micros * CAP)
        values = dot(picks[rows, :], total[rows, :].astype(BF16), 0, 0)
        token_land[:, group] = values.astype(BF16).reshape(devices, CHUNK_ROWS, D)
    put("layer", token_land, layer_out)
    load_mid.start()
    load_mid.wait()
    gain_grad[...] = jnp.zeros_like(gain_grad)

    def branch(index, carry):
        rows = pl.ds(pl.multiple_of(index * ROW_CHUNK, ROW_CHUNK), ROW_CHUNK)
        normal, inverse = normed(total[rows, :])
        grad = grad_b[rows, :]
        gain_grad[...] += jnp.sum(grad * normal, axis=0, keepdims=True)
        grad_mid = top[rows, :].astype(F32) + norm_back(
            grad * gain_rows[1:2, :], normal, inverse
        )
        total[rows, :] = grad_mid
        weight[rows, :D] = grad_mid.astype(BF16)
        return carry

    lax.fori_loop(0, ROWS // ROW_CHUNK, branch, 0)
    put("far", total, grad_mid_out)
    weight[:, D : 2 * D] = dot(weight[:, :D], full_out[...], 1, 1).astype(BF16)
    put("o", weight.at[:, pl.ds(D, D)], grad_o_out)
    load_attn.wait()
    weight[:, 2 * D :] = dot(act_b[...], weight[:, :D], 0, 0).astype(BF16)
    put("w", weight.at[:, pl.ds(2 * D, D)], grad_out_out)
    for name in list(pending):
        free(name)
    for chunk in range(2, chunks):
        sent(chunk)


def forward_all(lengths, gain, tables, sends, shards, devices, micros):
    anywhere = pl.BlockSpec(memory_space=pl.ANY)
    inside = pl.BlockSpec(memory_space=pltpu.VMEM)
    dma = pltpu.SemaphoreType.DMA
    groups = MICRO // micros
    exchanged = sends[0].shape
    chunks = len(GATHER_CHUNKS)
    full = [(SHARDS * v.shape[0], v.shape[1]) for v in shards]
    full[2] = (D, 2 * SHARDS * ff_shard(SHARDS))
    rows16 = jax.ShapeDtypeStruct((ROWS, D), BF16)
    rows32 = jax.ShapeDtypeStruct((ROWS, D), F32)
    return pl.pallas_call(
        functools.partial(forward_kernel, devices, micros),
        in_specs=[inside, anywhere, inside, inside, *[anywhere] * 6],
        out_specs=[inside, inside, *[anywhere] * 13],
        out_shape=[
            jax.ShapeDtypeStruct((2, D), F32),
            jax.ShapeDtypeStruct((1, D), F32),
            rows16,
            rows16,
            jax.ShapeDtypeStruct((ROWS, 3 * D), BF16),
            jax.ShapeDtypeStruct((BLOCKS, PAIRS, BLK, 2 * BLK), BF16),
            rows16,
            rows32,
            jax.ShapeDtypeStruct(exchanged, BF16),
            rows32,
            jax.ShapeDtypeStruct(full[2], BF16),
            jax.ShapeDtypeStruct(full[3], BF16),
            jax.ShapeDtypeStruct(full[0], BF16),
            rows16,
            jax.ShapeDtypeStruct((D, D), BF16),
        ],
        scratch_shapes=[
            *[pltpu.VMEM(v, BF16) for v in full],
            pltpu.VMEM(exchanged, BF16),
            pltpu.VMEM(exchanged, BF16),
            pltpu.VMEM((SHARDS, *gain.shape), BF16),
            pltpu.VMEM((ROWS, devices * CHUNK_ROWS), BF16),
            pltpu.VMEM((ROWS, D), BF16),
            pltpu.VMEM((D, ROWS), BF16),
            pltpu.VMEM((ROWS, D), BF16),
            pltpu.VMEM((ROWS, D), F32),
            pltpu.VMEM((ROWS, D), F32),
            pltpu.VMEM((CAP, D), BF16),
            pltpu.VMEM((CAP, D), BF16),
            pltpu.VMEM((CAP, 3 * D), BF16),
            pltpu.VMEM((SEQ_DEV, PAIRS, BLK, 2 * BLK), BF16),
            pltpu.VMEM((CAP, D), BF16),
            pltpu.VMEM((CAP, D), F32),
            pltpu.VMEM((D, 2 * FF_TILE), BF16),
            pltpu.VMEM((FF_TILE, D), BF16),
            pltpu.VMEM(shards[2].shape, BF16),
            pltpu.VMEM((shards[2].shape[0], full[2][1]), BF16),
            dma((15,)),
            dma,
            dma((SHARDS,)),
            dma((SHARDS,)),
            dma((2 * groups,)),
            dma((2 * groups, devices)),
            dma((2 * groups, devices)),
            dma((chunks,)),
            dma((chunks, 9)),
            dma((chunks, 9)),
        ],
        compiler_params=pltpu.CompilerParams(
            vmem_limit_bytes=63 * MIB, collective_id=0, has_side_effects=True
        ),
        cost_estimate=cost(30 * ROWS * D * FF, 600 * MIB),
    )(lengths, gain, *tables, *sends, *shards)


def ff_shard(group_size):
    return -(-FF // group_size // CHUNK_ROWS) * CHUNK_ROWS


def weave(weight, group_size):
    each, wide = FF // group_size, ff_shard(group_size)
    gap = jnp.zeros((weight.shape[0], wide - each), weight.dtype)
    halves = []
    for half in range(2):
        parts = []
        for shard in range(group_size):
            first = half * FF + shard * each
            parts += [weight[:, first : first + each], gap]
        halves.append(jnp.concatenate(parts, axis=1))
    steps = group_size * wide // FF_TILE
    return jnp.concatenate(
        [
            halves[half][:, step * FF_TILE : (step + 1) * FF_TILE]
            for step in range(steps)
            for half in range(2)
        ],
        axis=1,
    )


def weave_block(block):
    each, wide = FF // SHARDS, ff_shard(SHARDS)
    sources = []
    for lane in range(block * 128, (block + 1) * 128):
        half = lane % (2 * FF_TILE) // FF_TILE
        unit = lane // (2 * FF_TILE) * FF_TILE + lane % FF_TILE
        if unit % wide < each:
            sources.append(half * FF + unit // wide * each + unit % wide)
    return min(sources) // 128 * 128, -(-(max(sources) + 1) // 128) * 128


def weave_inside(raw, woven):
    each, wide = FF // SHARDS, ff_shard(SHARDS)
    for block in range(woven.shape[1] // 128):
        start, end = weave_block(block)
        first = block * 128
        half = first % (2 * FF_TILE) // FF_TILE
        base = first // (2 * FF_TILE) * FF_TILE + first % FF_TILE
        shape = (end - start, 128)
        unit = base + lax.broadcasted_iota(jnp.int32, shape, 1)
        low, turn = base // wide, (base // wide + 1) * wide
        shard = jnp.where(unit >= turn, low + 1, low)
        inner = unit - shard * wide
        source = half * FF + shard * each + inner
        mine = start + lax.broadcasted_iota(jnp.int32, shape, 0)
        pick = ((source == mine) & (inner < each)).astype(F32).astype(BF16)
        woven[:, first : first + 128] = dot(raw[:, start:end], pick).astype(BF16)


def unweave(woven, group_size):
    each, wide = FF // group_size, ff_shard(group_size)
    steps = group_size * wide // FF_TILE
    parts = []
    for half in range(2):
        row = jnp.concatenate(
            [
                woven[:, (2 * step + half) * FF_TILE : (2 * step + half + 1) * FF_TILE]
                for step in range(steps)
            ],
            axis=1,
        )
        parts += [row[:, i * wide : i * wide + each] for i in range(group_size)]
    return jnp.concatenate(parts, axis=1)


def body(tokens, cotangent, seq_lengths, w_qkv, w_out, w_in, w_down, attn_gain, mlp_gain):
    group_size = lax.axis_size("grp")
    devices = lax.axis_size("rep") * group_size
    device = lax.axis_index("rep") * group_size + lax.axis_index("grp")
    micros = min(MICRO, max(1, CHUNK_ROWS * devices // CAP))
    both = ("rep", "grp")

    def swap(rows):
        return lax.all_to_all(rows, both, split_axis=0, concat_axis=0, tiled=True)

    near = group_size == SHARDS and devices == REPLICAS * SHARDS
    sends = pack_rows(
        seq_lengths, (tokens[:, :, 0], cotangent[:, :, 0]), devices, micros
    )
    gains = jnp.stack([attn_gain, mlp_gain])
    pad = ff_shard(group_size) - w_down.shape[0]
    held = w_in if near else weave(w_in, group_size)
    shards = (w_qkv, w_out, held, jnp.pad(w_down, ((0, pad), (0, 0))))
    tables = rotary_tables()
    if near:
        gain = jnp.pad(gains, ((0, CHUNK_ROWS - 2), (0, 0)))
        (
            gains,
            grad_gain_two,
            hidden,
            act_a,
            qkv,
            prob,
            _,
            _,
            layer_send,
            grad_mid,
            grad_in_w,
            grad_down_w,
            full_qkv,
            grad_o,
            grad_out_w,
        ) = forward_all(seq_lengths, gain, tables, sends, shards, devices, micros)
        gain_one = gains[:1]
    else:
        token_rows, top_rows = (swap(v) for v in sends)
        full_qkv, full_out, full_in, full_down = (
            lax.all_gather(v, "grp", axis=0, tiled=True) for v in shards
        )
        gains = lax.all_gather(gains, "grp", axis=1, tiled=True).astype(F32)
        gain_one, gain_two = gains[:1], gains[1:]
        hidden, act_a, top = unpack_rows(
            seq_lengths, token_rows, top_rows, gain_one, devices, micros
        )
        qkv = qkv_rows(act_a, full_qkv, *tables)
        attn_o, prob = attend(qkv, seq_lengths, devices)
        middle, act_b = middle_rows(attn_o, hidden, full_out, gain_two)
        layer_rows, grad_b, grad_in_w, grad_down_w = ffn(
            act_b, top, middle, full_in, full_down
        )
        layer_send = repack_rows(seq_lengths, layer_rows, devices, micros)
        grad_mid, grad_o, grad_out_w, grad_gain_two = branch_back(
            layer_send, grad_b, middle, top, attn_o, full_out, gain_two
        )
    if near:
        grad_down, grad_in, grad_out, grad_qkv, gain_sums, layer_back, grad_back = return_all(
            (grad_down_w, grad_in_w, grad_out_w),
            layer_send,
            seq_lengths,
            qkv,
            prob,
            grad_o,
            act_a,
            hidden,
            grad_mid,
            full_qkv,
            gain_one,
            grad_gain_two,
            tables,
            devices,
            micros,
        )
        gain_sums = gain_sums[0].reshape(2, -1)
    else:
        layer_back = swap(layer_send)
        grad_qkv_rows = attend_back(qkv, grad_o, prob, *tables)
        grad_qkv_w = qkv_grad(act_a, grad_qkv_rows)
        grad_rows, gain_parts = input_back(
            grad_qkv_rows, full_qkv, hidden, grad_mid, gain_one, grad_gain_two
        )
        grad_back = swap(repack_rows(seq_lengths, grad_rows, devices, micros))
        grad_down, grad_in, grad_out, grad_qkv = (
            lax.psum(lax.psum_scatter(v, "grp", scatter_dimension=0, tiled=True), "rep")
            for v in (grad_down_w, grad_in_w, grad_out_w, grad_qkv_w)
        )
        gain_parts = gain_parts[:, 0].reshape(SHARDS, 2, -1).swapaxes(0, 1).reshape(2, D)
        gain_sums = lax.psum(
            lax.psum_scatter(gain_parts, "grp", scatter_dimension=1, tiled=True), "rep"
        )
    grad_down, grad_in, grad_out, grad_qkv = (
        v.astype(F32) for v in (grad_down, grad_in, grad_out, grad_qkv)
    )
    layer_out = spread_rows(seq_lengths, layer_back, devices, micros)[:, :, None, :]
    grad_tokens = spread_rows(seq_lengths, grad_back, devices, micros)[:, :, None, :]
    return (
        layer_out,
        grad_tokens,
        gain_sums[0],
        gain_sums[1],
        grad_qkv,
        grad_out,
        unweave(grad_in, group_size),
        grad_down[: w_down.shape[0]],
    )


def solution(mesh):
    return jax.shard_map(
        body,
        mesh=mesh,
        in_specs=(
            P(None, None, ("rep", "grp"), None),
            P(None, None, ("rep", "grp"), None),
            P(),
            P("grp", None),
            P("grp", None),
            P("grp", None),
            P("grp", None),
            P("grp"),
            P("grp"),
        ),
        out_specs=(
            P(None, None, ("rep", "grp"), None),
            P(None, None, ("rep", "grp"), None),
            P("grp"),
            P("grp"),
            P("grp", None),
            P("grp", None),
            P("grp", None),
            P("grp", None),
        ),
        check_vma=False,
    )
```

```python
import functools
import math

import jax
import jax.numpy as jnp
import numpy as np
from jax import lax
from jax.experimental import pallas as pl
from jax.experimental.pallas import tpu as pltpu
from jax.sharding import PartitionSpec as P

D = 1024
HEADS = 16
HD = 64
FF = 2624
BLK = 128
MICRO = 4
SEQ_DEV = 2
CAP = 256
TOK_DEV = 192
ROWS = MICRO * CAP
BLOCKS = ROWS // BLK
PAIRS = HEADS // 2
LANES = 2 * HD

EPS = 1e-05
THETA = 160000.0
NEG = -1e30
ROOT_HALF = math.sqrt(0.5)
INV_ROOT_TWO_PI = 1.0 / math.sqrt(2.0 * math.pi)
SCALE = HD**-0.5

FF_TILE = 384
ROW_CHUNK = 256
CHUNK_ROWS = 16
SHARDS = 8
REPLICAS = 4
GAIN_ROWS = 8

F32 = jnp.float32
BF16 = jnp.bfloat16
MIB = 1 << 20


def dot(left, right, left_dim=1, right_dim=0):
    return lax.dot_general(
        left, right, (((left_dim,), (right_dim,)), ((), ())), preferred_element_type=F32
    )


def params(mib, steps=1):
    return pltpu.CompilerParams(
        vmem_limit_bytes=mib * MIB, dimension_semantics=("arbitrary",) * steps
    )


def cost(flops, moved, transcendentals=0):
    return pl.CostEstimate(
        flops=flops, bytes_accessed=moved, transcendentals=transcendentals
    )


def normed(values):
    center = values - jnp.mean(values, axis=-1, keepdims=True)
    inverse = lax.rsqrt(jnp.mean(center * center, axis=-1, keepdims=True) + EPS)
    return center * inverse, inverse


def norm_back(grad, normal, inverse):
    centred = grad - jnp.mean(grad, axis=-1, keepdims=True)
    return inverse * (centred - normal * jnp.mean(grad * normal, axis=-1, keepdims=True))


def rotary_tables():
    half = HD // 2
    frequency = np.float32(THETA) ** (-2.0 * np.arange(half, dtype=np.float32) / HD)
    angles = np.arange(BLK, dtype=np.float32)[:, None] * frequency.astype(np.float32)[None]
    cosine, sine = np.cos(angles), np.sin(angles)
    return (
        np.concatenate([cosine] * 4, axis=1).astype(np.float32),
        np.concatenate([-sine, sine] * 2, axis=1).astype(np.float32),
    )


def widen(table):
    return jnp.concatenate([table] * (QKV_TILE // LANES), axis=1)


def turned(values):
    axis = values.ndim - 1
    half = HD // 2
    width = values.shape[axis]
    lane = lax.broadcasted_iota(jnp.int32, values.shape, axis) % HD
    return jnp.where(
        lane < half,
        pltpu.roll(values, width - half, axis),
        pltpu.roll(values, half, axis),
    )


def position(devices):
    return lax.axis_index("rep") * (devices // lax.axis_size("rep")) + lax.axis_index("grp")


def length_sums(lengths_ref, chosen):
    return dot(
        lengths_ref[...].astype(F32).astype(BF16), chosen.astype(F32).astype(BF16)
    )


def slot_grid(sequences, devices):
    shape = (sequences, devices * CHUNK_ROWS)
    sequence = lax.broadcasted_iota(jnp.int32, shape, 0)
    slot = lax.broadcasted_iota(jnp.int32, shape, 1)
    inner = slot % CHUNK_ROWS
    pair_cap = CAP // devices
    return sequence, slot // CHUNK_ROWS, inner % pair_cap, inner // pair_cap


def ceil_div(value, count):
    return jnp.floor((value + (count - 0.5)) * (1.0 / count))


def sent_rows(lengths_ref, group, micros, devices):
    sequence, peer, rank, part = slot_grid(lengths_ref.shape[1], devices)
    starts = length_sums(lengths_ref, sequence < SEQ_DEV * peer)
    device = position(devices).astype(F32)
    wanted = ceil_div(starts - device, devices) + rank[:1].astype(F32)
    return pick_micros(wanted, part, group, micros, -1.0)


def pick_micros(values, part, group, micros, other):
    micro = lax.broadcasted_iota(jnp.int32, values.shape, 0)
    rows = []
    for step in range(micros):
        chosen = jnp.where(micro == group * micros + step, values, 0.0)
        row = jnp.sum(chosen, axis=0, keepdims=True)
        rows.append(jnp.where(part[:1] == step, row, other))
    return rows


def held_rows(lengths_ref, group, micros, devices):
    sequence, peer, rank, part = slot_grid(lengths_ref.shape[1], devices)
    device = position(devices)
    first = length_sums(lengths_ref, sequence < SEQ_DEV * device)
    source = peer[:1].astype(F32)
    given = (ceil_div(first - source, devices) + rank[:1].astype(F32)) * devices + source
    parts = [[None] * (CAP // BLK) for _ in range(micros)]
    for block in range(CAP // BLK):
        own = SEQ_DEV * device + block
        start = length_sums(lengths_ref, sequence < own)
        length = length_sums(lengths_ref, sequence == own)
        offsets = pick_micros(given - start, part, group, micros, -1.0)
        limits = pick_micros(length, part, group, micros, 0.0)
        for step in range(micros):
            place = lax.broadcasted_iota(jnp.int32, (BLK, part.shape[1]), 0).astype(F32)
            hit = (place == offsets[step]) & (place < limits[step])
            parts[step][block] = hit.astype(F32).astype(BF16)
    return jnp.concatenate([v for blocks in parts for v in blocks], axis=0)


def row_match(row):
    mine = lax.broadcasted_iota(jnp.int32, (TOK_DEV, row.shape[1]), 0).astype(F32)
    return (mine == row).astype(F32).astype(BF16)


def pack_kernel(micros, devices, lengths_ref, *refs):
    rows = sent_rows(lengths_ref, pl.program_id(0), micros, devices)
    picks = [row_match(row) for row in rows]
    count = len(refs) // 2
    for rows_ref, out_ref in zip(refs[:count], refs[count:]):
        total = None
        for step in range(micros):
            term = dot(picks[step], rows_ref[step], 0, 0)
            total = term if total is None else total + term
        out_ref[...] = total.astype(BF16).reshape(out_ref.shape)


def pack_rows(lengths, tables, devices, micros):
    groups = MICRO // micros
    slots = devices * CHUNK_ROWS
    count = len(tables)
    return pl.pallas_call(
        functools.partial(pack_kernel, micros, devices),
        grid=(groups,),
        in_specs=[
            pl.BlockSpec(lengths.shape, lambda g: (0, 0)),
            *[pl.BlockSpec((micros, TOK_DEV, D), lambda g: (g, 0, 0))] * count,
        ],
        out_specs=[
            pl.BlockSpec((devices, 1, CHUNK_ROWS, D), lambda g: (0, g, 0, 0))
        ]
        * count,
        out_shape=[jax.ShapeDtypeStruct((devices, groups, CHUNK_ROWS, D), BF16)] * count,
        compiler_params=params(48),
        cost_estimate=cost(
            2 * count * MICRO * TOK_DEV * slots * D, 4 * count * groups * slots * D
        ),
    )(lengths, *tables)


def spread_kernel(micros, devices, lengths_ref, back_ref, out_ref):
    arrived = back_ref[...].reshape(-1, D)
    rows = sent_rows(lengths_ref, pl.program_id(0), micros, devices)
    for step in range(micros):
        out_ref[step] = dot(row_match(rows[step]), arrived).astype(BF16)


def spread_rows(lengths, back, devices, micros):
    groups = MICRO // micros
    slots = devices * CHUNK_ROWS
    return pl.pallas_call(
        functools.partial(spread_kernel, micros, devices),
        grid=(groups,),
        in_specs=[
            pl.BlockSpec(lengths.shape, lambda g: (0, 0)),
            pl.BlockSpec((devices, 1, CHUNK_ROWS, D), lambda g: (0, g, 0, 0)),
        ],
        out_specs=pl.BlockSpec((micros, TOK_DEV, D), lambda g: (g, 0, 0)),
        out_shape=jax.ShapeDtypeStruct((MICRO, TOK_DEV, D), BF16),
        compiler_params=params(40),
        cost_estimate=cost(2 * MICRO * TOK_DEV * slots * D, 4 * groups * slots * D),
    )(lengths, back)


def unpack_kernel(
    micros, devices, lengths_ref, token_ref, top_ref, gain_ref, hidden_ref, act_ref, grad_ref
):
    pick = held_rows(lengths_ref, pl.program_id(0), micros, devices)
    rows = dot(pick, token_ref[...].reshape(-1, D))
    hidden_ref[...] = rows.astype(BF16)
    act_ref[...] = (normed(rows)[0] * gain_ref[...]).astype(BF16)
    grad_ref[...] = dot(pick, top_ref[...].reshape(-1, D)).astype(BF16)


def unpack_rows(lengths, tokens, top, gain, devices, micros):
    groups = MICRO // micros
    slots = devices * CHUNK_ROWS
    chunk = pl.BlockSpec((devices, 1, CHUNK_ROWS, D), lambda g: (0, g, 0, 0))
    return pl.pallas_call(
        functools.partial(unpack_kernel, micros, devices),
        grid=(groups,),
        in_specs=[
            pl.BlockSpec(lengths.shape, lambda g: (0, 0)),
            chunk,
            chunk,
            pl.BlockSpec((1, D), lambda g: (0, 0)),
        ],
        out_specs=[pl.BlockSpec((micros * CAP, D), lambda g: (g, 0))] * 3,
        out_shape=[jax.ShapeDtypeStruct((ROWS, D), BF16)] * 3,
        compiler_params=params(48),
        cost_estimate=cost(4 * ROWS * slots * D, 8 * groups * slots * D),
    )(lengths, tokens, top, gain)


def repack_kernel(micros, devices, lengths_ref, rows_ref, out_ref):
    pick = held_rows(lengths_ref, pl.program_id(0), micros, devices)
    out_ref[...] = dot(pick, rows_ref[...], 0, 0).astype(BF16).reshape(out_ref.shape)


def repack_rows(lengths, rows, devices, micros):
    groups = MICRO // micros
    slots = devices * CHUNK_ROWS
    return pl.pallas_call(
        functools.partial(repack_kernel, micros, devices),
        grid=(groups,),
        in_specs=[
            pl.BlockSpec(lengths.shape, lambda g: (0, 0)),
            pl.BlockSpec((micros * CAP, D), lambda g: (g, 0)),
        ],
        out_specs=pl.BlockSpec((devices, 1, CHUNK_ROWS, D), lambda g: (0, g, 0, 0)),
        out_shape=jax.ShapeDtypeStruct((devices, groups, CHUNK_ROWS, D), BF16),
        compiler_params=params(40),
        cost_estimate=cost(2 * ROWS * slots * D, 4 * groups * slots * D),
    )(lengths, rows)


QKV_TILE = 512


def qkv_kernel(act_ref, weight_ref, cos_ref, sin_ref, out_ref):
    packed = dot(act_ref[...], weight_ref[...])
    is_value = pl.program_id(0) >= 2 * D // QKV_TILE

    @pl.when(is_value)
    def _():
        out_ref[...] = packed.astype(BF16)

    @pl.when(jnp.logical_not(is_value))
    def _():
        split = packed.reshape(BLOCKS, BLK, QKV_TILE)
        spun = split * widen(cos_ref[...])[None] + turned(split) * widen(sin_ref[...])[None]
        out_ref[...] = spun.reshape(ROWS, QKV_TILE).astype(BF16)


def qkv_rows(act, weight, cosine, sine):
    return pl.pallas_call(
        qkv_kernel,
        grid=(3 * D // QKV_TILE,),
        in_specs=[
            pl.BlockSpec((ROWS, D), lambda j: (0, 0)),
            pl.BlockSpec((D, QKV_TILE), lambda j: (0, j)),
            pl.BlockSpec((BLK, LANES), lambda j: (0, 0)),
            pl.BlockSpec((BLK, LANES), lambda j: (0, 0)),
        ],
        out_specs=pl.BlockSpec((ROWS, QKV_TILE), lambda j: (0, j)),
        out_shape=jax.ShapeDtypeStruct((ROWS, 3 * D), BF16),
        compiler_params=params(40),
        cost_estimate=cost(2 * ROWS * D * 3 * D, 2 * (3 * D * D + ROWS * 4 * D)),
    )(act, weight, cosine, sine)


def head_masks(dtype):
    lane = lax.broadcasted_iota(jnp.int32, (BLK, LANES), 1)
    low = (lane < HD).astype(F32).astype(dtype)
    high = (lane >= HD).astype(F32).astype(dtype)
    return low, high


def attend_pair(query, key, value, valid):
    low, high = head_masks(BF16)
    scores = dot(query, jnp.concatenate([key * low, key * high], axis=0), 1, 1)
    parts = []
    for head in range(2):
        score = scores[:, head * BLK : (head + 1) * BLK] * SCALE
        score = jnp.where(valid, score, NEG)
        expo = jnp.exp(score - jnp.max(score, axis=-1, keepdims=True))
        parts.append(expo / jnp.sum(expo, axis=-1, keepdims=True))
    prob = jnp.concatenate(parts, axis=1).astype(BF16)
    both = jnp.concatenate([value * low, value * high], axis=0)
    return dot(prob, both).astype(BF16), prob


def block_lengths(length_ref, block, devices):
    shape = (length_ref.shape[1], BLK)
    own = lax.broadcasted_iota(jnp.int32, shape, 0) == (
        SEQ_DEV * position(devices) + block
    )
    return length_sums(length_ref, own)


def key_mask(length):
    return lax.broadcasted_iota(jnp.int32, (BLK, BLK), 1).astype(F32) < length


def attend_kernel(devices, length_ref, q_ref, k_ref, v_ref, out_ref, prob_ref):
    block = pl.program_id(0)
    lengths = block_lengths(length_ref, block % SEQ_DEV, devices)
    micro = lax.broadcasted_iota(jnp.int32, lengths.shape, 0) == block // SEQ_DEV
    valid = key_mask(jnp.sum(jnp.where(micro, lengths, 0.0), axis=0, keepdims=True))
    for pair in range(PAIRS):
        lanes = slice(pair * LANES, (pair + 1) * LANES)
        out_ref[:, lanes], prob_ref[0, pair] = attend_pair(
            q_ref[:, lanes], k_ref[:, lanes], v_ref[:, lanes], valid
        )


def attend(qkv, lengths, devices):
    return pl.pallas_call(
        functools.partial(attend_kernel, devices),
        grid=(BLOCKS,),
        in_specs=[
            pl.BlockSpec(lengths.shape, lambda b: (0, 0)),
            pl.BlockSpec((BLK, D), lambda b: (b, 0)),
            pl.BlockSpec((BLK, D), lambda b: (b, 1)),
            pl.BlockSpec((BLK, D), lambda b: (b, 2)),
        ],
        out_specs=[
            pl.BlockSpec((BLK, D), lambda b: (b, 0)),
            pl.BlockSpec((1, PAIRS, BLK, 2 * BLK), lambda b: (b, 0, 0, 0)),
        ],
        out_shape=[
            jax.ShapeDtypeStruct((ROWS, D), BF16),
            jax.ShapeDtypeStruct((BLOCKS, PAIRS, BLK, 2 * BLK), BF16),
        ],
        compiler_params=params(32),
        cost_estimate=cost(8 * ROWS * BLK * D, 2 * ROWS * 6 * D, ROWS * HEADS * BLK),
    )(lengths, qkv, qkv, qkv)


def attend_back_kernel(
    q_ref, k_ref, v_ref, grad_ref, prob_ref, cos_ref, sin_ref, out_ref
):
    for pair in range(PAIRS):
        start = pair * LANES
        lanes = slice(start, start + LANES)
        results = attend_back_pair(
            q_ref[:, lanes],
            k_ref[:, lanes],
            v_ref[:, lanes],
            grad_ref[:, lanes],
            prob_ref[0, pair],
            cos_ref[...],
            sin_ref[...],
        )
        for part, result in enumerate(results):
            out_ref[:, part * D + start : part * D + start + LANES] = result


def attend_back(qkv, grad_o, prob, cosine, sine):
    return pl.pallas_call(
        attend_back_kernel,
        grid=(BLOCKS,),
        in_specs=[
            pl.BlockSpec((BLK, D), lambda b: (b, 0)),
            pl.BlockSpec((BLK, D), lambda b: (b, 1)),
            pl.BlockSpec((BLK, D), lambda b: (b, 2)),
            pl.BlockSpec((BLK, D), lambda b: (b, 0)),
            pl.BlockSpec((1, PAIRS, BLK, 2 * BLK), lambda b: (b, 0, 0, 0)),
            pl.BlockSpec((BLK, LANES), lambda b: (0, 0)),
            pl.BlockSpec((BLK, LANES), lambda b: (0, 0)),
        ],
        out_specs=pl.BlockSpec((BLK, 3 * D), lambda b: (b, 0)),
        out_shape=jax.ShapeDtypeStruct((ROWS, 3 * D), BF16),
        compiler_params=params(32),
        cost_estimate=cost(20 * ROWS * BLK * D, 2 * ROWS * 9 * D),
    )(qkv, qkv, qkv, grad_o, prob, cosine, sine)


def middle_kernel(attn_ref, hidden_ref, weight_ref, gain_ref, mid_ref, act_ref):
    middle = hidden_ref[...].astype(F32) + dot(attn_ref[...], weight_ref[...])
    mid_ref[...] = middle
    act_ref[...] = (normed(middle)[0] * gain_ref[...]).astype(BF16)


def middle_rows(attn_o, hidden, weight, gain):
    tile = pl.BlockSpec((ROW_CHUNK, D), lambda i: (i, 0))
    return pl.pallas_call(
        middle_kernel,
        grid=(ROWS // ROW_CHUNK,),
        in_specs=[
            tile,
            tile,
            pl.BlockSpec((D, D), lambda i: (0, 0)),
            pl.BlockSpec((1, D), lambda i: (0, 0)),
        ],
        out_specs=[tile, tile],
        out_shape=[
            jax.ShapeDtypeStruct((ROWS, D), F32),
            jax.ShapeDtypeStruct((ROWS, D), BF16),
        ],
        compiler_params=params(32),
        cost_estimate=cost(2 * ROWS * D * D, 2 * D * D + 10 * ROWS * D),
    )(attn_o, hidden, weight, gain)


def ffn_kernel(
    act_ref,
    top_ref,
    mid_ref,
    in_ref,
    down_ref,
    layer_ref,
    grad_b_ref,
    grad_in_ref,
    grad_down_ref,
    total,
    act_t,
    kept_c,
    kept_gu,
):
    step = pl.program_id(0)

    @pl.when(step == 0)
    def _():
        total[...] = mid_ref[...]
        grad_b_ref[...] = jnp.zeros_like(grad_b_ref)
        act_t[...] = act_ref[...].T

    def rows_step(index, carry):
        rows = pl.ds(pl.multiple_of(index * ROW_CHUNK, ROW_CHUNK), ROW_CHUNK)
        act, top = act_ref[rows, :], top_ref[rows, :]
        gate_up = dot(act, in_ref[...])
        gelu_in, linear = gate_up[:, :FF_TILE], gate_up[:, FF_TILE:]
        grad_c = dot(top, down_ref[...], 1, 1)
        phi = 0.5 * (1.0 + lax.erf(gelu_in * ROOT_HALF))
        gelu_out = gelu_in * phi
        slope = phi + gelu_in * (jnp.exp(-0.5 * gelu_in * gelu_in) * INV_ROOT_TWO_PI)
        act_c = (gelu_out * linear).astype(BF16)
        kept_c[rows, :] = act_c
        kept_gu[rows, :FF_TILE] = (grad_c * linear * slope).astype(BF16)
        kept_gu[rows, FF_TILE:] = (grad_c * gelu_out).astype(BF16)
        total[rows, :] += dot(act_c, down_ref[...])
        grad_b_ref[rows, :] += dot(kept_gu[rows, :], in_ref[...], 1, 1)
        return carry

    lax.fori_loop(0, ROWS // ROW_CHUNK, rows_step, 0)
    grad_in_ref[...] = dot(act_t[...], kept_gu[...]).astype(BF16)
    grad_down_ref[...] = dot(kept_c[...], top_ref[...], 0, 0).astype(BF16)

    @pl.when(step == pl.num_programs(0) - 1)
    def _():
        layer_ref[...] = total[...].astype(BF16)


def ffn(act, top, middle, full_in, full_down):
    whole = pl.BlockSpec((ROWS, D), lambda j: (0, 0))
    tall = pl.BlockSpec((D, 2 * FF_TILE), lambda j: (0, j))
    wide = pl.BlockSpec((FF_TILE, D), lambda j: (j, 0))
    return pl.pallas_call(
        ffn_kernel,
        grid=(full_down.shape[0] // FF_TILE,),
        in_specs=[
            whole,
            whole,
            whole,
            tall,
            wide,
        ],
        out_specs=[whole, whole, tall, wide],
        out_shape=[
            jax.ShapeDtypeStruct((ROWS, D), BF16),
            jax.ShapeDtypeStruct((ROWS, D), F32),
            jax.ShapeDtypeStruct(full_in.shape, BF16),
            jax.ShapeDtypeStruct(full_down.shape, BF16),
        ],
        scratch_shapes=[
            pltpu.VMEM((ROWS, D), F32),
            pltpu.VMEM((D, ROWS), BF16),
            pltpu.VMEM((ROWS, FF_TILE), BF16),
            pltpu.VMEM((ROWS, 2 * FF_TILE), BF16),
        ],
        compiler_params=params(60),
        cost_estimate=cost(18 * ROWS * D * FF, 12 * D * FF, 2 * ROWS * FF),
    )(act, top, middle, full_in, full_down)


def branch_kernel(
    order_ref,
    grad_b_ref,
    mid_ref,
    top_ref,
    attn_ref,
    weight_ref,
    gain_ref,
    grad_mid_ref,
    grad_o_ref,
    grad_w_ref,
    grad_gain_ref,
    total,
):
    step = pl.program_id(0)

    @pl.when(step == 0)
    def _():
        total[...] = jnp.zeros_like(total)
        grad_gain_ref[...] = jnp.zeros_like(grad_gain_ref)

    grad_b = grad_b_ref[...]
    normal, inverse = normed(mid_ref[...])
    grad_gain_ref[...] += jnp.sum(grad_b * normal, axis=0, keepdims=True)
    grad_mid = top_ref[...].astype(F32) + norm_back(
        grad_b * gain_ref[...], normal, inverse
    )
    grad_mid_ref[...] = grad_mid
    grad_r = grad_mid.astype(BF16)
    grad_o_ref[...] = dot(grad_r, weight_ref[...], 1, 1).astype(BF16)
    total[...] += dot(attn_ref[...], grad_r, 0, 0)

    @pl.when(step == ROWS // ROW_CHUNK - 1)
    def _():
        grad_w_ref[...] = total[...].astype(BF16)


def branch_back(order, grad_b, middle, top, attn_o, weight, gain):
    tile = pl.BlockSpec((ROW_CHUNK, D), lambda i: (i, 0))
    square = pl.BlockSpec((D, D), lambda i: (0, 0))
    line = pl.BlockSpec((1, D), lambda i: (0, 0))
    return pl.pallas_call(
        branch_kernel,
        grid=(ROWS // ROW_CHUNK,),
        in_specs=[
            pl.BlockSpec(memory_space=pl.ANY),
            *[tile] * 4,
            square,
            line,
        ],
        out_specs=[tile, tile, square, line],
        out_shape=[
            jax.ShapeDtypeStruct((ROWS, D), F32),
            jax.ShapeDtypeStruct((ROWS, D), BF16),
            jax.ShapeDtypeStruct((D, D), BF16),
            jax.ShapeDtypeStruct((1, D), F32),
        ],
        scratch_shapes=[pltpu.VMEM((D, D), F32)],
        compiler_params=params(40),
        cost_estimate=cost(4 * ROWS * D * D, 4 * D * D + 18 * ROWS * D),
    )(order, grad_b, middle, top, attn_o, weight, gain)


def input_kernel(
    grad_qkv_ref,
    weight_ref,
    hidden_ref,
    grad_mid_ref,
    gain_ref,
    other_ref,
    out_ref,
    gains_ref,
    grad_gain,
):
    @pl.when(pl.program_id(0) == 0)
    def _():
        grad_gain[...] = jnp.zeros_like(grad_gain)

    grad_a = dot(grad_qkv_ref[...], weight_ref[...], 1, 1)
    normal, inverse = normed(hidden_ref[...].astype(F32))
    grad_gain[...] += jnp.sum(grad_a * normal, axis=0, keepdims=True)
    out_ref[...] = (
        grad_mid_ref[...] + norm_back(grad_a * gain_ref[...], normal, inverse)
    ).astype(BF16)

    @pl.when(pl.program_id(0) == ROWS // ROW_CHUNK - 1)
    def _():
        width = D // SHARDS
        for shard in range(SHARDS):
            lanes = slice(shard * width, (shard + 1) * width)
            for part, values in enumerate((grad_gain, other_ref)):
                gains_ref[shard, :, part * width : (part + 1) * width] = jnp.broadcast_to(
                    values[:, lanes], (GAIN_ROWS, width)
                )


def input_back(grad_qkv, weight, hidden, grad_mid, gain, other):
    tile = pl.BlockSpec((ROW_CHUNK, D), lambda i: (i, 0))
    line = pl.BlockSpec((1, D), lambda i: (0, 0))
    return pl.pallas_call(
        input_kernel,
        grid=(ROWS // ROW_CHUNK,),
        in_specs=[
            pl.BlockSpec((ROW_CHUNK, 3 * D), lambda i: (i, 0)),
            pl.BlockSpec((D, 3 * D), lambda i: (0, 0)),
            tile,
            tile,
            line,
            line,
        ],
        out_specs=[
            tile,
            pl.BlockSpec((SHARDS, GAIN_ROWS, 2 * D // SHARDS), lambda i: (0, 0, 0)),
        ],
        out_shape=[
            jax.ShapeDtypeStruct((ROWS, D), BF16),
            jax.ShapeDtypeStruct((SHARDS, GAIN_ROWS, 2 * D // SHARDS), F32),
        ],
        scratch_shapes=[pltpu.VMEM((1, D), F32)],
        compiler_params=params(40),
        cost_estimate=cost(6 * ROWS * D * D, 6 * D * D + 14 * ROWS * D),
    )(grad_qkv, weight, hidden, grad_mid, gain, other)


def qkv_grad_kernel(act_ref, grad_ref, out_ref, act_t):
    @pl.when(pl.program_id(0) == 0)
    def _():
        act_t[...] = act_ref[...].T

    out_ref[...] = dot(act_t[...], grad_ref[...]).astype(BF16)


def qkv_grad(act, grad_qkv):
    return pl.pallas_call(
        qkv_grad_kernel,
        grid=(3 * D // QKV_TILE,),
        in_specs=[
            pl.BlockSpec((ROWS, D), lambda j: (0, 0)),
            pl.BlockSpec((ROWS, QKV_TILE), lambda j: (0, j)),
        ],
        out_specs=pl.BlockSpec((D, QKV_TILE), lambda j: (0, j)),
        out_shape=jax.ShapeDtypeStruct((D, 3 * D), BF16),
        scratch_shapes=[pltpu.VMEM((D, ROWS), BF16)],
        compiler_params=params(32),
        cost_estimate=cost(6 * ROWS * D * D, 2 * (7 * D * D)),
    )(act, grad_qkv)


MESH = pl.DeviceIdType.MESH
EARLY_CHUNKS = (
    (0, 0, 512),
    (0, 512, 512),
    *[(1, i * 768, 768) for i in range(7)],
    (2, 0, 1024),
)
LATE_CHUNKS = (
    (3, 0, 768),
    (3, 768, 768),
    (3, 1536, 768),
    (3, 2304, 512),
    (4, 0, 256),
    (3, 2816, 256),
)
REDUCE_CHUNKS = EARLY_CHUNKS + LATE_CHUNKS
HOP_CORE, HOP_X, HOP_Y, HOP_XY, HOP_YX, HOP_IN, HOP_MID, HOP_OUT = range(8)


def place():
    rep, grp = lax.axis_index("rep"), lax.axis_index("grp")
    core, x, y = grp % 2, grp // 2 % 2, grp // 4
    return rep, grp, core, x, y, grp + 1 - 2 * core, grp + 2 - 4 * x, grp + 4 - 8 * y


def mesh_id(index):
    return (index // SHARDS, lax.rem(index, SHARDS))


def greet_all(devices):
    device = position(devices)
    barrier = pltpu.get_barrier_semaphore()

    def greet(step, carry):
        to = mesh_id(lax.rem(device + step, devices))
        pl.semaphore_signal(barrier, device_id=to, device_id_type=MESH)
        return carry

    lax.fori_loop(1, devices, greet, 0)
    pl.semaphore_wait(barrier, devices - 1)


def row_exchange(send, land, local_sem, send_sem, recv_sem, devices):
    device = position(devices)

    def copy(step, slot):
        to = lax.rem(device + step, devices)
        return pltpu.make_async_remote_copy(
            src_ref=send(to),
            dst_ref=land(slot),
            send_sem=send_sem.at[step],
            recv_sem=recv_sem.at[step],
            device_id=mesh_id(to),
            device_id_type=MESH,
        )

    def keep():
        return pltpu.make_async_copy(send(device), land(device), local_sem)

    def start():
        def one(step, carry):
            copy(step, device).start()
            return carry

        keep().start()
        lax.fori_loop(1, devices, one, 0)

    def finish():
        def one(step, carry):
            copy(step, lax.rem(device + devices - step, devices)).wait_recv()
            copy(step, device).wait_send()
            return carry

        lax.fori_loop(1, devices, one, 0)
        keep().wait()

    return start, finish


def reduction(table, tensors, outs, refs):
    chunks = len(table)
    sums, from_core, from_near, from_cross, from_far = (
        refs[i * chunks : (i + 1) * chunks] for i in range(5)
    )
    load_sem, send_sem, recv_sem, store_sem = refs[5 * chunks :]
    rep, grp, core, x, y, by_core, by_x, by_y = place()
    is_middle = (rep == 1) | (rep == 2)
    inward, outward, across = 1 + rep // 2, 3 * (rep // 2), 3 - rep

    def hop(chunk, which):
        tensor, start, width = table[chunk]
        half = width // 2
        left, right, columns = pl.ds(0, half), pl.ds(half, half), pl.ds(start, width)
        total, far = sums[chunk], from_far[chunk]
        near, cross = from_near[chunk], from_cross[chunk]
        if which == HOP_CORE:
            source, target = tensors[tensor].at[:, :, 1 - core, :, columns], from_core[chunk]
        elif which == HOP_X:
            source, target = total.at[:, 1 - x, :, left], near.at[0]
        elif which == HOP_Y:
            source, target = total.at[1 - y, :, :, right], near.at[1]
        elif which == HOP_XY:
            source, target = total.at[1 - y, x, :, left], cross.at[0]
        elif which == HOP_YX:
            source, target = total.at[y, 1 - x, :, right], cross.at[1]
        elif which == HOP_IN:
            source, target = total.at[y, x], far.at[0]
        elif which == HOP_MID:
            source, target = total.at[y, x], far.at[1]
        else:
            source, target = far.at[0], outs[tensor].at[:, columns]
        to_rep = (rep, rep, rep, rep, rep, inward, across, outward)[which]
        to_grp = (by_core, by_x, by_y, by_y, by_x, grp, grp, grp)[which]
        return pltpu.make_async_remote_copy(
            src_ref=source,
            dst_ref=target,
            send_sem=send_sem.at[chunk, which],
            recv_sem=recv_sem.at[chunk, which],
            device_id=(to_rep, to_grp),
            device_id_type=MESH,
        )

    def load(chunk):
        tensor, start, width = table[chunk]
        return pltpu.make_async_copy(
            tensors[tensor].at[:, :, core, :, pl.ds(start, width)],
            sums[chunk],
            load_sem.at[chunk],
        )

    def store(chunk):
        tensor, start, width = table[chunk]
        return pltpu.make_async_copy(
            from_far[chunk].at[0],
            outs[tensor].at[:, pl.ds(start, width)],
            store_sem.at[chunk],
        )

    def add(one, other):
        return (one.astype(F32) + other.astype(F32)).astype(one.dtype)

    def after_core(chunk):
        load(chunk).wait()
        hop(chunk, HOP_CORE).wait_recv()
        total = sums[chunk]

        def plane(index, carry):
            row, column = index // 2, index % 2
            total[row, column] = add(total[row, column], from_core[chunk][row, column])
            return carry

        lax.fori_loop(0, 4, plane, 0)
        hop(chunk, HOP_X).start()
        hop(chunk, HOP_Y).start()

    def after_near(chunk):
        half = table[chunk][2] // 2
        hop(chunk, HOP_X).wait_recv()
        hop(chunk, HOP_Y).wait_recv()
        total, near = sums[chunk], from_near[chunk]

        def plane(index, carry):
            total[index, x, :, :half] = add(total[index, x, :, :half], near[0, index])
            total[y, index, :, half:] = add(total[y, index, :, half:], near[1, index])
            return carry

        lax.fori_loop(0, 2, plane, 0)
        hop(chunk, HOP_XY).start()
        hop(chunk, HOP_YX).start()

    def after_cross(chunk):
        half = table[chunk][2] // 2
        hop(chunk, HOP_XY).wait_recv()
        hop(chunk, HOP_YX).wait_recv()
        total, cross = sums[chunk], from_cross[chunk]
        total[y, x, :, :half] = add(total[y, x, :, :half], cross[0])
        total[y, x, :, half:] = add(total[y, x, :, half:], cross[1])

        @pl.when(jnp.logical_not(is_middle))
        def _():
            hop(chunk, HOP_IN).start()

    def after_in(chunk):
        @pl.when(is_middle)
        def _():
            hop(chunk, HOP_IN).wait_recv()
            total = sums[chunk]
            total[y, x] = add(total[y, x], from_far[chunk][0])
            hop(chunk, HOP_MID).start()

    def after_middle(chunk):
        @pl.when(is_middle)
        def _():
            hop(chunk, HOP_MID).wait_recv()
            far = from_far[chunk]
            far[0] = add(sums[chunk][y, x], far[1])
            hop(chunk, HOP_OUT).start()
            store(chunk).start()

    def start(some):
        for chunk in some:
            load(chunk).start()
            hop(chunk, HOP_CORE).start()

    stages = (after_core, after_near, after_cross, after_in, after_middle)

    def one_step(step):
        for late, stage in enumerate(stages):
            if 0 <= step - late < chunks:
                stage(step - late)

    steps = [functools.partial(one_step, i) for i in range(chunks + len(stages) - 1)]

    def finish():
        for chunk in range(chunks):
            for which in (HOP_CORE, HOP_X, HOP_Y, HOP_XY, HOP_YX):
                hop(chunk, which).wait_send()

        @pl.when(is_middle)
        def _():
            for chunk in range(chunks):
                hop(chunk, HOP_MID).wait_send()
                hop(chunk, HOP_OUT).wait_send()
                store(chunk).wait()

        @pl.when(jnp.logical_not(is_middle))
        def _():
            for chunk in range(chunks):
                hop(chunk, HOP_IN).wait_send()
                hop(chunk, HOP_OUT).wait_recv()

    return start, steps, finish


def reduction_scratch(table, split):
    kinds = [(split[t].dtype, split[t].shape[3], width) for t, _, width in table]
    dma = pltpu.SemaphoreType.DMA
    return [
        *[pltpu.VMEM((2, 2, r, w), t) for t, r, w in kinds],
        *[pltpu.VMEM((2, 2, r, w), t) for t, r, w in kinds],
        *[pltpu.VMEM((2, 2, r, w // 2), t) for t, r, w in kinds],
        *[pltpu.VMEM((2, r, w // 2), t) for t, r, w in kinds],
        *[pltpu.VMEM((2, r, w), t) for t, r, w in kinds],
        dma((len(table),)),
        dma((len(table), 8)),
        dma((len(table), 8)),
        dma((len(table),)),
    ]


def split_shards(parts):
    return [part.reshape(2, 2, 2, -1, part.shape[-1]) for part in parts]


def attend_back_pair(query, key, value, grad, prob, cosine, sine):
    low, high = head_masks(BF16)
    is_low = lax.broadcasted_iota(jnp.int32, (BLK, LANES), 1) < HD
    grad_v = dot(prob, grad, 0, 0)
    grad_v = jnp.where(is_low, grad_v[:BLK], grad_v[BLK:])
    grad_p = dot(grad, jnp.concatenate([value * low, value * high], axis=0), 1, 1)
    parts = []
    for head in range(2):
        keys = slice(head * BLK, (head + 1) * BLK)
        weight, slope = prob[:, keys].astype(F32), grad_p[:, keys]
        inner = jnp.sum(weight * slope, axis=-1, keepdims=True)
        parts.append(weight * (slope - inner))
    grad_s = jnp.concatenate(parts, axis=1).astype(BF16)
    both = jnp.concatenate([key * low, key * high], axis=0)
    grad_q = dot(grad_s, both) * SCALE
    grad_k = dot(grad_s, query, 0, 0)
    grad_k = jnp.where(is_low, grad_k[:BLK], grad_k[BLK:]) * SCALE
    return (
        (grad_q * cosine - turned(grad_q) * sine).astype(BF16),
        (grad_k * cosine - turned(grad_k) * sine).astype(BF16),
        grad_v.astype(BF16),
    )


FEATURES = D // SHARDS
SOME_ROWS = 256
ROW_PIECES = ROWS // SOME_ROWS


def interleave(steps, pieces, ahead):
    for piece in pieces[:ahead]:
        piece()
    pieces = pieces[ahead:]
    done = 0
    for index, step in enumerate(steps):
        step()
        upto = -(-len(pieces) * (index + 1) // len(steps))
        for piece in pieces[done:upto]:
            piece()
        done = upto


def return_kernel(devices, micros, *refs):
    groups = MICRO // micros
    early = refs[:3]
    send, lengths_ref, qkv_ref, prob_ref, grad_o_ref, act_ref, hidden_ref = refs[3:10]
    mid_ref, weight_ref, gain_ref, other_ref, cos_ref, sin_ref = refs[10:16]
    outs, layer_land, grad_land, grad_w_ref, gains_ref = refs[16:21], *refs[21:25]
    wide, grads, block_prob, block_grad, act_part, w_part = refs[25:31]
    row_hidden, row_mid, kept, packed, grad_gain, gain_parts = refs[31:37]
    wide_sem, block_sem, act_sem, w_sem, row_sem, gain_sem = refs[37:43]
    layer_sems, grad_sems, refs = refs[43:46], refs[46:49], refs[49:]
    tensors = (*early, grad_w_ref, gains_ref)
    start, steps, finish = reduction(REDUCE_CHUNKS, tensors, outs, refs)
    start_layer, finish_layer = row_exchange(
        lambda to: send.at[to], lambda slot: layer_land.at[slot], *layer_sems, devices
    )
    exchanges = [
        row_exchange(
            lambda to, group=group: packed.at[group, to],
            lambda slot, group=group: grad_land.at[slot, group],
            *[sem.at[group] for sem in grad_sems],
            devices,
        )
        for group in range(groups)
    ]
    copy = pltpu.make_async_copy

    def block_loads(block):
        slot = block % 2
        rows = pl.ds(block * BLK, BLK)
        return (
            copy(prob_ref.at[block], block_prob.at[slot], block_sem.at[slot, 0]),
            copy(grad_o_ref.at[rows], block_grad.at[slot], block_sem.at[slot, 1]),
        )

    def act_load(part):
        columns = pl.ds(part * FEATURES, FEATURES)
        return copy(act_ref.at[:, columns], act_part.at[part % 2], act_sem.at[part % 2])

    def w_store(part):
        target = grad_w_ref.at[part // 4, part // 2 % 2, part % 2]
        return copy(w_part, target, w_sem)

    def row_loads(part):
        rows = pl.ds(part * SOME_ROWS, SOME_ROWS)
        return (
            copy(hidden_ref.at[rows], row_hidden, row_sem.at[0]),
            copy(mid_ref.at[rows], row_mid, row_sem.at[1]),
        )

    load_qkv = copy(qkv_ref, wide, wide_sem.at[0])
    load_weight = copy(weight_ref, wide, wide_sem.at[1])

    def attend_piece(block):
        if block == 0:
            load_qkv.wait()
        for load in block_loads(block):
            load.wait()
        if block + 1 < BLOCKS:
            for load in block_loads(block + 1):
                load.start()
        slot = block % 2
        rows = slice(block * BLK, (block + 1) * BLK)

        def two(index, carry):
            for inner in range(4):
                pair = index * 4 + inner
                base = pl.multiple_of(pair * LANES, LANES)
                columns = [
                    pl.ds(pl.multiple_of(part * D + base, LANES), LANES) for part in range(3)
                ]
                results = attend_back_pair(
                    *[wide[rows, c] for c in columns],
                    block_grad[slot, :, pl.ds(base, LANES)],
                    block_prob[slot, pair],
                    cos_ref[...],
                    sin_ref[...],
                )
                for c, result in zip(columns, results):
                    grads[rows, c] = result
            return carry

        lax.fori_loop(0, PAIRS // 4, two, 0)
        if block == BLOCKS - 1:
            load_weight.start()
            act_load(0).start()

    def weight_piece(part):
        act_load(part).wait()
        if part + 1 < SHARDS:
            act_load(part + 1).start()
        act_t = act_part[part % 2].T
        if part:
            w_store(part - 1).wait()
        for third in range(3):
            columns = slice(third * D, (third + 1) * D)
            w_part[:, columns] = dot(act_t, grads[:, columns]).astype(BF16)
        w_store(part).start()
        if part == SHARDS - 1:
            w_store(part).wait()
            start([i for i, c in enumerate(REDUCE_CHUNKS) if c[0] == 3])
            for load in row_loads(0):
                load.start()

    def row_piece(part):
        if part == 0:
            load_weight.wait()
            grad_gain[...] = jnp.zeros_like(grad_gain)
        for load in row_loads(part):
            load.wait()
        rows = slice(part * SOME_ROWS, (part + 1) * SOME_ROWS)
        grad_a = dot(grads[rows, :], wide[...], 1, 1)
        normal, inverse = normed(row_hidden[...].astype(F32))
        grad_gain[...] += jnp.sum(grad_a * normal, axis=0, keepdims=True)
        each = ROW_PIECES // groups
        inner = slice(part % each * SOME_ROWS, (part % each + 1) * SOME_ROWS)
        kept[inner] = (
            row_mid[...] + norm_back(grad_a * gain_ref[...], normal, inverse)
        ).astype(BF16)
        if part + 1 < ROW_PIECES:
            for load in row_loads(part + 1):
                load.start()
        if part % each == each - 1:
            group = part // each
            pick = held_rows(lengths_ref, group, micros, devices)
            packed[group] = (
                dot(pick, kept[...], 0, 0).astype(BF16).reshape(packed.shape[1:])
            )
            exchanges[group][0]()

    def gain_piece():
        width = D // SHARDS
        for shard in range(SHARDS):
            columns = slice(shard * width, (shard + 1) * width)
            for part, values in enumerate((grad_gain, other_ref)):
                gain_parts[shard // 4, shard // 2 % 2, shard % 2, :, part * width : (part + 1) * width] = (
                    jnp.broadcast_to(values[:, columns], (GAIN_ROWS, width))
                )
        keep = copy(gain_parts, gains_ref, gain_sem)
        keep.start()
        keep.wait()
        start([i for i, c in enumerate(REDUCE_CHUNKS) if c[0] == 4])

    greet_all(devices)
    load_qkv.start()
    for load in block_loads(0):
        load.start()
    start(range(len(EARLY_CHUNKS)))
    start_layer()
    pieces = [
        *[functools.partial(attend_piece, i) for i in range(BLOCKS)],
        *[functools.partial(weight_piece, i) for i in range(SHARDS)],
        *[functools.partial(row_piece, i) for i in range(ROW_PIECES)],
        gain_piece,
    ]
    count = len(EARLY_CHUNKS)
    interleave(steps[:count], pieces, 2)
    for step in steps[count:]:
        step()
    finish()
    finish_layer()
    for exchange in exchanges:
        exchange[1]()


def return_all(
    parts,
    send,
    lengths,
    qkv,
    prob,
    grad_o,
    act,
    hidden,
    grad_mid,
    weight,
    gain,
    other,
    tables,
    devices,
    micros,
):
    early = split_shards(parts)
    groups = MICRO // micros
    rows = D // SHARDS
    split = [
        *early,
        jax.ShapeDtypeStruct((2, 2, 2, rows, 3 * D), BF16),
        jax.ShapeDtypeStruct((2, 2, 2, GAIN_ROWS, 2 * rows), F32),
    ]
    anywhere = pl.BlockSpec(memory_space=pl.ANY)
    inside = pl.BlockSpec(memory_space=pltpu.VMEM)
    dma = pltpu.SemaphoreType.DMA
    *owned, layer_back, grad_back, _, _ = pl.pallas_call(
        functools.partial(return_kernel, devices, micros),
        in_specs=[
            *[anywhere] * 4,
            inside,
            *[anywhere] * 7,
            *[inside] * 4,
        ],
        out_specs=[anywhere] * 9,
        out_shape=[
            *[jax.ShapeDtypeStruct(v.shape[3:], v.dtype) for v in split],
            jax.ShapeDtypeStruct(send.shape, send.dtype),
            jax.ShapeDtypeStruct(send.shape, send.dtype),
            *split[3:],
        ],
        scratch_shapes=[
            pltpu.VMEM((ROWS, 3 * D), BF16),
            pltpu.VMEM((ROWS, 3 * D), BF16),
            pltpu.VMEM((2, PAIRS, BLK, 2 * BLK), BF16),
            pltpu.VMEM((2, BLK, D), BF16),
            pltpu.VMEM((2, ROWS, FEATURES), BF16),
            pltpu.VMEM((FEATURES, 3 * D), BF16),
            pltpu.VMEM((SOME_ROWS, D), BF16),
            pltpu.VMEM((SOME_ROWS, D), F32),
            pltpu.VMEM((ROWS // groups, D), BF16),
            pltpu.VMEM((groups, devices, CHUNK_ROWS, D), BF16),
            pltpu.VMEM((1, D), F32),
            pltpu.VMEM((2, 2, 2, GAIN_ROWS, 2 * rows), F32),
            dma((2,)),
            dma((2, 2)),
            dma((2,)),
            dma,
            dma((2,)),
            dma,
            dma,
            dma((devices,)),
            dma((devices,)),
            dma((groups,)),
            dma((groups, devices)),
            dma((groups, devices)),
            *reduction_scratch(REDUCE_CHUNKS, split),
        ],
        compiler_params=pltpu.CompilerParams(
            vmem_limit_bytes=63 * MIB, collective_id=1, has_side_effects=True
        ),
        cost_estimate=cost(16 * ROWS * D * D, 600 * MIB),
    )(
        *early,
        send,
        lengths,
        qkv,
        prob,
        grad_o,
        act,
        hidden,
        grad_mid,
        weight,
        gain,
        other,
        *tables,
    )
    return (*owned, layer_back, grad_back)


WAY_X, WAY_Y, WAY_CORE, WAY_CORE_X, WAY_CORE_Y = range(5)
WAY_XY, WAY_YX, WAY_CORE_XY, WAY_CORE_YX = range(5, 9)


GATHER_CHUNKS = (
    (0, 0, 1536),
    (0, 1536, 1536),
    (1, 0, 1024),
    (2, 0, 768),
    (3, 0, 512),
    (3, 512, 512),
    *[(2, i * 768, 768) for i in range(1, 7)],
)
OUT_CHUNK = 2
FF_CHUNKS = (3, 6, 7, 8, 9, 10, 11)
EARLY_FIRSTS = 7


def gathering(table, shards, fulls, keep_sem, send_sem, recv_sem):
    rep, grp, core, x, y, by_core, by_x, by_y = place()
    by_xy = by_x + by_y - grp
    other = by_core - grp

    def view(chunk, slot, half=None):
        tensor, start, width = table[chunk]
        rows = shards[tensor].shape[0]
        if half is not None:
            start, width = start + half * (width // 2), width // 2
        first = pl.multiple_of(slot * rows, rows)
        return fulls[tensor].at[pl.ds(first, rows), pl.ds(start, width)]

    def own(chunk):
        tensor, start, width = table[chunk]
        return shards[tensor].at[:, pl.ds(start, width)]

    def way(chunk, which):
        slot, landing, half, to = {
            WAY_X: (grp, by_x, None, by_x),
            WAY_Y: (grp, by_y, None, by_y),
            WAY_CORE: (grp, by_core, None, by_core),
            WAY_CORE_X: (by_x, by_x + other, None, by_core),
            WAY_CORE_Y: (by_y, by_y + other, None, by_core),
            WAY_XY: (by_x, by_xy, 0, by_y),
            WAY_YX: (by_y, by_xy, 1, by_x),
            WAY_CORE_XY: (by_xy, by_xy + other, 0, by_core),
            WAY_CORE_YX: (by_xy, by_xy + other, 1, by_core),
        }[which]
        from_own = which in (WAY_X, WAY_Y, WAY_CORE)

        def copy(source, target):
            return pltpu.make_async_remote_copy(
                src_ref=source,
                dst_ref=target,
                send_sem=send_sem.at[chunk, which],
                recv_sem=recv_sem.at[chunk, which],
                device_id=(rep, to),
                device_id_type=MESH,
            )

        source = own(chunk) if from_own else view(chunk, slot, half)
        here = view(chunk, landing, half)
        return (
            lambda: copy(source, view(chunk, slot, half)).start(),
            lambda: copy(here, here).wait_recv(),
            lambda: copy(source, view(chunk, slot, half)).wait_send(),
        )

    def keep(chunk):
        return pltpu.make_async_copy(own(chunk), view(chunk, grp), keep_sem.at[chunk])

    def start(chunk, *ways):
        for which in ways:
            way(chunk, which)[0]()

    def arrive(chunk, *ways):
        for which in ways:
            way(chunk, which)[1]()

    def first(chunk):
        start(chunk, WAY_X, WAY_Y, WAY_CORE)
        keep(chunk).start()

    def forward(chunk):
        arrive(chunk, WAY_X)
        start(chunk, WAY_XY, WAY_CORE_X)
        arrive(chunk, WAY_Y)
        start(chunk, WAY_YX, WAY_CORE_Y)

    def last(chunk):
        arrive(chunk, WAY_XY)
        start(chunk, WAY_CORE_XY)
        arrive(chunk, WAY_YX)
        start(chunk, WAY_CORE_YX)

    def complete(chunk):
        keep(chunk).wait()
        arrive(chunk, WAY_CORE, WAY_CORE_X, WAY_CORE_Y, WAY_CORE_XY, WAY_CORE_YX)

    def sent(chunk):
        for which in range(9):
            way(chunk, which)[2]()

    return first, forward, last, complete, sent


def forward_kernel(devices, micros, *refs):
    groups = MICRO // micros
    lengths_ref, gain_shard, cos_ref, sin_ref, token_send, top_send = refs[:6]
    w_qkv_ref, w_out_ref, w_in_ref, w_down_ref = refs[6:10]
    gain_rows, gain_grad, hidden_out, act_out, qkv_out, prob_out = refs[10:16]
    attn_out, mid_out, layer_out, grad_mid_out, grad_in_out, grad_down_out = refs[16:22]
    weight_out, grad_o_out, grad_out_out, refs = *refs[22:25], refs[25:]
    weight, full_out, full_in, full_down, token_land, top_land, gain_land = refs[:7]
    picks, act_b, act_t, top, total, grad_b = refs[7:13]
    s_hidden, s_act, s_qkv, s_prob, s_attn, s_mid, s_in, s_down = refs[13:21]
    raw_in, own_in = refs[21:23]
    store_sem, gain_sem, gain_send, gain_recv = refs[23:27]
    row_sems, refs = refs[27:30], refs[30:]
    shards = (w_qkv_ref, w_out_ref, own_in, w_down_ref)
    fulls = (weight, full_out, full_in, full_down)
    first, forward, last, complete, sent = gathering(GATHER_CHUNKS, shards, fulls, *refs)
    rep, grp = lax.axis_index("rep"), lax.axis_index("grp")
    chunks = len(GATHER_CHUNKS)
    slots = devices * CHUNK_ROWS

    def exchange(send, land, group, index):
        return row_exchange(
            lambda to: send.at[to, group],
            lambda slot: land.at[slot, group],
            *[sem.at[index] for sem in row_sems],
            devices,
        )

    token_swaps = [exchange(token_send, token_land, g, g) for g in range(groups)]
    top_swaps = [exchange(top_send, top_land, g, groups + g) for g in range(groups)]

    def gain_copy(step, slot):
        return pltpu.make_async_remote_copy(
            src_ref=gain_shard,
            dst_ref=gain_land.at[slot],
            send_sem=gain_send.at[step],
            recv_sem=gain_recv.at[step],
            device_id=(rep, lax.rem(grp + step, SHARDS)),
            device_id_type=MESH,
        )

    pending = {}

    def free(name):
        if name in pending:
            pending.pop(name).wait()

    def put(name, source, target):
        index = ("hidden", "act", "qkv", "prob", "attn", "mid", "in", "down", "late", "layer", "far", "o", "w")
        copy = pltpu.make_async_copy(source, target, store_sem.at[index.index(name)])
        copy.start()
        pending[name] = copy

    def tick(step):
        if step < chunks:
            forward(step)
            if EARLY_FIRSTS <= step + 2 < chunks:
                first(step + 2)
        if 0 < step <= chunks:
            last(step - 1)

    def gain_row(part):
        table = gain_land[...].astype(F32)
        return jnp.concatenate([table[s, part : part + 1] for s in range(SHARDS)], axis=1)

    def micro_rows(micro):
        return slice(micro * CAP, (micro + 1) * CAP)

    def qkv_piece(micro):
        group, rows = micro // micros, micro_rows(micro)
        for name in ("hidden", "act", "qkv"):
            free(name)
        values = dot(picks[rows, :], token_land[:, group].reshape(slots, D))
        s_hidden[...] = values.astype(BF16)
        act = (normed(values)[0] * gain_rows[0:1, :]).astype(BF16)
        s_act[...] = act
        for step in range(3 * D // QKV_TILE):
            lanes = slice(step * QKV_TILE, (step + 1) * QKV_TILE)
            packed = dot(act, weight[:, lanes])
            if step < 2 * D // QKV_TILE:
                split = packed.reshape(CAP // BLK, BLK, QKV_TILE)
                split = (
                    split * widen(cos_ref[...])[None]
                    + turned(split) * widen(sin_ref[...])[None]
                )
                packed = split.reshape(CAP, QKV_TILE)
            s_qkv[:, lanes] = packed.astype(BF16)
        put("hidden", s_hidden, hidden_out.at[rows])
        put("act", s_act, act_out.at[rows])
        put("qkv", s_qkv, qkv_out.at[rows])

    def attend_piece(micro):
        free("prob")
        free("attn")

        def one(block, carry):
            rows = pl.ds(pl.multiple_of(block * BLK, BLK), BLK)
            lengths = block_lengths(lengths_ref, block, devices)
            valid = key_mask(lengths[micro : micro + 1])
            for pair in range(PAIRS):
                columns = [
                    slice(part * D + pair * LANES, part * D + (pair + 1) * LANES)
                    for part in range(3)
                ]
                context, prob = attend_pair(*[s_qkv[rows, c] for c in columns], valid)
                s_attn[rows, columns[0]] = context
                s_prob[block, pair] = prob
            return carry

        lax.fori_loop(0, SEQ_DEV, one, 0)

    def middle_piece(micro):
        rows = micro_rows(micro)
        free("mid")
        middle = s_hidden[...].astype(F32) + dot(s_attn[...], full_out[...])
        s_mid[...] = middle
        total[rows, :] = middle
        act_b[rows, :] = (normed(middle)[0] * gain_rows[1:2, :]).astype(BF16)
        put("prob", s_prob, prob_out.at[pl.ds(micro * SEQ_DEV, SEQ_DEV)])
        put("attn", s_attn, attn_out.at[rows])
        put("mid", s_mid, mid_out.at[rows])

    def top_piece(micro):
        group, rows = micro // micros, micro_rows(micro)
        values = dot(picks[rows, :], top_land[:, group].reshape(slots, D))
        top[rows, :] = values.astype(BF16)

    def ff_views(step):
        return (
            slice(step * 2 * FF_TILE, (step + 1) * 2 * FF_TILE),
            slice(step * FF_TILE, (step + 1) * FF_TILE),
            step % 2 * 3 * FF_TILE,
        )

    def ff_forward(step):
        both, hidden, base = ff_views(step)
        gate_up = dot(act_b[...], full_in[:, both])
        gelu_in, linear = gate_up[:, :FF_TILE], gate_up[:, FF_TILE:]
        phi = 0.5 * (1.0 + lax.erf(gelu_in * ROOT_HALF))
        gelu_out = gelu_in * phi
        slope = phi + gelu_in * (jnp.exp(-0.5 * gelu_in * gelu_in) * INV_ROOT_TWO_PI)
        act_c = (gelu_out * linear).astype(BF16)
        weight[:, base : base + FF_TILE] = (linear * slope).astype(BF16)
        weight[:, base + FF_TILE : base + 2 * FF_TILE] = gelu_out.astype(BF16)
        weight[:, base + 2 * FF_TILE : base + 3 * FF_TILE] = act_c
        total[...] += dot(act_c, full_down[hidden, :])

    def ff_backward(step):
        both, hidden, base = ff_views(step)
        kept = slice(6 * FF_TILE, 8 * FF_TILE)
        grad_c = dot(top[...], full_down[hidden, :], 1, 1)
        for part in range(2):
            factor = weight[:, base + part * FF_TILE : base + (part + 1) * FF_TILE]
            start = (6 + part) * FF_TILE
            weight[:, start : start + FF_TILE] = (grad_c * factor.astype(F32)).astype(BF16)
        grad_b[...] += dot(weight[:, kept], full_in[:, both], 1, 1)
        s_in[...] = dot(act_t[...], weight[:, kept]).astype(BF16)
        act_c = weight[:, base + 2 * FF_TILE : base + 3 * FF_TILE]
        s_down[...] = dot(act_c, top[...], 0, 0).astype(BF16)

    raw_load = pltpu.make_async_copy(w_in_ref, raw_in, store_sem.at[12])
    raw_load.start()
    greet_all(devices)
    gain_keep = pltpu.make_async_copy(gain_shard, gain_land.at[grp], gain_sem)
    gain_keep.start()
    for step in range(1, SHARDS):
        gain_copy(step, grp).start()
    token_swaps[0][0]()
    first(0)
    first(1)
    for swap in token_swaps[1:]:
        swap[0]()
    first(2)
    first(4)
    first(5)
    for group in range(groups):
        rows = slice(group * micros * CAP, (group + 1) * micros * CAP)
        picks[rows, :] = held_rows(lengths_ref, group, micros, devices)
    grad_b[...] = jnp.zeros_like(grad_b)
    tick(0)
    tick(1)
    raw_load.wait()
    weave_inside(raw_in, own_in)
    first(3)
    first(6)
    tick(2)
    gain_keep.wait()
    for step in range(1, SHARDS):
        gain_copy(step, lax.rem(grp + SHARDS - step, SHARDS)).wait_recv()
        gain_copy(step, grp).wait_send()
    for part in range(2):
        gain_rows[part : part + 1, :] = gain_row(part)
    for swap in token_swaps:
        swap[1]()
    for swap in top_swaps:
        swap[0]()
    complete(0)
    complete(1)
    put("late", weight, weight_out)
    for micro in range(MICRO):
        qkv_piece(micro)
        tick(3 + micro)
        attend_piece(micro)
        if micro == 0:
            complete(OUT_CHUNK)
        middle_piece(micro)
    act_t[...] = act_b[...].T
    tick(7)
    for chunk in (4, 5):
        complete(chunk)
    free("late")
    for chunk in range(2):
        sent(chunk)
    steps = len(FF_CHUNKS)
    for step in range(2):
        if step:
            tick(8)
        complete(FF_CHUNKS[step])
        ff_forward(step)
    for swap in top_swaps:
        swap[1]()
    for micro in range(MICRO):
        top_piece(micro)
    for step in range(steps):
        if step + 2 < steps:
            tick(9 + step)
            complete(FF_CHUNKS[step + 2])
        free("in")
        free("down")
        ff_backward(step)
        if step + 2 < steps:
            ff_forward(step + 2)
        both, hidden, _ = ff_views(step)
        put("in", s_in, grad_in_out.at[:, both])
        put("down", s_down, grad_down_out.at[hidden])
    free("attn")
    free("mid")
    load_attn = pltpu.make_async_copy(attn_out, act_b, store_sem.at[13])
    load_mid = pltpu.make_async_copy(mid_out, total, store_sem.at[14])
    load_attn.start()
    for group in range(groups):
        rows = slice(group * micros * CAP, (group + 1) * micros * CAP)
        values = dot(picks[rows, :], total[rows, :].astype(BF16), 0, 0)
        token_land[:, group] = values.astype(BF16).reshape(devices, CHUNK_ROWS, D)
    put("layer", token_land, layer_out)
    load_mid.start()
    load_mid.wait()
    gain_grad[...] = jnp.zeros_like(gain_grad)

    def branch(index, carry):
        rows = pl.ds(pl.multiple_of(index * ROW_CHUNK, ROW_CHUNK), ROW_CHUNK)
        normal, inverse = normed(total[rows, :])
        grad = grad_b[rows, :]
        gain_grad[...] += jnp.sum(grad * normal, axis=0, keepdims=True)
        grad_mid = top[rows, :].astype(F32) + norm_back(
            grad * gain_rows[1:2, :], normal, inverse
        )
        total[rows, :] = grad_mid
        weight[rows, :D] = grad_mid.astype(BF16)
        return carry

    lax.fori_loop(0, ROWS // ROW_CHUNK, branch, 0)
    put("far", total, grad_mid_out)
    weight[:, D : 2 * D] = dot(weight[:, :D], full_out[...], 1, 1).astype(BF16)
    put("o", weight.at[:, pl.ds(D, D)], grad_o_out)
    load_attn.wait()
    weight[:, 2 * D :] = dot(act_b[...], weight[:, :D], 0, 0).astype(BF16)
    put("w", weight.at[:, pl.ds(2 * D, D)], grad_out_out)
    for name in list(pending):
        free(name)
    for chunk in range(2, chunks):
        sent(chunk)


def forward_all(lengths, gain, tables, sends, shards, devices, micros):
    anywhere = pl.BlockSpec(memory_space=pl.ANY)
    inside = pl.BlockSpec(memory_space=pltpu.VMEM)
    dma = pltpu.SemaphoreType.DMA
    groups = MICRO // micros
    exchanged = sends[0].shape
    chunks = len(GATHER_CHUNKS)
    full = [(SHARDS * v.shape[0], v.shape[1]) for v in shards]
    full[2] = (D, 2 * SHARDS * ff_shard(SHARDS))
    rows16 = jax.ShapeDtypeStruct((ROWS, D), BF16)
    rows32 = jax.ShapeDtypeStruct((ROWS, D), F32)
    return pl.pallas_call(
        functools.partial(forward_kernel, devices, micros),
        in_specs=[inside, anywhere, inside, inside, *[anywhere] * 6],
        out_specs=[inside, inside, *[anywhere] * 13],
        out_shape=[
            jax.ShapeDtypeStruct((2, D), F32),
            jax.ShapeDtypeStruct((1, D), F32),
            rows16,
            rows16,
            jax.ShapeDtypeStruct((ROWS, 3 * D), BF16),
            jax.ShapeDtypeStruct((BLOCKS, PAIRS, BLK, 2 * BLK), BF16),
            rows16,
            rows32,
            jax.ShapeDtypeStruct(exchanged, BF16),
            rows32,
            jax.ShapeDtypeStruct(full[2], BF16),
            jax.ShapeDtypeStruct(full[3], BF16),
            jax.ShapeDtypeStruct(full[0], BF16),
            rows16,
            jax.ShapeDtypeStruct((D, D), BF16),
        ],
        scratch_shapes=[
            *[pltpu.VMEM(v, BF16) for v in full],
            pltpu.VMEM(exchanged, BF16),
            pltpu.VMEM(exchanged, BF16),
            pltpu.VMEM((SHARDS, *gain.shape), BF16),
            pltpu.VMEM((ROWS, devices * CHUNK_ROWS), BF16),
            pltpu.VMEM((ROWS, D), BF16),
            pltpu.VMEM((D, ROWS), BF16),
            pltpu.VMEM((ROWS, D), BF16),
            pltpu.VMEM((ROWS, D), F32),
            pltpu.VMEM((ROWS, D), F32),
            pltpu.VMEM((CAP, D), BF16),
            pltpu.VMEM((CAP, D), BF16),
            pltpu.VMEM((CAP, 3 * D), BF16),
            pltpu.VMEM((SEQ_DEV, PAIRS, BLK, 2 * BLK), BF16),
            pltpu.VMEM((CAP, D), BF16),
            pltpu.VMEM((CAP, D), F32),
            pltpu.VMEM((D, 2 * FF_TILE), BF16),
            pltpu.VMEM((FF_TILE, D), BF16),
            pltpu.VMEM(shards[2].shape, BF16),
            pltpu.VMEM((shards[2].shape[0], full[2][1]), BF16),
            dma((15,)),
            dma,
            dma((SHARDS,)),
            dma((SHARDS,)),
            dma((2 * groups,)),
            dma((2 * groups, devices)),
            dma((2 * groups, devices)),
            dma((chunks,)),
            dma((chunks, 9)),
            dma((chunks, 9)),
        ],
        compiler_params=pltpu.CompilerParams(
            vmem_limit_bytes=63 * MIB, collective_id=0, has_side_effects=True
        ),
        cost_estimate=cost(30 * ROWS * D * FF, 600 * MIB),
    )(lengths, gain, *tables, *sends, *shards)


def ff_shard(group_size):
    return -(-FF // group_size // CHUNK_ROWS) * CHUNK_ROWS


def weave(weight, group_size):
    each, wide = FF // group_size, ff_shard(group_size)
    gap = jnp.zeros((weight.shape[0], wide - each), weight.dtype)
    halves = []
    for half in range(2):
        parts = []
        for shard in range(group_size):
            first = half * FF + shard * each
            parts += [weight[:, first : first + each], gap]
        halves.append(jnp.concatenate(parts, axis=1))
    steps = group_size * wide // FF_TILE
    return jnp.concatenate(
        [
            halves[half][:, step * FF_TILE : (step + 1) * FF_TILE]
            for step in range(steps)
            for half in range(2)
        ],
        axis=1,
    )


def weave_block(block):
    each, wide = FF // SHARDS, ff_shard(SHARDS)
    sources = []
    for lane in range(block * 128, (block + 1) * 128):
        half = lane % (2 * FF_TILE) // FF_TILE
        unit = lane // (2 * FF_TILE) * FF_TILE + lane % FF_TILE
        if unit % wide < each:
            sources.append(half * FF + unit // wide * each + unit % wide)
    return min(sources) // 128 * 128, -(-(max(sources) + 1) // 128) * 128


def weave_inside(raw, woven):
    each, wide = FF // SHARDS, ff_shard(SHARDS)
    for block in range(woven.shape[1] // 128):
        start, end = weave_block(block)
        first = block * 128
        half = first % (2 * FF_TILE) // FF_TILE
        base = first // (2 * FF_TILE) * FF_TILE + first % FF_TILE
        shape = (end - start, 128)
        unit = base + lax.broadcasted_iota(jnp.int32, shape, 1)
        low, turn = base // wide, (base // wide + 1) * wide
        shard = jnp.where(unit >= turn, low + 1, low)
        inner = unit - shard * wide
        source = half * FF + shard * each + inner
        mine = start + lax.broadcasted_iota(jnp.int32, shape, 0)
        pick = ((source == mine) & (inner < each)).astype(F32).astype(BF16)
        woven[:, first : first + 128] = dot(raw[:, start:end], pick).astype(BF16)


def unweave(woven, group_size):
    each, wide = FF // group_size, ff_shard(group_size)
    steps = group_size * wide // FF_TILE
    parts = []
    for half in range(2):
        row = jnp.concatenate(
            [
                woven[:, (2 * step + half) * FF_TILE : (2 * step + half + 1) * FF_TILE]
                for step in range(steps)
            ],
            axis=1,
        )
        parts += [row[:, i * wide : i * wide + each] for i in range(group_size)]
    return jnp.concatenate(parts, axis=1)


def body(tokens, cotangent, seq_lengths, w_qkv, w_out, w_in, w_down, attn_gain, mlp_gain):
    group_size = lax.axis_size("grp")
    devices = lax.axis_size("rep") * group_size
    device = lax.axis_index("rep") * group_size + lax.axis_index("grp")
    micros = min(MICRO, max(1, CHUNK_ROWS * devices // CAP))
    both = ("rep", "grp")

    def swap(rows):
        return lax.all_to_all(rows, both, split_axis=0, concat_axis=0, tiled=True)

    near = group_size == SHARDS and devices == REPLICAS * SHARDS
    sends = pack_rows(
        seq_lengths, (tokens[:, :, 0], cotangent[:, :, 0]), devices, micros
    )
    gains = jnp.stack([attn_gain, mlp_gain])
    pad = ff_shard(group_size) - w_down.shape[0]
    held = w_in if near else weave(w_in, group_size)
    shards = (w_qkv, w_out, held, jnp.pad(w_down, ((0, pad), (0, 0))))
    tables = rotary_tables()
    if near:
        gain = jnp.pad(gains, ((0, CHUNK_ROWS - 2), (0, 0)))
        (
            gains,
            grad_gain_two,
            hidden,
            act_a,
            qkv,
            prob,
            _,
            _,
            layer_send,
            grad_mid,
            grad_in_w,
            grad_down_w,
            full_qkv,
            grad_o,
            grad_out_w,
        ) = forward_all(seq_lengths, gain, tables, sends, shards, devices, micros)
        gain_one = gains[:1]
    else:
        token_rows, top_rows = (swap(v) for v in sends)
        full_qkv, full_out, full_in, full_down = (
            lax.all_gather(v, "grp", axis=0, tiled=True) for v in shards
        )
        gains = lax.all_gather(gains, "grp", axis=1, tiled=True).astype(F32)
        gain_one, gain_two = gains[:1], gains[1:]
        hidden, act_a, top = unpack_rows(
            seq_lengths, token_rows, top_rows, gain_one, devices, micros
        )
        qkv = qkv_rows(act_a, full_qkv, *tables)
        attn_o, prob = attend(qkv, seq_lengths, devices)
        middle, act_b = middle_rows(attn_o, hidden, full_out, gain_two)
        layer_rows, grad_b, grad_in_w, grad_down_w = ffn(
            act_b, top, middle, full_in, full_down
        )
        layer_send = repack_rows(seq_lengths, layer_rows, devices, micros)
        grad_mid, grad_o, grad_out_w, grad_gain_two = branch_back(
            layer_send, grad_b, middle, top, attn_o, full_out, gain_two
        )
    if near:
        grad_down, grad_in, grad_out, grad_qkv, gain_sums, layer_back, grad_back = return_all(
            (grad_down_w, grad_in_w, grad_out_w),
            layer_send,
            seq_lengths,
            qkv,
            prob,
            grad_o,
            act_a,
            hidden,
            grad_mid,
            full_qkv,
            gain_one,
            grad_gain_two,
            tables,
            devices,
            micros,
        )
        gain_sums = gain_sums[0].reshape(2, -1)
    else:
        layer_back = swap(layer_send)
        grad_qkv_rows = attend_back(qkv, grad_o, prob, *tables)
        grad_qkv_w = qkv_grad(act_a, grad_qkv_rows)
        grad_rows, gain_parts = input_back(
            grad_qkv_rows, full_qkv, hidden, grad_mid, gain_one, grad_gain_two
        )
        grad_back = swap(repack_rows(seq_lengths, grad_rows, devices, micros))
        grad_down, grad_in, grad_out, grad_qkv = (
            lax.psum(lax.psum_scatter(v, "grp", scatter_dimension=0, tiled=True), "rep")
            for v in (grad_down_w, grad_in_w, grad_out_w, grad_qkv_w)
        )
        gain_parts = gain_parts[:, 0].reshape(SHARDS, 2, -1).swapaxes(0, 1).reshape(2, D)
        gain_sums = lax.psum(
            lax.psum_scatter(gain_parts, "grp", scatter_dimension=1, tiled=True), "rep"
        )
    grad_down, grad_in, grad_out, grad_qkv = (
        v.astype(F32) for v in (grad_down, grad_in, grad_out, grad_qkv)
    )
    layer_out = spread_rows(seq_lengths, layer_back, devices, micros)[:, :, None, :]
    grad_tokens = spread_rows(seq_lengths, grad_back, devices, micros)[:, :, None, :]
    return (
        layer_out,
        grad_tokens,
        gain_sums[0],
        gain_sums[1],
        grad_qkv,
        grad_out,
        unweave(grad_in, group_size),
        grad_down[: w_down.shape[0]],
    )


def solution(mesh):
    return jax.shard_map(
        body,
        mesh=mesh,
        in_specs=(
            P(None, None, ("rep", "grp"), None),
            P(None, None, ("rep", "grp"), None),
            P(),
            P("grp", None),
            P("grp", None),
            P("grp", None),
            P("grp", None),
            P("grp"),
            P("grp"),
        ),
        out_specs=(
            P(None, None, ("rep", "grp"), None),
            P(None, None, ("rep", "grp"), None),
            P("grp"),
            P("grp"),
            P("grp", None),
            P("grp", None),
            P("grp", None),
            P("grp", None),
        ),
        check_vma=False,
    )
```
